32 devices in a mesh: parts: 2 (over x), seq: 16 (over z, y, core).
Axes of the slice: x: 2, y: 2, z: 4, core: 2. Of those that a mesh axis runs over, the one named last changes fastest.
Arguments:
- tokens: bfloat16 [131072, 512], P(('parts', 'seq')), parts along dimension 0, may hold values from -6 to 6
- w_value: bfloat16 [512, 512], replicated, may hold values from -0.25 to 0.25
- w_gate: bfloat16 [512, 512], replicated, may hold values from -0.25 to 0.25
- first_block: bfloat16 [256, 256], replicated, may hold values from -0.375 to 0.375
- second_block: bfloat16 [256, 256], replicated, may hold values from -0.375 to 0.375
- third_block: bfloat16 [256, 256], replicated, may hold values from -0.375 to 0.375
- fourth_block: bfloat16 [256, 256], replicated, may hold values from -0.375 to 0.375
- kernel: bfloat16 [512, 256, 256], P('seq'), may hold values from -6 to 6
- skip_gain: float32 [512], replicated, may hold values from 0.25 to 2
- cotangent: bfloat16 [131072, 512], P(('parts', 'seq')), parts along dimension 0, may hold values from -6 to 6
Outputs:
- grad_tokens: bfloat16 [131072, 512], P(('parts', 'seq')), parts along dimension 0
- grad_kernel: bfloat16 [1024, 256, 256], P(('parts', 'seq')), parts along dimension 0
- grad_weights: float32 [4, 512, 512], P('parts'), parts along dimension 0
- grad_skip: float32 [1024], P('parts'), parts along dimension 0
The draws below stay inside these ranges and needn't reach their ends.
There are 2 independent parts, one for each index of `parts`. The reference program is written for one: setup_inputs(seed, part) draws one part's arguments, and reference() takes and returns one part's arrays. A program takes and returns all parts, laid end to end along the dimension named above; an argument that names none is the same for every part. Nothing has to cross between parts.
All inputs are finite; a program needn't handle non-finite values.
Results may differ from the reference program's by a relative error of at most 0.025.
Values may be sent and summed in bfloat16 or wider, within the bound.
No kernel may reach another device: no remote copies, remote signals or barrier semaphores. Data moves between devices by JAX's collectives and lax.ppermute only.
A program may use at most 128 MiB of HBM per device.

```python
import math
import jax
import jax.numpy as jnp
from jax import lax

D = 512
N1 = 256
N2 = 256
LEN = 65536


def level_of(key, extent, split, least, top_value):
    gain = 1.0
    for position, blocks in split:
        draws = jax.random.uniform(jax.random.fold_in(jax.random.fold_in(key, 6), position), (blocks,), jnp.float32, least / len(split), top_value / len(split))
        gain = gain * jnp.repeat(jnp.exp(draws), extent[position] // blocks).reshape((-1,) + (1,) * (len(extent) - 1 - position))
    return gain


def scatter_about(own_key, extent, spread, reach, split=(), dtype=jnp.bfloat16):
    array = jax.random.normal(own_key, extent, jnp.float32) * spread
    if len(split) > 0:
        array = level_of(own_key, extent, split, -0.22, 0.18) * array
    return jnp.clip(array, min=-reach, max=reach).astype(dtype)


def setup_inputs(seed: int = 0, part: int = 0) -> dict:
    key_list = jax.random.split(jax.random.key(seed), 11)
    own_keys = jax.random.split(jax.random.fold_in(key_list[10], part), 11)
    tokens = scatter_about(own_keys[0], (LEN, D), 1.0, 6.0, ((0, 16),))
    w_value = scatter_about(key_list[1], (D, D), D ** -0.5, 0.25)
    w_gate = scatter_about(key_list[2], (D, D), D ** -0.5, 0.25)
    first_block = scatter_about(key_list[3], (N2, N2), N2 ** -0.5, 0.375)
    second_block = scatter_about(key_list[4], (N1, N1), N1 ** -0.5, 0.375)
    third_block = scatter_about(key_list[5], (N1, N1), N1 ** -0.5, 0.375)
    fourth_block = scatter_about(key_list[6], (N2, N2), N2 ** -0.5, 0.375)
    kernel = scatter_about(key_list[7], (D, N1, N2), 1.0, 6.0, ((0, 16),))
    skip_gain = jnp.clip(jnp.exp(jax.random.uniform(key_list[8], (D,), jnp.float32, math.log(0.25), math.log(2.0))), 0.25, 2.0)
    cotangent = scatter_about(own_keys[9], (LEN, D), 1.0, 6.0, ((0, 16),))
    return {"tokens": tokens, "w_value": w_value, "w_gate": w_gate, "first_block": first_block, "second_block": second_block, "third_block": third_block, "fourth_block": fourth_block, "kernel": kernel, "skip_gain": skip_gain, "cotangent": cotangent}


def reference(tokens, w_value, w_gate, first_block, second_block, third_block, fourth_block, kernel, skip_gain, cotangent):
    f32 = jnp.float32
    bf16 = jnp.bfloat16
    length = N1 * N2
    value = jnp.dot(tokens, w_value, preferred_element_type=f32).astype(bf16)
    gate = jnp.dot(tokens, w_gate, preferred_element_type=f32).astype(bf16)
    cube = value.reshape(N1, N2, D).astype(f32)
    section_one = jnp.einsum('abc,pb->apc', cube, first_block.astype(f32)).astype(bf16)
    spectrum = jnp.einsum('apc,qa->qpc', section_one.astype(f32), second_block.astype(f32))
    kernel_t = jnp.transpose(kernel.astype(f32), (1, 2, 0))
    filtered = (spectrum * kernel_t).astype(bf16)
    section_three = jnp.einsum('qpc,rq->rpc', filtered.astype(f32), third_block.astype(f32)).astype(bf16)
    conv = jnp.einsum('rpc,sp->rsc', section_three.astype(f32), fourth_block.astype(f32)).reshape(length, D)
    mixed = conv + skip_gain * value.astype(f32)
    upstream = cotangent.astype(f32)
    d_mix = (upstream * gate.astype(f32)).astype(bf16)
    d_gate = (upstream * mixed).astype(bf16)
    d_three = jnp.einsum('rsc,sp->rpc', d_mix.reshape(N1, N2, D).astype(f32), fourth_block.astype(f32)).astype(bf16)
    d_freq = jnp.einsum('rpc,rq->qpc', d_three.astype(f32), third_block.astype(f32))
    grad_kernel = jnp.transpose((d_freq * spectrum).astype(bf16), (2, 0, 1))
    d_spec = (d_freq * kernel_t).astype(bf16)
    d_one = jnp.einsum('qpc,qa->apc', d_spec.astype(f32), second_block.astype(f32)).astype(bf16)
    d_cube = jnp.einsum('apc,pb->abc', d_one.astype(f32), first_block.astype(f32)).reshape(length, D)
    d_value = (d_cube + skip_gain * d_mix.astype(f32)).astype(bf16)
    grad_tokens = (jnp.dot(d_value, w_value.T, preferred_element_type=f32) + jnp.dot(d_gate, w_gate.T, preferred_element_type=f32)).astype(bf16)
    factor = 1.0 / jnp.sqrt(jnp.asarray(length, f32))
    grad_value_w = jnp.dot(tokens.T, d_value, preferred_element_type=f32) * factor
    grad_gate_w = jnp.dot(tokens.T, d_gate, preferred_element_type=f32) * factor
    grad_skip = lax.optimization_barrier(jnp.sum(d_mix.astype(f32) * value.astype(f32), axis=0)) * factor
    return (grad_tokens, grad_kernel, jnp.stack([grad_value_w, grad_gate_w]), grad_skip)
```

```python
import jax
import jax.numpy as jnp
from jax import lax
from jax.sharding import PartitionSpec as P

D = 512
N1 = 256
N2 = 256


def partners(n):
    return [0] + list(range(n - 1, 0, -1))


def exchange(pieces, steps):
    n = lax.axis_size("seq")
    out = []
    for piece, k in zip(pieces, steps):
        if k == 0:
            out.append(piece)
        else:
            out.append(lax.ppermute(piece, "seq", [(i, i ^ k) for i in range(n)]))
    return out


def swap(array, steps):
    me = lax.axis_index("seq")
    pieces = [lax.dynamic_index_in_dim(array, me ^ k, 0, keepdims=False) for k in steps]
    return jnp.stack(exchange(pieces, steps))


def on_device(
    tokens,
    w_value,
    w_gate,
    first_block,
    second_block,
    third_block,
    fourth_block,
    kernel,
    skip_gain,
    cotangent,
):
    f32 = jnp.float32
    bf16 = jnp.bfloat16
    n = lax.axis_size("seq")
    me = lax.axis_index("seq")
    rows = N1 // n
    chans = D // n
    local_rows = tokens.shape[0]
    steps = partners(n)
    order = me ^ jnp.array(steps)
    inverse = jnp.array([steps.index(k) for k in range(n)])[me ^ jnp.arange(n)]
    value = jnp.dot(tokens, w_value, preferred_element_type=f32).astype(bf16)
    gate = jnp.dot(tokens, w_gate, preferred_element_type=f32).astype(bf16)
    upstream = cotangent.astype(f32)
    d_mix = (upstream * gate.astype(f32)).astype(bf16)
    cube = value.reshape(rows, N2, D)
    section_one = jnp.einsum("abc,pb->cap", cube, first_block, preferred_element_type=f32).astype(
        bf16
    )
    one_in = swap(section_one.reshape(n, chans, rows, N2), steps)
    d_mix_cube = d_mix.reshape(rows, N2, D)
    d_three = jnp.einsum(
        "rsc,sp->crp", d_mix_cube, fourth_block, preferred_element_type=f32
    ).astype(bf16)
    three_in = swap(d_three.reshape(n, chans, rows, N2), steps)
    second_order = second_block.reshape(N1, n, rows)[:, order]
    third_order = third_block.reshape(n, rows, N1)[order]
    spectrum = jnp.einsum("kcap,qka->cqp", one_in, second_order, preferred_element_type=f32)
    filtered = (spectrum * kernel.astype(f32)).astype(bf16)
    section_three = jnp.einsum(
        "cqp,drq->dcrp", filtered, third_block.reshape(n, rows, N1), preferred_element_type=f32
    ).astype(bf16)
    three_out = swap(section_three, steps)[inverse]
    d_freq = jnp.einsum("kcrp,krq->cqp", three_in, third_order, preferred_element_type=f32)
    grad_kernel = (d_freq * spectrum).astype(bf16)
    d_spec = (d_freq * kernel.astype(f32)).astype(bf16)
    d_one = jnp.einsum(
        "cqp,qda->dcap", d_spec, second_block.reshape(N1, n, rows), preferred_element_type=f32
    ).astype(bf16)
    one_out = swap(d_one, steps)[inverse]
    conv = jnp.einsum(
        "kcrp,sp->rskc", three_out, fourth_block, preferred_element_type=f32
    )
    mixed = conv.reshape(local_rows, D) + skip_gain * value.astype(f32)
    d_gate = (upstream * mixed).astype(bf16)
    factor = 1.0 / jnp.sqrt(jnp.asarray(N1 * N2, f32))

    def total(term):
        parts = swap(term.astype(bf16).reshape(n, -1, D), steps)
        mine = jnp.sum(parts.astype(f32), axis=0).astype(bf16)
        got = jnp.stack(exchange([mine] * n, steps))[inverse]
        return got.reshape(term.shape).astype(f32)

    gate_total = total(jnp.dot(tokens.T, d_gate, preferred_element_type=f32) * factor)
    skip_term = jnp.sum(d_mix.astype(f32) * value.astype(f32), axis=0) * factor
    skip_total = lax.psum(skip_term.astype(bf16), "seq").astype(f32)
    d_cube = jnp.einsum("kcap,pb->abkc", one_out, first_block, preferred_element_type=f32)
    d_value = (d_cube.reshape(local_rows, D) + skip_gain * d_mix.astype(f32)).astype(bf16)
    grad_tokens = (
        jnp.dot(d_value, w_value.T, preferred_element_type=f32)
        + jnp.dot(d_gate, w_gate.T, preferred_element_type=f32)
    ).astype(bf16)
    value_total = total(jnp.dot(tokens.T, d_value, preferred_element_type=f32) * factor)
    return (grad_tokens, grad_kernel, jnp.stack([value_total, gate_total]), skip_total)


def solution(mesh):
    in_specs = (
        P(("parts", "seq"), None),
        P(),
        P(),
        P(),
        P(),
        P(),
        P(),
        P("seq", None, None),
        P(),
        P(("parts", "seq"), None),
    )
    out_specs = (
        P(("parts", "seq"), None),
        P(("parts", "seq"), None, None),
        P("parts", None, None),
        P("parts"),
    )
    return jax.shard_map(
        on_device, mesh=mesh, in_specs=in_specs, out_specs=out_specs, check_vma=False
    )
```

```python
import functools

import jax
import jax.numpy as jnp
from jax import lax
from jax.experimental import pallas as pl
from jax.experimental.pallas import tpu as pltpu
from jax.sharding import PartitionSpec as P

D = 512
N1 = 256
N2 = 256
GROUP = 16
VMEM_LIMIT = 56 * 1024 * 1024

f32 = jnp.float32
bf16 = jnp.bfloat16


def dot_nn(a, b):
    return jnp.dot(a, b, preferred_element_type=f32)


def dot_nt(a, b):
    return lax.dot_general(a, b, (((1,), (1,)), ((), ())), preferred_element_type=f32)


def dot_tn(a, b):
    return lax.dot_general(a, b, (((0,), (0,)), ((), ())), preferred_element_type=f32)


def params():
    return pltpu.CompilerParams(vmem_limit_bytes=VMEM_LIMIT)


def whole(shape):
    return pl.BlockSpec(shape, lambda i: (0,) * len(shape))


def rows_of(step):
    return pl.BlockSpec((N2, D), lambda i: (i, 0))


def by_device(n, chans):
    return pl.BlockSpec((n, 1, chans, N2), lambda i: (0, i, 0, 0))


def section_one_kernel(tokens, w_value, first, out, w_turned):
    @pl.when(pl.program_id(0) == 0)
    def _():
        w_turned[...] = w_value[...].T

    value_t = dot_nt(w_turned[...], tokens[...]).astype(bf16)
    section = dot_nt(value_t, first[...]).astype(bf16)
    out[...] = section.reshape(out.shape)


def d_three_kernel(
    tokens, cotangent, w_value, w_gate, fourth, out, value_out, d_mix_out, skip_out
):
    value = dot_nn(tokens[...], w_value[...]).astype(bf16)
    gate = dot_nn(tokens[...], w_gate[...]).astype(bf16)
    d_mix = (cotangent[...].astype(f32) * gate.astype(f32)).astype(bf16)
    value_out[...] = value
    d_mix_out[...] = d_mix
    term = jnp.sum(d_mix.astype(f32) * value.astype(f32), axis=0, keepdims=True)

    @pl.when(pl.program_id(0) == 0)
    def _():
        skip_out[...] = jnp.zeros_like(skip_out)

    skip_out[...] += term
    section = dot_tn(d_mix, fourth[...]).astype(bf16)
    out[...] = section.reshape(out.shape)


def turn_in(swap, arrived, by_channel):
    def body(i, _):
        rows = pl.ds(pl.multiple_of(i * GROUP, GROUP), GROUP)
        block = arrived[rows].reshape(GROUP * GROUP, N2)
        turned = dot_nn(swap[...], block).astype(bf16)
        by_channel[:, rows, :] = turned.reshape(GROUP, GROUP, N2)
        return 0

    lax.fori_loop(0, N1 // GROUP, body, 0, unroll=2)


def turn_out(swap, by_channel, out):
    def body(i, _):
        rows = pl.ds(pl.multiple_of(i * GROUP, GROUP), GROUP)
        block = by_channel[:, rows, :].reshape(GROUP * GROUP, N2)
        turned = dot_nn(swap[...], block).astype(bf16)
        out[rows] = turned.reshape(GROUP, GROUP, N2)
        return 0

    lax.fori_loop(0, N1 // GROUP, body, 0, unroll=2)


def home_forward_kernel(arrived, kernel, second, third, swap, out, spectrum_out, by_channel):
    turn_in(swap, arrived, by_channel)

    def body(c, _):
        spectrum = dot_nn(second[...], by_channel[c])
        spectrum_out[c] = spectrum
        filtered = (spectrum * kernel[c].astype(f32)).astype(bf16)
        by_channel[c] = dot_nn(third[...], filtered).astype(bf16)
        return 0

    lax.fori_loop(0, GROUP, body, 0, unroll=2)
    turn_out(swap, by_channel, out)


def home_backward_kernel(
    arrived, kernel, spectrum, second_t, third_t, swap, out, grad_kernel, by_channel
):
    turn_in(swap, arrived, by_channel)

    def body(c, _):
        d_freq = dot_nn(third_t[...], by_channel[c])
        grad_kernel[c] = (d_freq * spectrum[c]).astype(bf16)
        d_spec = (d_freq * kernel[c].astype(f32)).astype(bf16)
        by_channel[c] = dot_nn(second_t[...], d_spec).astype(bf16)
        return 0

    lax.fori_loop(0, GROUP, body, 0, unroll=2)
    turn_out(swap, by_channel, out)


def accumulate(total, term):
    @pl.when(pl.program_id(0) == 0)
    def _():
        total[...] = term

    @pl.when(pl.program_id(0) > 0)
    def _():
        total[...] += term


def gate_kernel(
    arrived, tokens, value, cotangent, fourth, w_gate, skip, factor, partial, grad_w, total
):
    conv = dot_nt(fourth[...], arrived[...].reshape(D, N2))
    mixed = conv + skip[...] * value[...].astype(f32)
    d_gate = (cotangent[...].astype(f32) * mixed).astype(bf16)
    partial[...] = dot_nt(d_gate, w_gate[...])
    accumulate(total, dot_tn(tokens[...], d_gate))

    @pl.when(pl.program_id(0) == pl.num_programs(0) - 1)
    def _():
        grad_w[...] = (total[...] * factor[0, 0]).astype(bf16)


def value_kernel(
    arrived, tokens, d_mix, partial, first_t, w_value, skip, factor, grad_tokens, grad_w, total
):
    d_cube = dot_nt(first_t[...], arrived[...].reshape(D, N2))
    d_value = (d_cube + skip[...] * d_mix[...].astype(f32)).astype(bf16)
    grad_tokens[...] = (partial[...] + dot_nt(d_value, w_value[...])).astype(bf16)
    accumulate(total, dot_tn(tokens[...], d_value))

    @pl.when(pl.program_id(0) == pl.num_programs(0) - 1)
    def _():
        grad_w[...] = (total[...] * factor[0, 0]).astype(bf16)


def on_device(
    tokens,
    w_value,
    w_gate,
    first_block,
    second_block,
    third_block,
    fourth_block,
    kernel,
    skip_gain,
    cotangent,
):
    n = lax.axis_size("seq")
    rows = N1 // n
    chans = D // n
    local_rows = tokens.shape[0]
    sections = (n, rows, chans, N2)
    factor = (1.0 / jnp.sqrt(jnp.asarray(N1 * N2, f32))).reshape(1, 1)
    skip = skip_gain.reshape(1, D)
    square = whole((D, D))
    block = whole((N1, N2))
    line = whole((1, D))
    row = rows_of(0)
    sent = by_device(n, chans)
    one = pl.BlockSpec(memory_space=pltpu.SMEM)
    place = jnp.arange(GROUP * GROUP)
    swap = (
        place[None, :] == ((place % GROUP) * GROUP + place // GROUP)[:, None]
    ).astype(bf16)

    def cost(gflop, mib):
        scale = rows / 16
        return pl.CostEstimate(
            flops=int(gflop * 1e9 * scale), bytes_accessed=int(mib * 2**20 * scale), transcendentals=0
        )

    def shape(dims, dtype=bf16):
        return jax.ShapeDtypeStruct(dims, dtype)

    def transfer(array):
        return lax.all_to_all(array, "seq", split_axis=0, concat_axis=0, tiled=True)

    one_sent = pl.pallas_call(
        section_one_kernel,
        grid=(rows,),
        in_specs=[row, square, block],
        out_specs=sent,
        out_shape=shape(sections),
        scratch_shapes=[pltpu.VMEM((D, D), bf16)],
        compiler_params=params(),
        cost_estimate=cost(3.2, 9),
    )(tokens, w_value, first_block)
    one_home = transfer(one_sent)

    three_sent, value, d_mix, skip_term = pl.pallas_call(
        d_three_kernel,
        grid=(rows,),
        in_specs=[row, row, square, square, block],
        out_specs=[sent, row, row, line],
        out_shape=[
            shape(sections),
            shape((local_rows, D)),
            shape((local_rows, D)),
            shape((1, D), f32),
        ],
        compiler_params=params(),
        cost_estimate=cost(5.4, 21),
    )(tokens, cotangent, w_value, w_gate, fourth_block)
    three_home = transfer(three_sent)

    at_home = pl.BlockSpec((N1, GROUP, N2), lambda i: (0, i, 0))
    filters = pl.BlockSpec((GROUP, N1, N2), lambda i: (i, 0, 0))
    three_back, spectrum = pl.pallas_call(
        home_forward_kernel,
        grid=(chans // GROUP,),
        in_specs=[at_home, filters, block, block, block],
        out_specs=[at_home, filters],
        out_shape=[shape((N1, chans, N2)), shape((chans, N1, N2), f32)],
        scratch_shapes=[pltpu.VMEM((GROUP, N1, N2), bf16)],
        compiler_params=params(),
        cost_estimate=cost(4.3, 20),
    )(one_home.reshape(N1, chans, N2), kernel, second_block, third_block, swap)
    three_here = transfer(three_back.reshape(sections))

    one_back, grad_kernel = pl.pallas_call(
        home_backward_kernel,
        grid=(chans // GROUP,),
        in_specs=[at_home, filters, filters, block, block, block],
        out_specs=[at_home, filters],
        out_shape=[shape((N1, chans, N2)), shape((chans, N1, N2))],
        scratch_shapes=[pltpu.VMEM((GROUP, N1, N2), bf16)],
        compiler_params=params(),
        cost_estimate=cost(4.3, 24),
    )(
        three_home.reshape(N1, chans, N2),
        kernel,
        spectrum,
        second_block.T,
        third_block.T,
        swap,
    )
    one_here = transfer(one_back.reshape(sections))

    partial, gate_term = pl.pallas_call(
        gate_kernel,
        grid=(rows,),
        in_specs=[sent, row, row, row, block, square, line, one],
        out_specs=[row, square],
        out_shape=[shape((local_rows, D), f32), shape((D, D))],
        scratch_shapes=[pltpu.VMEM((D, D), f32)],
        compiler_params=params(),
        cost_estimate=cost(5.4, 25),
    )(three_here, tokens, value, cotangent, fourth_block, w_gate, skip, factor)

    grad_tokens, value_term = pl.pallas_call(
        value_kernel,
        grid=(rows,),
        in_specs=[sent, row, row, row, block, square, line, one],
        out_specs=[row, square],
        out_shape=[shape((local_rows, D)), shape((D, D))],
        scratch_shapes=[pltpu.VMEM((D, D), f32)],
        compiler_params=params(),
        cost_estimate=cost(5.4, 25),
    )(one_here, tokens, d_mix, partial, first_block.T, w_value, skip, factor)

    gate_total, skip_total = lax.psum(
        (gate_term, (skip_term.reshape(D) * factor[0, 0]).astype(bf16)), "seq"
    )
    parts = transfer(value_term.reshape(n, D // n, D))
    mine = jnp.sum(parts.astype(f32), axis=0).astype(bf16)
    value_total = transfer(jnp.broadcast_to(mine, (n, D // n, D))).reshape(D, D)
    return (
        grad_tokens,
        grad_kernel,
        jnp.stack([value_total, gate_total]).astype(f32),
        skip_total.astype(f32),
    )


def solution(mesh):
    in_specs = (
        P(("parts", "seq"), None),
        P(),
        P(),
        P(),
        P(),
        P(),
        P(),
        P("seq", None, None),
        P(),
        P(("parts", "seq"), None),
    )
    out_specs = (
        P(("parts", "seq"), None),
        P(("parts", "seq"), None, None),
        P("parts", None, None),
        P("parts"),
    )
    return jax.shard_map(
        on_device, mesh=mesh, in_specs=in_specs, out_specs=out_specs, check_vma=False
    )
```

```python
import functools

import jax
import jax.numpy as jnp
from jax import lax
from jax.experimental import pallas as pl
from jax.experimental.pallas import tpu as pltpu
from jax.sharding import PartitionSpec as P

D = 512
N1 = 256
N2 = 256
GROUP = 16
VMEM_LIMIT = 56 * 1024 * 1024

f32 = jnp.float32
bf16 = jnp.bfloat16


def dot_nn(a, b):
    return jnp.dot(a, b, preferred_element_type=f32)


def dot_nt(a, b):
    return lax.dot_general(a, b, (((1,), (1,)), ((), ())), preferred_element_type=f32)


def dot_tn(a, b):
    return lax.dot_general(a, b, (((0,), (0,)), ((), ())), preferred_element_type=f32)


def params():
    return pltpu.CompilerParams(vmem_limit_bytes=VMEM_LIMIT)


def whole(shape):
    return pl.BlockSpec(shape, lambda i: (0,) * len(shape))


def rows_of(per):
    return pl.BlockSpec((per * N2, D), lambda i: (i, 0))


def by_device(n, per, chans):
    return pl.BlockSpec((n, per, chans, N2), lambda i: (0, i, 0, 0))


def row_slice(r):
    return slice(r * N2, (r + 1) * N2)


def section_one_kernel(tokens, w_value, first, out, w_turned, first_turned):
    @pl.when(pl.program_id(0) == 0)
    def _():
        w_turned[...] = w_value[...].T
        first_turned[...] = first[...].T

    n, per, chans, _ = out.shape
    for r in range(per):
        value_t = dot_nt(w_turned[...], tokens[row_slice(r)]).astype(bf16)
        section = dot_nn(value_t, first_turned[...]).astype(bf16)
        out[:, r] = section.reshape(n, chans, N2)


def d_three_kernel(
    tokens,
    cotangent,
    w_value,
    w_gate,
    fourth,
    out,
    value_out,
    d_mix_out,
    tokens_t_out,
    skip_out,
):
    n, per, chans, _ = out.shape

    @pl.when(pl.program_id(0) == 0)
    def _():
        skip_out[...] = jnp.zeros_like(skip_out)

    for r in range(per):
        here = row_slice(r)
        value = dot_nn(tokens[here], w_value[...]).astype(bf16)
        gate = dot_nn(tokens[here], w_gate[...]).astype(bf16)
        d_mix = (cotangent[here].astype(f32) * gate.astype(f32)).astype(bf16)
        value_out[here] = value
        d_mix_out[here] = d_mix
        tokens_t_out[:, here] = tokens[here].T
        skip_out[...] += jnp.sum(
            d_mix.astype(f32) * value.astype(f32), axis=0, keepdims=True
        )
        section = dot_tn(d_mix, fourth[...]).astype(bf16)
        out[:, r] = section.reshape(n, chans, N2)


def turn_in(swap, arrived, by_channel):
    def body(i, _):
        rows = pl.ds(pl.multiple_of(i * GROUP, GROUP), GROUP)
        block = arrived[rows].reshape(GROUP * GROUP, N2)
        turned = dot_nn(swap[...], block).astype(bf16)
        by_channel[:, rows, :] = turned.reshape(GROUP, GROUP, N2)
        return 0

    lax.fori_loop(0, N1 // GROUP, body, 0, unroll=2)


def turn_out(swap, by_channel, out):
    def body(i, _):
        rows = pl.ds(pl.multiple_of(i * GROUP, GROUP), GROUP)
        block = by_channel[:, rows, :].reshape(GROUP * GROUP, N2)
        turned = dot_nn(swap[...], block).astype(bf16)
        out[rows] = turned.reshape(GROUP, GROUP, N2)
        return 0

    lax.fori_loop(0, N1 // GROUP, body, 0, unroll=2)


def home_forward_kernel(arrived, kernel, second, third, swap, out, spectrum_out, by_channel):
    turn_in(swap, arrived, by_channel)

    def body(c, _):
        spectrum = dot_nn(second[...], by_channel[c])
        spectrum_out[c] = spectrum
        filtered = (spectrum * kernel[c].astype(f32)).astype(bf16)
        by_channel[c] = dot_nn(third[...], filtered).astype(bf16)
        return 0

    lax.fori_loop(0, GROUP, body, 0, unroll=2)
    turn_out(swap, by_channel, out)


def home_backward_kernel(
    arrived, kernel, spectrum, second_t, third_t, swap, out, grad_kernel, by_channel
):
    turn_in(swap, arrived, by_channel)

    def body(c, _):
        d_freq = dot_nn(third_t[...], by_channel[c])
        grad_kernel[c] = (d_freq * spectrum[c]).astype(bf16)
        d_spec = (d_freq * kernel[c].astype(f32)).astype(bf16)
        by_channel[c] = dot_nn(second_t[...], d_spec).astype(bf16)
        return 0

    lax.fori_loop(0, GROUP, body, 0, unroll=2)
    turn_out(swap, by_channel, out)


def accumulate(total, term):
    @pl.when(pl.program_id(0) == 0)
    def _():
        total[...] = term

    @pl.when(pl.program_id(0) > 0)
    def _():
        total[...] += term


def finish(total, factor, grad_w):
    @pl.when(pl.program_id(0) == pl.num_programs(0) - 1)
    def _():
        grad_w[...] = (total[...] * factor[0, 0]).astype(bf16)


def gate_kernel(
    arrived,
    tokens_t,
    value,
    cotangent,
    fourth,
    w_gate_t,
    skip,
    factor,
    partial,
    grad_w,
    total,
    d_gate,
):
    for r in range(arrived.shape[1]):
        here = row_slice(r)
        conv = dot_nt(fourth[...], arrived[:, r].reshape(D, N2))
        mixed = conv + skip[...] * value[here].astype(f32)
        d_gate[here] = (cotangent[here].astype(f32) * mixed).astype(bf16)
        partial[here] = dot_nn(d_gate[here], w_gate_t[...])
    accumulate(total, dot_nn(tokens_t[...], d_gate[...]))
    finish(total, factor, grad_w)


def value_kernel(arrived, tokens_t, d_mix, first_t, skip, factor, _, d_value, grad_w, total):
    for r in range(arrived.shape[1]):
        here = row_slice(r)
        d_cube = dot_nt(first_t[...], arrived[:, r].reshape(D, N2))
        d_value[here] = (d_cube + skip[...] * d_mix[here].astype(f32)).astype(bf16)
    accumulate(total, dot_nn(tokens_t[...], d_value[...]))
    finish(total, factor, grad_w)


def tokens_kernel(d_value, partial, w_value_t, grad_tokens):
    for r in range(d_value.shape[0] // N2):
        here = row_slice(r)
        grad_tokens[here] = (
            partial[here] + dot_nn(d_value[here], w_value_t[...])
        ).astype(bf16)


def on_device(
    tokens,
    w_value,
    w_gate,
    first_block,
    second_block,
    third_block,
    fourth_block,
    kernel,
    skip_gain,
    cotangent,
):
    n = lax.axis_size("seq")
    rows = N1 // n
    chans = D // n
    local_rows = tokens.shape[0]
    sections = (n, rows, chans, N2)
    factor = (1.0 / jnp.sqrt(jnp.asarray(N1 * N2, f32))).reshape(1, 1)
    skip = skip_gain.reshape(1, D)
    square = whole((D, D))
    block = whole((N1, N2))
    line = whole((1, D))
    per = min(4, rows)
    row = rows_of(per)
    column = pl.BlockSpec((D, per * N2), lambda i: (0, i))
    sent = by_device(n, per, chans)
    one = pl.BlockSpec(memory_space=pltpu.SMEM)
    place = jnp.arange(GROUP * GROUP)
    swap = (
        place[None, :] == ((place % GROUP) * GROUP + place // GROUP)[:, None]
    ).astype(bf16)

    def cost(gflop, mib):
        scale = rows / 16
        return pl.CostEstimate(
            flops=int(gflop * 1e9 * scale), bytes_accessed=int(mib * 2**20 * scale), transcendentals=0
        )

    def shape(dims, dtype=bf16):
        return jax.ShapeDtypeStruct(dims, dtype)

    def transfer(array):
        return lax.all_to_all(array, "seq", split_axis=0, concat_axis=0, tiled=True)

    one_sent = pl.pallas_call(
        section_one_kernel,
        grid=(rows // per,),
        in_specs=[row, square, block],
        out_specs=sent,
        out_shape=shape(sections),
        scratch_shapes=[pltpu.VMEM((D, D), bf16), pltpu.VMEM((N2, N2), bf16)],
        compiler_params=params(),
        cost_estimate=cost(3.2, 9),
    )(tokens, w_value, first_block)
    one_home = transfer(one_sent)

    three_sent, value, d_mix, tokens_t, skip_term = pl.pallas_call(
        d_three_kernel,
        grid=(rows // per,),
        in_specs=[row, row, square, square, block],
        out_specs=[sent, row, row, column, line],
        out_shape=[
            shape(sections),
            shape((local_rows, D)),
            shape((local_rows, D)),
            shape((D, local_rows)),
            shape((1, D), f32),
        ],
        compiler_params=params(),
        cost_estimate=cost(5.4, 25),
    )(tokens, cotangent, w_value, w_gate, fourth_block)
    three_home = transfer(three_sent)

    at_home = pl.BlockSpec((N1, GROUP, N2), lambda i: (0, i, 0))
    filters = pl.BlockSpec((GROUP, N1, N2), lambda i: (i, 0, 0))
    three_back, spectrum = pl.pallas_call(
        home_forward_kernel,
        grid=(chans // GROUP,),
        in_specs=[at_home, filters, block, block, block],
        out_specs=[at_home, filters],
        out_shape=[shape((N1, chans, N2)), shape((chans, N1, N2), f32)],
        scratch_shapes=[pltpu.VMEM((GROUP, N1, N2), bf16)],
        compiler_params=params(),
        cost_estimate=cost(4.3, 20),
    )(one_home.reshape(N1, chans, N2), kernel, second_block, third_block, swap)
    three_here = transfer(three_back.reshape(sections))

    one_back, grad_kernel = pl.pallas_call(
        home_backward_kernel,
        grid=(chans // GROUP,),
        in_specs=[at_home, filters, filters, block, block, block],
        out_specs=[at_home, filters],
        out_shape=[shape((N1, chans, N2)), shape((chans, N1, N2))],
        scratch_shapes=[pltpu.VMEM((GROUP, N1, N2), bf16)],
        compiler_params=params(),
        cost_estimate=cost(4.3, 24),
    )(
        three_home.reshape(N1, chans, N2),
        kernel,
        spectrum,
        second_block.T,
        third_block.T,
        swap,
    )
    one_here = transfer(one_back.reshape(sections))

    partial, gate_term = pl.pallas_call(
        gate_kernel,
        grid=(rows // per,),
        in_specs=[sent, column, row, row, block, square, line, one],
        out_specs=[row, square],
        out_shape=[shape((local_rows, D), f32), shape((D, D))],
        scratch_shapes=[pltpu.VMEM((D, D), f32), pltpu.VMEM((per * N2, D), bf16)],
        compiler_params=params(),
        cost_estimate=cost(5.4, 25),
    )(three_here, tokens_t, value, cotangent, fourth_block, w_gate.T, skip, factor)

    skip_rows = jnp.pad((skip_term * factor[0, 0]).astype(bf16), ((0, GROUP - 1), (0, 0)))
    early = lax.psum(jnp.concatenate([gate_term, skip_rows]), "seq")

    d_value, value_term = pl.pallas_call(
        value_kernel,
        grid=(rows // per,),
        in_specs=[sent, column, row, block, line, one, pl.BlockSpec(memory_space=pl.ANY)],
        out_specs=[row, square],
        out_shape=[shape((local_rows, D)), shape((D, D))],
        scratch_shapes=[pltpu.VMEM((D, D), f32)],
        compiler_params=params(),
        cost_estimate=cost(3.3, 17),
    )(one_here, tokens_t, d_mix, first_block.T, skip, factor, early)

    parts = transfer(value_term.reshape(n, D // n, D))
    grad_tokens = pl.pallas_call(
        tokens_kernel,
        grid=(rows // per,),
        in_specs=[row, row, square],
        out_specs=row,
        out_shape=shape((local_rows, D)),
        compiler_params=params(),
        cost_estimate=cost(2.1, 16),
    )(d_value, partial, w_value.T)
    mine = jnp.sum(parts.astype(f32), axis=0).astype(bf16)
    value_total = transfer(jnp.broadcast_to(mine, (n, D // n, D))).reshape(D, D)
    gate_total, skip_total = early[:D], early[D]
    return (
        grad_tokens,
        grad_kernel,
        jnp.stack([value_total, gate_total]).astype(f32),
        skip_total.astype(f32),
    )


def solution(mesh):
    in_specs = (
        P(("parts", "seq"), None),
        P(),
        P(),
        P(),
        P(),
        P(),
        P(),
        P("seq", None, None),
        P(),
        P(("parts", "seq"), None),
    )
    out_specs = (
        P(("parts", "seq"), None),
        P(("parts", "seq"), None, None),
        P("parts", None, None),
        P("parts"),
    )
    return jax.shard_map(
        on_device, mesh=mesh, in_specs=in_specs, out_specs=out_specs, check_vma=False
    )
```

```python
import functools

import jax
import jax.numpy as jnp
from jax import lax
from jax.experimental import pallas as pl
from jax.experimental.pallas import tpu as pltpu
from jax.sharding import PartitionSpec as P

D = 512
N1 = 256
N2 = 256
GROUP = 16
LANES = 128
VMEM_LIMIT = 56 * 1024 * 1024

f32 = jnp.float32
bf16 = jnp.bfloat16


def dot_nn(a, b):
    return jnp.dot(a, b, preferred_element_type=f32)


def dot_nt(a, b):
    return lax.dot_general(a, b, (((1,), (1,)), ((), ())), preferred_element_type=f32)


def dot_tn(a, b):
    return lax.dot_general(a, b, (((0,), (0,)), ((), ())), preferred_element_type=f32)


def params():
    return pltpu.CompilerParams(vmem_limit_bytes=VMEM_LIMIT)


def whole(shape):
    return pl.BlockSpec(shape, lambda i: (0,) * len(shape))


def rows_of(per):
    return pl.BlockSpec((per * N2, D), lambda i: (i, 0))


def by_device(n, per, chans):
    return pl.BlockSpec((n, per, chans, N2), lambda i: (0, i, 0, 0))


def row_slice(r):
    return slice(r * N2, (r + 1) * N2)


def section_one_kernel(tokens, w_value, first, out, w_turned, first_turned):
    @pl.when(pl.program_id(0) == 0)
    def _():
        w_turned[...] = w_value[...].T
        first_turned[...] = first[...].T

    n, per, chans, _ = out.shape
    for r in range(per):
        value_t = dot_nt(w_turned[...], tokens[row_slice(r)]).astype(bf16)
        section = dot_nn(value_t, first_turned[...]).astype(bf16)
        out[:, r] = section.reshape(n, chans, N2)


def d_three_kernel(
    tokens,
    cotangent,
    w_value,
    w_gate,
    fourth,
    out,
    value_out,
    d_mix_out,
    tokens_t_out,
    skip_out,
):
    n, per, chans, _ = out.shape

    @pl.when(pl.program_id(0) == 0)
    def _():
        skip_out[...] = jnp.zeros_like(skip_out)

    for r in range(per):
        here = row_slice(r)
        value = dot_nn(tokens[here], w_value[...]).astype(bf16)
        gate = dot_nn(tokens[here], w_gate[...]).astype(bf16)
        d_mix = (cotangent[here].astype(f32) * gate.astype(f32)).astype(bf16)
        value_out[here] = value
        d_mix_out[here] = d_mix
        tokens_t_out[:, here] = tokens[here].T
        skip_out[...] += jnp.sum(
            d_mix.astype(f32) * value.astype(f32), axis=0, keepdims=True
        )
        section = dot_tn(d_mix, fourth[...]).astype(bf16)
        out[:, r] = section.reshape(n, chans, N2)


def turn_in(swap, arrived, by_channel):
    def body(i, _):
        rows = pl.ds(pl.multiple_of(i * GROUP, GROUP), GROUP)
        block = arrived[rows].reshape(GROUP * GROUP, N2)
        turned = dot_nn(swap[...], block).astype(bf16)
        by_channel[:, rows, :] = turned.reshape(GROUP, GROUP, N2)
        return 0

    lax.fori_loop(0, N1 // GROUP, body, 0, unroll=2)


def turn_out(swap, by_channel, out):
    def body(i, _):
        rows = pl.ds(pl.multiple_of(i * GROUP, GROUP), GROUP)
        block = by_channel[:, rows, :].reshape(GROUP * GROUP, N2)
        turned = dot_nn(swap[...], block).astype(bf16)
        out[rows] = turned.reshape(GROUP, GROUP, N2)
        return 0

    lax.fori_loop(0, N1 // GROUP, body, 0, unroll=2)


def home_forward_kernel(arrived, kernel, second, third, swap, out, spectrum_out, by_channel):
    turn_in(swap, arrived, by_channel)

    def body(c, _):
        spectrum = dot_nn(second[...], by_channel[c])
        spectrum_out[c] = spectrum
        filtered = (spectrum * kernel[c].astype(f32)).astype(bf16)
        by_channel[c] = dot_nn(third[...], filtered).astype(bf16)
        return 0

    lax.fori_loop(0, GROUP, body, 0, unroll=2)
    turn_out(swap, by_channel, out)


def home_backward_kernel(
    arrived, kernel, spectrum, second_t, third_t, swap, out, grad_kernel, by_channel
):
    turn_in(swap, arrived, by_channel)

    def body(c, _):
        d_freq = dot_nn(third_t[...], by_channel[c])
        grad_kernel[c] = (d_freq * spectrum[c]).astype(bf16)
        d_spec = (d_freq * kernel[c].astype(f32)).astype(bf16)
        by_channel[c] = dot_nn(second_t[...], d_spec).astype(bf16)
        return 0

    lax.fori_loop(0, GROUP, body, 0, unroll=2)
    turn_out(swap, by_channel, out)


def accumulate(total, term):
    @pl.when(pl.program_id(0) == 0)
    def _():
        total[...] = term

    @pl.when(pl.program_id(0) > 0)
    def _():
        total[...] += term


def finish(total, factor, grad_w):
    @pl.when(pl.program_id(0) == pl.num_programs(0) - 1)
    def _():
        grad_w[...] = (total[...] * factor[0, 0]).astype(bf16)


def gate_kernel(
    arrived,
    tokens_t,
    value,
    cotangent,
    fourth,
    w_gate_t,
    skip,
    factor,
    partial,
    grad_w,
    total,
    d_gate,
):
    for r in range(arrived.shape[1]):
        here = row_slice(r)
        conv = dot_nt(fourth[...], arrived[:, r].reshape(D, N2))
        mixed = conv + skip[...] * value[here].astype(f32)
        d_gate[here] = (cotangent[here].astype(f32) * mixed).astype(bf16)
        partial[here] = dot_nn(d_gate[here], w_gate_t[...])
    accumulate(total, dot_nn(tokens_t[...], d_gate[...]))
    finish(total, factor, grad_w)


def value_row(arrived, d_mix, first_t, skip, r):
    d_cube = dot_nt(first_t[...], arrived[:, r].reshape(D, N2))
    return (d_cube + skip[...] * d_mix[row_slice(r)].astype(f32)).astype(bf16)


def value_kernel(arrived, tokens_t, d_mix, first_t, skip, factor, _, grad_w, total, d_value):
    for r in range(arrived.shape[1]):
        d_value[row_slice(r)] = value_row(arrived, d_mix, first_t, skip, r)
    accumulate(total, dot_nn(tokens_t[...], d_value[...]))
    finish(total, factor, grad_w)


def tokens_kernel(arrived, d_mix, partial, first_t, skip, w_value_t, grad_tokens):
    for r in range(arrived.shape[1]):
        d_value = value_row(arrived, d_mix, first_t, skip, r)
        grad_tokens[row_slice(r)] = (
            partial[row_slice(r)] + dot_nn(d_value, w_value_t[...])
        ).astype(bf16)


def sum_over_seq(term, n):
    me = lax.axis_index("seq")
    bits = n.bit_length() - 1

    def from_partner(array, b):
        return lax.ppermute(array, "seq", [(i, i ^ (1 << b)) for i in range(n)])

    part = term.reshape((2,) * bits + (term.shape[0] // n, term.shape[1]))
    for b in range(bits):
        axis = bits - 1 - b
        bit = (me >> b) & 1
        kept = lax.dynamic_index_in_dim(part, bit, axis, keepdims=False)
        sent = lax.dynamic_index_in_dim(part, 1 - bit, axis, keepdims=False)
        part = (kept.astype(f32) + from_partner(sent, b).astype(f32)).astype(bf16)
    for b in reversed(range(bits)):
        axis = bits - 1 - b
        bit = (me >> b) & 1
        other = from_partner(part, b)
        part = jnp.where(
            bit == 0, jnp.stack([part, other], axis), jnp.stack([other, part], axis)
        )
    return part.reshape(term.shape)


def on_device(
    tokens,
    w_value,
    w_gate,
    first_block,
    second_block,
    third_block,
    fourth_block,
    kernel,
    skip_gain,
    cotangent,
):
    n = lax.axis_size("seq")
    rows = N1 // n
    chans = D // n
    local_rows = tokens.shape[0]
    sections = (n, rows, chans, N2)
    factor = (1.0 / jnp.sqrt(jnp.asarray(N1 * N2, f32))).reshape(1, 1)
    skip = skip_gain.reshape(1, D)
    square = whole((D, D))
    block = whole((N1, N2))
    line = whole((1, D))
    per = min(4, rows)
    row = rows_of(per)
    column = pl.BlockSpec((D, per * N2), lambda i: (0, i))
    sent = by_device(n, per, chans)
    one = pl.BlockSpec(memory_space=pltpu.SMEM)
    place = jnp.arange(GROUP * GROUP)
    swap = (
        place[None, :] == ((place % GROUP) * GROUP + place // GROUP)[:, None]
    ).astype(bf16)

    def cost(gflop, mib):
        scale = rows / 16
        return pl.CostEstimate(
            flops=int(gflop * 1e9 * scale), bytes_accessed=int(mib * 2**20 * scale), transcendentals=0
        )

    def shape(dims, dtype=bf16):
        return jax.ShapeDtypeStruct(dims, dtype)

    def transfer(array):
        return lax.all_to_all(array, "seq", split_axis=0, concat_axis=0, tiled=True)

    one_sent = pl.pallas_call(
        section_one_kernel,
        grid=(rows // per,),
        in_specs=[row, square, block],
        out_specs=sent,
        out_shape=shape(sections),
        scratch_shapes=[pltpu.VMEM((D, D), bf16), pltpu.VMEM((N2, N2), bf16)],
        compiler_params=params(),
        cost_estimate=cost(3.2, 9),
    )(tokens, w_value, first_block)
    one_home = transfer(one_sent)

    three_sent, value, d_mix, tokens_t, skip_term = pl.pallas_call(
        d_three_kernel,
        grid=(rows // per,),
        in_specs=[row, row, square, square, block],
        out_specs=[sent, row, row, column, line],
        out_shape=[
            shape(sections),
            shape((local_rows, D)),
            shape((local_rows, D)),
            shape((D, local_rows)),
            shape((1, D), f32),
        ],
        compiler_params=params(),
        cost_estimate=cost(5.4, 25),
    )(tokens, cotangent, w_value, w_gate, fourth_block)
    three_home = transfer(three_sent)

    at_home = pl.BlockSpec((N1, GROUP, N2), lambda i: (0, i, 0))
    filters = pl.BlockSpec((GROUP, N1, N2), lambda i: (i, 0, 0))
    three_back, spectrum = pl.pallas_call(
        home_forward_kernel,
        grid=(chans // GROUP,),
        in_specs=[at_home, filters, block, block, block],
        out_specs=[at_home, filters],
        out_shape=[shape((N1, chans, N2)), shape((chans, N1, N2), f32)],
        scratch_shapes=[pltpu.VMEM((GROUP, N1, N2), bf16)],
        compiler_params=params(),
        cost_estimate=cost(4.3, 20),
    )(one_home.reshape(N1, chans, N2), kernel, second_block, third_block, swap)
    three_here = transfer(three_back.reshape(sections))

    one_back, grad_kernel = pl.pallas_call(
        home_backward_kernel,
        grid=(chans // GROUP,),
        in_specs=[at_home, filters, filters, block, block, block],
        out_specs=[at_home, filters],
        out_shape=[shape((N1, chans, N2)), shape((chans, N1, N2))],
        scratch_shapes=[pltpu.VMEM((GROUP, N1, N2), bf16)],
        compiler_params=params(),
        cost_estimate=cost(4.3, 24),
    )(
        three_home.reshape(N1, chans, N2),
        kernel,
        spectrum,
        second_block.T,
        third_block.T,
        swap,
    )
    one_here = transfer(one_back.reshape(sections))

    partial, gate_term = pl.pallas_call(
        gate_kernel,
        grid=(rows // per,),
        in_specs=[sent, column, row, row, block, square, line, one],
        out_specs=[row, square],
        out_shape=[shape((local_rows, D), f32), shape((D, D))],
        scratch_shapes=[pltpu.VMEM((D, D), f32), pltpu.VMEM((per * N2, D), bf16)],
        compiler_params=params(),
        cost_estimate=cost(5.4, 25),
    )(three_here, tokens_t, value, cotangent, fourth_block, w_gate.T, skip, factor)

    skip_lanes = jnp.broadcast_to((skip_term * factor[0, 0]).astype(bf16).T, (D, LANES))
    early = sum_over_seq(jnp.concatenate([gate_term, skip_lanes], axis=1), n)

    first_t = first_block.T
    value_term = pl.pallas_call(
        value_kernel,
        grid=(rows // per,),
        in_specs=[sent, column, row, block, line, one, pl.BlockSpec(memory_space=pl.ANY)],
        out_specs=square,
        out_shape=shape((D, D)),
        scratch_shapes=[pltpu.VMEM((D, D), f32), pltpu.VMEM((per * N2, D), bf16)],
        compiler_params=params(),
        cost_estimate=cost(3.3, 13),
    )(one_here, tokens_t, d_mix, first_t, skip, factor, early)

    parts = transfer(value_term.reshape(n, D // n, D))
    grad_tokens = pl.pallas_call(
        tokens_kernel,
        grid=(rows // per,),
        in_specs=[sent, row, row, block, line, square],
        out_specs=row,
        out_shape=shape((local_rows, D)),
        compiler_params=params(),
        cost_estimate=cost(3.3, 20),
    )(one_here, d_mix, partial, first_t, skip, w_value.T)
    mine = jnp.sum(parts.astype(f32), axis=0).astype(bf16)
    value_total = transfer(jnp.broadcast_to(mine, (n, D // n, D))).reshape(D, D)
    gate_total, skip_total = early[:, :D], early[:, D]
    return (
        grad_tokens,
        grad_kernel,
        jnp.stack([value_total, gate_total]).astype(f32),
        skip_total.astype(f32),
    )


def solution(mesh):
    in_specs = (
        P(("parts", "seq"), None),
        P(),
        P(),
        P(),
        P(),
        P(),
        P(),
        P("seq", None, None),
        P(),
        P(("parts", "seq"), None),
    )
    out_specs = (
        P(("parts", "seq"), None),
        P(("parts", "seq"), None, None),
        P("parts", None, None),
        P("parts"),
    )
    return jax.shard_map(
        on_device, mesh=mesh, in_specs=in_specs, out_specs=out_specs, check_vma=False
    )
```

```python
import functools

import jax
import jax.numpy as jnp
from jax import lax
from jax.experimental import pallas as pl
from jax.experimental.pallas import tpu as pltpu
from jax.sharding import PartitionSpec as P

D = 512
N1 = 256
N2 = 256
GROUP = 16
LANES = 128
VMEM_LIMIT = 56 * 1024 * 1024

f32 = jnp.float32
bf16 = jnp.bfloat16


def dot_nn(a, b):
    return jnp.dot(a, b, preferred_element_type=f32)


def dot_nt(a, b):
    return lax.dot_general(a, b, (((1,), (1,)), ((), ())), preferred_element_type=f32)


def params():
    return pltpu.CompilerParams(vmem_limit_bytes=VMEM_LIMIT)


def whole(shape):
    return pl.BlockSpec(shape, lambda i: (0,) * len(shape))


def rows_of(per):
    return pl.BlockSpec((per * N2, D), lambda i: (i, 0))


def by_device(n, per, chans):
    return pl.BlockSpec((n, per, chans, N2), lambda i: (0, i, 0, 0))


def row_slice(r):
    return slice(r * N2, (r + 1) * N2)


def section_one_kernel(tokens, w_value, first, out, first_turned):
    @pl.when(pl.program_id(0) == 0)
    def _():
        first_turned[...] = first[...].T

    n, per, chans, _ = out.shape
    value = dot_nn(tokens[...], w_value[...]).astype(bf16)
    for r in range(per):
        section = dot_nn(value[row_slice(r)].T, first_turned[...]).astype(bf16)
        out[:, r] = section.reshape(n, chans, N2)


def d_three_kernel(
    tokens,
    cotangent,
    w_value,
    w_gate,
    fourth,
    out,
    value_out,
    d_mix_out,
    d_mix_t_out,
    tokens_t_out,
    skip_out,
):
    n, per, chans, _ = out.shape

    @pl.when(pl.program_id(0) == 0)
    def _():
        skip_out[...] = jnp.zeros_like(skip_out)

    for r in range(per):
        here = row_slice(r)
        value = dot_nn(tokens[here], w_value[...]).astype(bf16)
        gate = dot_nn(tokens[here], w_gate[...]).astype(bf16)
        d_mix = (cotangent[here].astype(f32) * gate.astype(f32)).astype(bf16)
        value_out[here] = value
        d_mix_out[here] = d_mix
        tokens_t_out[:, here] = tokens[here].T
        skip_out[...] += jnp.sum(
            d_mix.astype(f32) * value.astype(f32), axis=0, keepdims=True
        )
        d_mix_t = d_mix.T
        d_mix_t_out[:, here] = d_mix_t
        section = dot_nn(d_mix_t, fourth[...]).astype(bf16)
        out[:, r] = section.reshape(n, chans, N2)


def turn_in(swap, arrived, by_channel):
    def body(i, _):
        rows = pl.ds(pl.multiple_of(i * GROUP, GROUP), GROUP)
        block = arrived[rows].reshape(GROUP * GROUP, N2)
        turned = dot_nn(swap[...], block).astype(bf16)
        by_channel[:, rows, :] = turned.reshape(GROUP, GROUP, N2)
        return 0

    lax.fori_loop(0, N1 // GROUP, body, 0, unroll=2)


def turn_out(swap, by_channel, out):
    def body(i, _):
        rows = pl.ds(pl.multiple_of(i * GROUP, GROUP), GROUP)
        block = by_channel[:, rows, :].reshape(GROUP * GROUP, N2)
        turned = dot_nn(swap[...], block).astype(bf16)
        out[rows] = turned.reshape(GROUP, GROUP, N2)
        return 0

    lax.fori_loop(0, N1 // GROUP, body, 0, unroll=2)


def home_forward_kernel(arrived, kernel, second, third, swap, out, spectrum_out, by_channel):
    turn_in(swap, arrived, by_channel)

    def body(c, _):
        spectrum = dot_nn(second[...], by_channel[c])
        spectrum_out[c] = spectrum
        filtered = (spectrum * kernel[c].astype(f32)).astype(bf16)
        by_channel[c] = dot_nn(third[...], filtered).astype(bf16)
        return 0

    lax.fori_loop(0, GROUP, body, 0, unroll=2)
    turn_out(swap, by_channel, out)


def home_backward_kernel(
    arrived, kernel, spectrum, second_t, third_t, swap, out, grad_kernel, by_channel
):
    turn_in(swap, arrived, by_channel)

    def body(c, _):
        d_freq = dot_nn(third_t[...], by_channel[c])
        grad_kernel[c] = (d_freq * spectrum[c]).astype(bf16)
        d_spec = (d_freq * kernel[c].astype(f32)).astype(bf16)
        by_channel[c] = dot_nn(second_t[...], d_spec).astype(bf16)
        return 0

    lax.fori_loop(0, GROUP, body, 0, unroll=2)
    turn_out(swap, by_channel, out)


def accumulate(total, term):
    @pl.when(pl.program_id(0) == 0)
    def _():
        total[...] = term

    @pl.when(pl.program_id(0) > 0)
    def _():
        total[...] += term


def finish(total, factor, grad_w):
    @pl.when(pl.program_id(0) == pl.num_programs(0) - 1)
    def _():
        grad_w[...] = (total[...] * factor[0, 0]).astype(bf16)


def gate_kernel(
    arrived,
    tokens_t,
    value,
    cotangent,
    fourth,
    w_gate_t,
    skip,
    factor,
    partial,
    grad_w,
    total,
    d_gate,
):
    for r in range(arrived.shape[1]):
        here = row_slice(r)
        conv = dot_nt(fourth[...], arrived[:, r].reshape(D, N2))
        mixed = conv + skip[...] * value[here].astype(f32)
        d_gate[here] = (cotangent[here].astype(f32) * mixed).astype(bf16)
        partial[here] = dot_nn(d_gate[here], w_gate_t[...])
    accumulate(total, dot_nn(tokens_t[...], d_gate[...]))
    finish(total, factor, grad_w)


def value_kernel(
    arrived, tokens, d_mix_t, first, skip_column, factor, _, grad_w, total, d_value_t
):
    for r in range(arrived.shape[1]):
        here = row_slice(r)
        d_cube_t = dot_nn(arrived[:, r].reshape(D, N2), first[...])
        d_value_t[:, here] = (
            d_cube_t + skip_column[...] * d_mix_t[:, here].astype(f32)
        ).astype(bf16)
    accumulate(total, dot_nn(d_value_t[...], tokens[...]))

    @pl.when(pl.program_id(0) == pl.num_programs(0) - 1)
    def _():
        grad_w[...] = (total[...] * factor[0, 0]).astype(bf16).T


def tokens_kernel(arrived, d_mix, partial, first_t, skip, w_value_t, grad_tokens):
    for r in range(arrived.shape[1]):
        here = row_slice(r)
        d_cube = dot_nt(first_t[...], arrived[:, r].reshape(D, N2))
        d_value = (d_cube + skip[...] * d_mix[here].astype(f32)).astype(bf16)
        grad_tokens[here] = (partial[here] + dot_nn(d_value, w_value_t[...])).astype(bf16)


def sum_kernel(parts, _, out):
    total = jnp.sum(parts[...].astype(f32), axis=0, keepdims=True).astype(bf16)
    out[...] = jnp.broadcast_to(total, out.shape)


def from_partner(array, b, n):
    return lax.ppermute(array, "seq", [(i, i ^ (1 << b)) for i in range(n)])


def halve_over_seq(term, n):
    me = lax.axis_index("seq")
    bits = n.bit_length() - 1
    part = term.reshape((2,) * bits + (term.shape[0] // n, term.shape[1]))
    for b in range(bits):
        axis = bits - 1 - b
        bit = (me >> b) & 1
        kept = lax.dynamic_index_in_dim(part, bit, axis, keepdims=False)
        sent = lax.dynamic_index_in_dim(part, 1 - bit, axis, keepdims=False)
        part = (kept.astype(f32) + from_partner(sent, b, n).astype(f32)).astype(bf16)
    return part


def double_over_seq(part, n):
    me = lax.axis_index("seq")
    bits = n.bit_length() - 1
    lanes = part.shape[-1]
    for b in reversed(range(bits)):
        axis = bits - 1 - b
        bit = (me >> b) & 1
        other = from_partner(part, b, n)
        part = jnp.where(
            bit == 0, jnp.stack([part, other], axis), jnp.stack([other, part], axis)
        )
    return part.reshape(-1, lanes)


def on_device(
    tokens,
    w_value,
    w_gate,
    first_block,
    second_block,
    third_block,
    fourth_block,
    kernel,
    skip_gain,
    cotangent,
):
    n = lax.axis_size("seq")
    rows = N1 // n
    chans = D // n
    local_rows = tokens.shape[0]
    sections = (n, rows, chans, N2)
    factor = (1.0 / jnp.sqrt(jnp.asarray(N1 * N2, f32))).reshape(1, 1)
    skip = skip_gain.reshape(1, D)
    square = whole((D, D))
    block = whole((N1, N2))
    line = whole((1, D))
    per = min(4, rows)
    row = rows_of(per)
    column = pl.BlockSpec((D, per * N2), lambda i: (0, i))
    sent = by_device(n, per, chans)
    one = pl.BlockSpec(memory_space=pltpu.SMEM)
    place = jnp.arange(GROUP * GROUP)
    swap = (
        place[None, :] == ((place % GROUP) * GROUP + place // GROUP)[:, None]
    ).astype(bf16)

    def cost(gflop, mib):
        scale = rows / 16
        return pl.CostEstimate(
            flops=int(gflop * 1e9 * scale), bytes_accessed=int(mib * 2**20 * scale), transcendentals=0
        )

    def shape(dims, dtype=bf16):
        return jax.ShapeDtypeStruct(dims, dtype)

    def transfer(array):
        return lax.all_to_all(array, "seq", split_axis=0, concat_axis=0, tiled=True)

    one_sent = pl.pallas_call(
        section_one_kernel,
        grid=(rows // per,),
        in_specs=[row, square, block],
        out_specs=sent,
        out_shape=shape(sections),
        scratch_shapes=[pltpu.VMEM((N2, N2), bf16)],
        compiler_params=params(),
        cost_estimate=cost(3.2, 9),
    )(tokens, w_value, first_block)
    one_home = transfer(one_sent)

    three_sent, value, d_mix, d_mix_t, tokens_t, skip_term = pl.pallas_call(
        d_three_kernel,
        grid=(rows // per,),
        in_specs=[row, row, square, square, block],
        out_specs=[sent, row, row, column, column, line],
        out_shape=[
            shape(sections),
            shape((local_rows, D)),
            shape((local_rows, D)),
            shape((D, local_rows)),
            shape((D, local_rows)),
            shape((1, D), f32),
        ],
        compiler_params=params(),
        cost_estimate=cost(5.4, 25),
    )(tokens, cotangent, w_value, w_gate, fourth_block)
    three_home = transfer(three_sent)

    at_home = pl.BlockSpec((N1, GROUP, N2), lambda i: (0, i, 0))
    filters = pl.BlockSpec((GROUP, N1, N2), lambda i: (i, 0, 0))
    three_back, spectrum = pl.pallas_call(
        home_forward_kernel,
        grid=(chans // GROUP,),
        in_specs=[at_home, filters, block, block, block],
        out_specs=[at_home, filters],
        out_shape=[shape((N1, chans, N2)), shape((chans, N1, N2), f32)],
        scratch_shapes=[pltpu.VMEM((GROUP, N1, N2), bf16)],
        compiler_params=params(),
        cost_estimate=cost(4.3, 20),
    )(one_home.reshape(N1, chans, N2), kernel, second_block, third_block, swap)
    three_here = transfer(three_back.reshape(sections))

    one_back, grad_kernel = pl.pallas_call(
        home_backward_kernel,
        grid=(chans // GROUP,),
        in_specs=[at_home, filters, filters, block, block, block],
        out_specs=[at_home, filters],
        out_shape=[shape((N1, chans, N2)), shape((chans, N1, N2))],
        scratch_shapes=[pltpu.VMEM((GROUP, N1, N2), bf16)],
        compiler_params=params(),
        cost_estimate=cost(4.3, 24),
    )(
        three_home.reshape(N1, chans, N2),
        kernel,
        spectrum,
        second_block.T,
        third_block.T,
        swap,
    )
    one_here = transfer(one_back.reshape(sections))

    partial, gate_term = pl.pallas_call(
        gate_kernel,
        grid=(rows // per,),
        in_specs=[sent, column, row, row, block, square, line, one],
        out_specs=[row, square],
        out_shape=[shape((local_rows, D), f32), shape((D, D))],
        scratch_shapes=[pltpu.VMEM((D, D), f32), pltpu.VMEM((per * N2, D), bf16)],
        compiler_params=params(),
        cost_estimate=cost(5.4, 25),
    )(three_here, tokens_t, value, cotangent, fourth_block, w_gate.T, skip, factor)

    skip_lanes = jnp.broadcast_to((skip_term * factor[0, 0]).astype(bf16).T, (D, LANES))
    early = halve_over_seq(jnp.concatenate([gate_term, skip_lanes], axis=1), n)

    unread = pl.BlockSpec(memory_space=pl.ANY)
    value_term = pl.pallas_call(
        value_kernel,
        grid=(rows // per,),
        in_specs=[sent, row, column, block, whole((D, 1)), one, unread],
        out_specs=square,
        out_shape=shape((D, D)),
        scratch_shapes=[pltpu.VMEM((D, D), f32), pltpu.VMEM((D, per * N2), bf16)],
        compiler_params=params(),
        cost_estimate=cost(3.3, 13),
    )(one_here, tokens, d_mix_t, first_block, skip_gain.reshape(D, 1), factor, early)

    parts = transfer(value_term.reshape(n, D // n, D))
    grad_tokens = pl.pallas_call(
        tokens_kernel,
        grid=(rows // per,),
        in_specs=[sent, row, row, block, line, square],
        out_specs=row,
        out_shape=shape((local_rows, D)),
        compiler_params=params(),
        cost_estimate=cost(3.3, 20),
    )(one_here, d_mix, partial, first_block.T, skip, w_value.T)
    own = pl.pallas_call(
        sum_kernel,
        grid=(1,),
        in_specs=[whole(parts.shape), unread],
        out_specs=whole(parts.shape),
        out_shape=shape(parts.shape),
        compiler_params=params(),
        cost_estimate=cost(0.001, 1),
    )(parts, grad_tokens)
    value_total = transfer(own).reshape(D, D)
    early = double_over_seq(early, n)
    gate_total, skip_total = early[:, :D], early[:, D]
    return (
        grad_tokens,
        grad_kernel,
        jnp.stack([value_total, gate_total]).astype(f32),
        skip_total.astype(f32),
    )


def solution(mesh):
    in_specs = (
        P(("parts", "seq"), None),
        P(),
        P(),
        P(),
        P(),
        P(),
        P(),
        P("seq", None, None),
        P(),
        P(("parts", "seq"), None),
    )
    out_specs = (
        P(("parts", "seq"), None),
        P(("parts", "seq"), None, None),
        P("parts", None, None),
        P("parts"),
    )
    return jax.shard_map(
        on_device, mesh=mesh, in_specs=in_specs, out_specs=out_specs, check_vma=False
    )
```

```python
import functools

import functools

import jax
import jax.numpy as jnp
from jax import lax
from jax.experimental import pallas as pl
from jax.experimental.pallas import tpu as pltpu
from jax.sharding import PartitionSpec as P

D = 512
N1 = 256
N2 = 256
GROUP = 16
LANES = 128
VMEM_LIMIT = 56 * 1024 * 1024

f32 = jnp.float32
bf16 = jnp.bfloat16


def dot_nn(a, b):
    return jnp.dot(a, b, preferred_element_type=f32)


def dot_nt(a, b):
    return lax.dot_general(a, b, (((1,), (1,)), ((), ())), preferred_element_type=f32)


def params():
    return pltpu.CompilerParams(vmem_limit_bytes=VMEM_LIMIT)


def whole(shape):
    return pl.BlockSpec(shape, lambda i: (0,) * len(shape))


def rows_of(per):
    return pl.BlockSpec((per * N2, D), lambda i: (i, 0))


def by_device(n, per, chans):
    return pl.BlockSpec((n, per, chans, N2), lambda i: (0, i, 0, 0))


def row_slice(r):
    return slice(r * N2, (r + 1) * N2)


def section_one_kernel(
    per, tokens, w_value, first, out, tokens_v, w_v, first_v, out_v, arrive, leave
):
    n, rows, chans, _ = out.shape
    chunks = rows // per
    in_first = pltpu.make_async_copy(first, first_v, arrive.at[chunks])
    in_w = pltpu.make_async_copy(w_value, w_v, arrive.at[chunks + 1])
    in_tokens = [
        pltpu.make_async_copy(
            tokens.at[pl.ds(i * per * N2, per * N2)],
            tokens_v.at[pl.ds(i * per * N2, per * N2)],
            arrive.at[i],
        )
        for i in range(chunks)
    ]
    outs = [
        pltpu.make_async_copy(
            out_v.at[:, pl.ds(i * per, per)], out.at[:, pl.ds(i * per, per)], leave.at[i]
        )
        for i in range(chunks)
    ]
    in_w.start()
    in_tokens[0].start()
    in_first.start()
    for copy in in_tokens[1:]:
        copy.start()
    in_w.wait()
    for i in range(chunks):
        in_tokens[i].wait()
        value = dot_nn(tokens_v[i * per * N2 : (i + 1) * per * N2], w_v[...]).astype(bf16)
        if i == 0:
            in_first.wait()
            first_v[...] = first_v[...].T
        for r in range(per):
            section = dot_nn(value[row_slice(r)].T, first_v[...]).astype(bf16)
            out_v[:, i * per + r] = section.reshape(n, chans, N2)
        outs[i].start()
    for copy in outs:
        copy.wait()


def d_three_kernel(
    tokens,
    cotangent,
    w_value,
    w_gate,
    fourth,
    out,
    value_out,
    d_mix_out,
    tokens_t_out,
    skip_out,
):
    n, per, chans, _ = out.shape

    @pl.when(pl.program_id(0) == 0)
    def _():
        skip_out[...] = jnp.zeros_like(skip_out)

    for r in range(per):
        here = row_slice(r)
        value = dot_nn(tokens[here], w_value[...]).astype(bf16)
        gate = dot_nn(tokens[here], w_gate[...]).astype(bf16)
        d_mix = (cotangent[here].astype(f32) * gate.astype(f32)).astype(bf16)
        value_out[here] = value
        d_mix_out[here] = d_mix
        tokens_t_out[:, here] = tokens[here].T
        skip_out[...] += jnp.sum(
            d_mix.astype(f32) * value.astype(f32), axis=0, keepdims=True
        )
        section = dot_nn(d_mix.T, fourth[...]).astype(bf16)
        out[:, r] = section.reshape(n, chans, N2)


def turn_in(swap, arrived, by_channel):
    def body(i, _):
        rows = pl.ds(pl.multiple_of(i * GROUP, GROUP), GROUP)
        block = arrived[rows].reshape(GROUP * GROUP, N2)
        turned = dot_nn(swap[...], block).astype(bf16)
        by_channel[:, rows, :] = turned.reshape(GROUP, GROUP, N2)
        return 0

    lax.fori_loop(0, N1 // GROUP, body, 0, unroll=2)


def turn_out(swap, by_channel, out):
    def body(i, _):
        rows = pl.ds(pl.multiple_of(i * GROUP, GROUP), GROUP)
        block = by_channel[:, rows, :].reshape(GROUP * GROUP, N2)
        turned = dot_nn(swap[...], block).astype(bf16)
        out[rows] = turned.reshape(GROUP, GROUP, N2)
        return 0

    lax.fori_loop(0, N1 // GROUP, body, 0, unroll=2)


def home_forward_kernel(arrived, kernel, second, third, swap, out, spectrum_out, by_channel):
    turn_in(swap, arrived, by_channel)

    def body(c, _):
        spectrum = dot_nn(second[...], by_channel[c])
        spectrum_out[c] = spectrum
        filtered = (spectrum * kernel[c].astype(f32)).astype(bf16)
        by_channel[c] = dot_nn(third[...], filtered).astype(bf16)
        return 0

    lax.fori_loop(0, GROUP, body, 0, unroll=2)
    turn_out(swap, by_channel, out)


def home_backward_kernel(
    arrived, kernel, spectrum, second_t, third_t, swap, out, grad_kernel, by_channel
):
    turn_in(swap, arrived, by_channel)

    def body(c, _):
        d_freq = dot_nn(third_t[...], by_channel[c])
        grad_kernel[c] = (d_freq * spectrum[c]).astype(bf16)
        d_spec = (d_freq * kernel[c].astype(f32)).astype(bf16)
        by_channel[c] = dot_nn(second_t[...], d_spec).astype(bf16)
        return 0

    lax.fori_loop(0, GROUP, body, 0, unroll=2)
    turn_out(swap, by_channel, out)


def accumulate(total, term):
    @pl.when(pl.program_id(0) == 0)
    def _():
        total[...] = term

    @pl.when(pl.program_id(0) > 0)
    def _():
        total[...] += term


def finish(total, factor, grad_w):
    @pl.when(pl.program_id(0) == pl.num_programs(0) - 1)
    def _():
        grad_w[...] = (total[...] * factor[0, 0]).astype(bf16)


def gate_kernel(
    arrived,
    tokens_t,
    value,
    cotangent,
    fourth,
    w_gate_t,
    skip,
    factor,
    partial,
    grad_w,
    total,
    d_gate,
):
    for r in range(arrived.shape[1]):
        here = row_slice(r)
        conv = dot_nt(fourth[...], arrived[:, r].reshape(D, N2))
        mixed = conv + skip[...] * value[here].astype(f32)
        d_gate[here] = (cotangent[here].astype(f32) * mixed).astype(bf16)
        partial[here] = dot_nn(d_gate[here], w_gate_t[...])
    accumulate(total, dot_nn(tokens_t[...], d_gate[...]))
    finish(total, factor, grad_w)


def value_kernel(
    per,
    arrived,
    tokens_t,
    d_mix,
    first_t,
    skip,
    factor,
    _,
    grad_w,
    arrived_v,
    tokens_v,
    d_mix_v,
    d_value,
    total,
    arrive,
):
    rows = arrived.shape[1]
    chunks = rows // per

    def copies(i):
        lines = pl.ds(i * per, per)
        here = pl.ds(i * per * N2, per * N2)
        return [
            pltpu.make_async_copy(
                arrived.at[:, lines], arrived_v.at[:, lines], arrive.at[i, 0]
            ),
            pltpu.make_async_copy(d_mix.at[here], d_mix_v.at[here], arrive.at[i, 1]),
            pltpu.make_async_copy(
                tokens_t.at[:, here], tokens_v.at[:, here], arrive.at[i, 2]
            ),
        ]

    started = [copies(i) for i in range(chunks)]
    for group in started:
        for copy in group:
            copy.start()
    for i in range(chunks):
        started[i][0].wait()
        started[i][1].wait()
        for r in range(i * per, (i + 1) * per):
            here = row_slice(r)
            d_cube = dot_nt(first_t[...], arrived_v[:, r].reshape(D, N2))
            d_value[here] = (d_cube + skip[...] * d_mix_v[here].astype(f32)).astype(bf16)
        started[i][2].wait()
        here = slice(i * per * N2, (i + 1) * per * N2)
        term = dot_nn(tokens_v[:, here], d_value[here])
        if i == 0:
            total[...] = term
        elif i < chunks - 1:
            total[...] += term
        else:
            grad_w[...] = ((total[...] + term) * factor[0, 0]).astype(bf16)


def tokens_kernel(arrived, d_mix, partial, first_t, skip, w_value_t, grad_tokens):
    for r in range(arrived.shape[1]):
        here = row_slice(r)
        d_cube = dot_nt(first_t[...], arrived[:, r].reshape(D, N2))
        d_value = (d_cube + skip[...] * d_mix[here].astype(f32)).astype(bf16)
        grad_tokens[here] = (partial[here] + dot_nn(d_value, w_value_t[...])).astype(bf16)


def sum_kernel(parts, early, _, out, early_out):
    total = jnp.sum(parts[...].astype(f32), axis=0, keepdims=True).astype(bf16)
    out[...] = jnp.broadcast_to(total, out.shape)
    early_out[...] = early[...]


def from_partner(array, b, n):
    return lax.ppermute(array, "seq", [(i, i ^ (1 << b)) for i in range(n)])


def halve_over_seq(term, n):
    me = lax.axis_index("seq")
    bits = n.bit_length() - 1
    part = term.reshape((2,) * bits + (term.shape[0] // n, term.shape[1]))
    for b in range(bits):
        axis = bits - 1 - b
        bit = (me >> b) & 1
        kept = lax.dynamic_index_in_dim(part, bit, axis, keepdims=False)
        sent = lax.dynamic_index_in_dim(part, 1 - bit, axis, keepdims=False)
        part = (kept.astype(f32) + from_partner(sent, b, n).astype(f32)).astype(bf16)
    return part


def double_over_seq(part, n):
    me = lax.axis_index("seq")
    bits = n.bit_length() - 1
    lanes = part.shape[-1]
    for b in reversed(range(bits)):
        axis = bits - 1 - b
        bit = (me >> b) & 1
        other = from_partner(part, b, n)
        part = jnp.where(
            bit == 0, jnp.stack([part, other], axis), jnp.stack([other, part], axis)
        )
    return part.reshape(-1, lanes)


def on_device(
    tokens,
    w_value,
    w_gate,
    first_block,
    second_block,
    third_block,
    fourth_block,
    kernel,
    skip_gain,
    cotangent,
):
    n = lax.axis_size("seq")
    rows = N1 // n
    chans = D // n
    local_rows = tokens.shape[0]
    sections = (n, rows, chans, N2)
    factor = (1.0 / jnp.sqrt(jnp.asarray(N1 * N2, f32))).reshape(1, 1)
    skip = skip_gain.reshape(1, D)
    square = whole((D, D))
    block = whole((N1, N2))
    line = whole((1, D))
    per = min(4, rows)
    row = rows_of(per)
    column = pl.BlockSpec((D, per * N2), lambda i: (0, i))
    sent = by_device(n, per, chans)
    one = pl.BlockSpec(memory_space=pltpu.SMEM)
    place = jnp.arange(GROUP * GROUP)
    swap = (
        place[None, :] == ((place % GROUP) * GROUP + place // GROUP)[:, None]
    ).astype(bf16)

    def cost(gflop, mib):
        scale = rows / 16
        return pl.CostEstimate(
            flops=int(gflop * 1e9 * scale), bytes_accessed=int(mib * 2**20 * scale), transcendentals=0
        )

    def shape(dims, dtype=bf16):
        return jax.ShapeDtypeStruct(dims, dtype)

    def transfer(array):
        return lax.all_to_all(array, "seq", split_axis=0, concat_axis=0, tiled=True)

    unread = pl.BlockSpec(memory_space=pl.ANY)
    one_sent = pl.pallas_call(
        functools.partial(section_one_kernel, per),
        in_specs=[unread] * 3,
        out_specs=unread,
        out_shape=shape(sections),
        scratch_shapes=[
            pltpu.VMEM((local_rows, D), bf16),
            pltpu.VMEM((D, D), bf16),
            pltpu.VMEM((N2, N2), bf16),
            pltpu.VMEM(sections, bf16),
            pltpu.SemaphoreType.DMA((rows // per + 2,)),
            pltpu.SemaphoreType.DMA((rows // per,)),
        ],
        compiler_params=params(),
        cost_estimate=cost(3.2, 9),
    )(tokens, w_value, first_block)
    one_home = transfer(one_sent)

    three_sent, value, d_mix, tokens_t, skip_term = pl.pallas_call(
        d_three_kernel,
        grid=(rows // per,),
        in_specs=[row, row, square, square, block],
        out_specs=[sent, row, row, column, line],
        out_shape=[
            shape(sections),
            shape((local_rows, D)),
            shape((local_rows, D)),
            shape((D, local_rows)),
            shape((1, D), f32),
        ],
        compiler_params=params(),
        cost_estimate=cost(5.4, 25),
    )(tokens, cotangent, w_value, w_gate, fourth_block)
    three_home = transfer(three_sent)

    at_home = pl.BlockSpec((N1, GROUP, N2), lambda i: (0, i, 0))
    filters = pl.BlockSpec((GROUP, N1, N2), lambda i: (i, 0, 0))
    three_back, spectrum = pl.pallas_call(
        home_forward_kernel,
        grid=(chans // GROUP,),
        in_specs=[at_home, filters, block, block, block],
        out_specs=[at_home, filters],
        out_shape=[shape((N1, chans, N2)), shape((chans, N1, N2), f32)],
        scratch_shapes=[pltpu.VMEM((GROUP, N1, N2), bf16)],
        compiler_params=params(),
        cost_estimate=cost(4.3, 20),
    )(one_home.reshape(N1, chans, N2), kernel, second_block, third_block, swap)
    three_here = transfer(three_back.reshape(sections))

    one_back, grad_kernel = pl.pallas_call(
        home_backward_kernel,
        grid=(chans // GROUP,),
        in_specs=[at_home, filters, filters, block, block, block],
        out_specs=[at_home, filters],
        out_shape=[shape((N1, chans, N2)), shape((chans, N1, N2))],
        scratch_shapes=[pltpu.VMEM((GROUP, N1, N2), bf16)],
        compiler_params=params(),
        cost_estimate=cost(4.3, 24),
    )(
        three_home.reshape(N1, chans, N2),
        kernel,
        spectrum,
        second_block.T,
        third_block.T,
        swap,
    )
    one_here = transfer(one_back.reshape(sections))

    partial, gate_term = pl.pallas_call(
        gate_kernel,
        grid=(rows // per,),
        in_specs=[sent, column, row, row, block, square, line, one],
        out_specs=[row, square],
        out_shape=[shape((local_rows, D), f32), shape((D, D))],
        scratch_shapes=[pltpu.VMEM((D, D), f32), pltpu.VMEM((per * N2, D), bf16)],
        compiler_params=params(),
        cost_estimate=cost(5.4, 25),
    )(three_here, tokens_t, value, cotangent, fourth_block, w_gate.T, skip, factor)

    skip_lanes = jnp.broadcast_to((skip_term * factor[0, 0]).astype(bf16).T, (D, LANES))
    early = halve_over_seq(jnp.concatenate([gate_term, skip_lanes], axis=1), n)

    first_t = first_block.T
    in_vmem = pl.BlockSpec(memory_space=pltpu.VMEM)
    value_term = pl.pallas_call(
        functools.partial(value_kernel, per),
        in_specs=[unread, unread, unread, in_vmem, in_vmem, one, unread],
        out_specs=in_vmem,
        out_shape=shape((D, D)),
        scratch_shapes=[
            pltpu.VMEM(sections, bf16),
            pltpu.VMEM((D, local_rows), bf16),
            pltpu.VMEM((local_rows, D), bf16),
            pltpu.VMEM((local_rows, D), bf16),
            pltpu.VMEM((D, D), f32),
            pltpu.SemaphoreType.DMA((rows // per, 3)),
        ],
        compiler_params=params(),
        cost_estimate=cost(3.3, 13),
    )(one_here, tokens_t, d_mix, first_t, skip, factor, early)

    parts = transfer(value_term.reshape(n, D // n, D))
    grad_tokens = pl.pallas_call(
        tokens_kernel,
        grid=(rows // per,),
        in_specs=[sent, row, row, block, line, square],
        out_specs=row,
        out_shape=shape((local_rows, D)),
        compiler_params=params(),
        cost_estimate=cost(3.3, 20),
    )(one_here, d_mix, partial, first_t, skip, w_value.T)
    own, early = pl.pallas_call(
        sum_kernel,
        in_specs=[in_vmem, in_vmem, unread],
        out_specs=[in_vmem, in_vmem],
        out_shape=[shape(parts.shape), shape(early.shape)],
        compiler_params=params(),
        cost_estimate=cost(0.001, 1),
    )(parts, early, grad_tokens)
    value_total = transfer(own).reshape(D, D)
    early = double_over_seq(early, n)
    gate_total, skip_total = early[:, :D], early[:, D]
    return (
        grad_tokens,
        grad_kernel,
        jnp.stack([value_total, gate_total]).astype(f32),
        skip_total.astype(f32),
    )


def solution(mesh):
    in_specs = (
        P(("parts", "seq"), None),
        P(),
        P(),
        P(),
        P(),
        P(),
        P(),
        P("seq", None, None),
        P(),
        P(("parts", "seq"), None),
    )
    out_specs = (
        P(("parts", "seq"), None),
        P(("parts", "seq"), None, None),
        P("parts", None, None),
        P("parts"),
    )
    return jax.shard_map(
        on_device, mesh=mesh, in_specs=in_specs, out_specs=out_specs, check_vma=False
    )
```

```python
import functools

import functools

import jax
import jax.numpy as jnp
import numpy as np
from jax import lax
from jax.experimental import pallas as pl
from jax.experimental.pallas import tpu as pltpu
from jax.sharding import PartitionSpec as P

D = 512
N1 = 256
N2 = 256
GROUP = 16
LANES = 128
VMEM_LIMIT = 56 * 1024 * 1024

f32 = jnp.float32
bf16 = jnp.bfloat16


def dot_nn(a, b):
    return jnp.dot(a, b, preferred_element_type=f32)


def dot_nt(a, b):
    return lax.dot_general(a, b, (((1,), (1,)), ((), ())), preferred_element_type=f32)


def params():
    return pltpu.CompilerParams(vmem_limit_bytes=VMEM_LIMIT)


def whole(shape):
    return pl.BlockSpec(shape, lambda i: (0,) * len(shape))


def rows_of(per):
    return pl.BlockSpec((per * N2, D), lambda i: (i, 0))


def by_device(n, per, chans):
    return pl.BlockSpec((n, per, chans, N2), lambda i: (0, i, 0, 0))


def interleaved(n):
    return [i // 2 + (i % 2) * (n // 2) for i in range(n)]


def reversed_bits(n):
    bits = n.bit_length() - 1
    return [sum(((i >> b) & 1) << (bits - 1 - b) for b in range(bits)) for i in range(n)]


def strided(n):
    return [(i % 4) * (n // 4) + i // 4 for i in range(n)]


def mirrored(n):
    return [n - 1 - i // 2 if i % 2 else i // 2 for i in range(n)]


def to_blocks(section, order, out, r):
    chans = section.shape[0] // len(order)
    for i, device in enumerate(order):
        out[i, r] = section[device * chans : (device + 1) * chans]


def from_blocks(arrived, order, r):
    return jnp.concatenate([arrived[order.index(d), r] for d in range(len(order))])


def row_slice(r):
    return slice(r * N2, (r + 1) * N2)


def section_one_kernel(
    per, order, tokens, w_value, first, out, tokens_v, w_v, first_v, out_v, arrive, leave
):
    n, rows, chans, _ = out.shape
    chunks = rows // per
    in_first = pltpu.make_async_copy(first, first_v, arrive.at[chunks])
    in_w = pltpu.make_async_copy(w_value, w_v, arrive.at[chunks + 1])
    in_tokens = [
        pltpu.make_async_copy(
            tokens.at[pl.ds(i * per * N2, per * N2)],
            tokens_v.at[pl.ds(i * per * N2, per * N2)],
            arrive.at[i],
        )
        for i in range(chunks)
    ]
    outs = [
        pltpu.make_async_copy(
            out_v.at[:, pl.ds(i * per, per)], out.at[:, pl.ds(i * per, per)], leave.at[i]
        )
        for i in range(chunks)
    ]
    in_w.start()
    in_tokens[0].start()
    in_first.start()
    for copy in in_tokens[1:]:
        copy.start()
    in_w.wait()
    for i in range(chunks):
        in_tokens[i].wait()
        value = dot_nn(tokens_v[i * per * N2 : (i + 1) * per * N2], w_v[...]).astype(bf16)
        if i == 0:
            in_first.wait()
            first_v[...] = first_v[...].T
        for r in range(per):
            section = dot_nn(value[row_slice(r)].T, first_v[...]).astype(bf16)
            to_blocks(section, order, out_v, i * per + r)
        outs[i].start()
    for copy in outs:
        copy.wait()


def d_three_kernel(
    order,
    tokens,
    cotangent,
    w_value,
    w_gate,
    fourth,
    out,
    value_out,
    d_mix_out,
    tokens_t_out,
    skip_out,
):
    @pl.when(pl.program_id(0) == 0)
    def _():
        skip_out[...] = jnp.zeros_like(skip_out)

    for r in range(out.shape[1]):
        here = row_slice(r)
        value = dot_nn(tokens[here], w_value[...]).astype(bf16)
        gate = dot_nn(tokens[here], w_gate[...]).astype(bf16)
        d_mix = (cotangent[here].astype(f32) * gate.astype(f32)).astype(bf16)
        value_out[here] = value
        d_mix_out[here] = d_mix
        tokens_t_out[:, here] = tokens[here].T
        skip_out[...] += jnp.sum(
            d_mix.astype(f32) * value.astype(f32), axis=0, keepdims=True
        )
        section = dot_nn(d_mix.T, fourth[...]).astype(bf16)
        to_blocks(section, order, out, r)


def turn_in(swap, arrived, by_channel):
    def body(i, _):
        rows = pl.ds(pl.multiple_of(i * GROUP, GROUP), GROUP)
        block = arrived[rows].reshape(GROUP * GROUP, N2)
        turned = dot_nn(swap[...], block).astype(bf16)
        by_channel[:, rows, :] = turned.reshape(GROUP, GROUP, N2)
        return 0

    lax.fori_loop(0, N1 // GROUP, body, 0, unroll=2)


def turn_out(swap, by_channel, out):
    def body(i, _):
        rows = pl.ds(pl.multiple_of(i * GROUP, GROUP), GROUP)
        block = by_channel[:, rows, :].reshape(GROUP * GROUP, N2)
        turned = dot_nn(swap[...], block).astype(bf16)
        out[rows] = turned.reshape(GROUP, GROUP, N2)
        return 0

    lax.fori_loop(0, N1 // GROUP, body, 0, unroll=2)


def home_forward_kernel(arrived, kernel, second, third, swap, out, spectrum_out, by_channel):
    turn_in(swap, arrived, by_channel)

    def body(c, _):
        spectrum = dot_nn(second[...], by_channel[c])
        spectrum_out[c] = spectrum
        filtered = (spectrum * kernel[c].astype(f32)).astype(bf16)
        by_channel[c] = dot_nn(third[...], filtered).astype(bf16)
        return 0

    lax.fori_loop(0, GROUP, body, 0, unroll=2)
    turn_out(swap, by_channel, out)


def home_backward_kernel(
    arrived, kernel, spectrum, second_t, third_t, swap, out, grad_kernel, by_channel
):
    turn_in(swap, arrived, by_channel)

    def body(c, _):
        d_freq = dot_nn(third_t[...], by_channel[c])
        grad_kernel[c] = (d_freq * spectrum[c]).astype(bf16)
        d_spec = (d_freq * kernel[c].astype(f32)).astype(bf16)
        by_channel[c] = dot_nn(second_t[...], d_spec).astype(bf16)
        return 0

    lax.fori_loop(0, GROUP, body, 0, unroll=2)
    turn_out(swap, by_channel, out)


def accumulate(total, term):
    @pl.when(pl.program_id(0) == 0)
    def _():
        total[...] = term

    @pl.when(pl.program_id(0) > 0)
    def _():
        total[...] += term


def finish(total, factor, grad_w):
    @pl.when(pl.program_id(0) == pl.num_programs(0) - 1)
    def _():
        grad_w[...] = (total[...] * factor[0, 0]).astype(bf16)


def gate_kernel(
    order,
    arrived,
    tokens_t,
    value,
    cotangent,
    fourth,
    w_gate_t,
    skip,
    factor,
    partial,
    grad_w,
    total,
    d_gate,
):
    for r in range(arrived.shape[1]):
        here = row_slice(r)
        conv = dot_nt(fourth[...], from_blocks(arrived, order, r))
        mixed = conv + skip[...] * value[here].astype(f32)
        d_gate[here] = (cotangent[here].astype(f32) * mixed).astype(bf16)
        partial[here] = dot_nn(d_gate[here], w_gate_t[...])
    accumulate(total, dot_nn(tokens_t[...], d_gate[...]))
    finish(total, factor, grad_w)


def value_kernel(
    per,
    order,
    arrived,
    tokens_t,
    d_mix,
    first_t,
    skip,
    factor,
    _,
    grad_w,
    arrived_v,
    tokens_v,
    d_mix_v,
    d_value,
    total,
    arrive,
):
    rows = arrived.shape[1]
    chunks = rows // per

    def copies(i):
        lines = pl.ds(i * per, per)
        here = pl.ds(i * per * N2, per * N2)
        return [
            pltpu.make_async_copy(
                arrived.at[:, lines], arrived_v.at[:, lines], arrive.at[i, 0]
            ),
            pltpu.make_async_copy(d_mix.at[here], d_mix_v.at[here], arrive.at[i, 1]),
            pltpu.make_async_copy(
                tokens_t.at[:, here], tokens_v.at[:, here], arrive.at[i, 2]
            ),
        ]

    started = [copies(i) for i in range(chunks)]
    for group in started:
        for copy in group:
            copy.start()
    for i in range(chunks):
        started[i][0].wait()
        started[i][1].wait()
        for r in range(i * per, (i + 1) * per):
            here = row_slice(r)
            d_cube = dot_nt(first_t[...], from_blocks(arrived_v, order, r))
            d_value[here] = (d_cube + skip[...] * d_mix_v[here].astype(f32)).astype(bf16)
        started[i][2].wait()
        here = slice(i * per * N2, (i + 1) * per * N2)
        term = dot_nn(tokens_v[:, here], d_value[here])
        if i == 0:
            total[...] = term
        elif i < chunks - 1:
            total[...] += term
        else:
            grad_w[...] = ((total[...] + term) * factor[0, 0]).astype(bf16)


def tokens_kernel(order, arrived, d_mix, partial, first_t, skip, w_value_t, grad_tokens):
    for r in range(arrived.shape[1]):
        here = row_slice(r)
        d_cube = dot_nt(first_t[...], from_blocks(arrived, order, r))
        d_value = (d_cube + skip[...] * d_mix[here].astype(f32)).astype(bf16)
        grad_tokens[here] = (partial[here] + dot_nn(d_value, w_value_t[...])).astype(bf16)


def sum_kernel(parts, early, _, out, early_out):
    total = jnp.sum(parts[...].astype(f32), axis=0, keepdims=True).astype(bf16)
    out[...] = jnp.broadcast_to(total, out.shape)
    early_out[...] = early[...]


def from_partner(array, b, n):
    return lax.ppermute(array, "seq", [(i, i ^ (1 << b)) for i in range(n)])


def halve_over_seq(term, n):
    me = lax.axis_index("seq")
    bits = n.bit_length() - 1
    part = term.reshape((2,) * bits + (term.shape[0] // n, term.shape[1]))
    for b in range(bits):
        axis = bits - 1 - b
        bit = (me >> b) & 1
        kept = lax.dynamic_index_in_dim(part, bit, axis, keepdims=False)
        sent = lax.dynamic_index_in_dim(part, 1 - bit, axis, keepdims=False)
        part = (kept.astype(f32) + from_partner(sent, b, n).astype(f32)).astype(bf16)
    return part


def double_over_seq(part, n):
    me = lax.axis_index("seq")
    bits = n.bit_length() - 1
    lanes = part.shape[-1]
    for b in reversed(range(bits)):
        axis = bits - 1 - b
        bit = (me >> b) & 1
        other = from_partner(part, b, n)
        part = jnp.where(
            bit == 0, jnp.stack([part, other], axis), jnp.stack([other, part], axis)
        )
    return part.reshape(-1, lanes)


def on_device(
    tokens,
    w_value,
    w_gate,
    first_block,
    second_block,
    third_block,
    fourth_block,
    kernel,
    skip_gain,
    cotangent,
):
    n = lax.axis_size("seq")
    rows = N1 // n
    chans = D // n
    local_rows = tokens.shape[0]
    sections = (n, rows, chans, N2)
    factor = (1.0 / jnp.sqrt(jnp.asarray(N1 * N2, f32))).reshape(1, 1)
    skip = skip_gain.reshape(1, D)
    square = whole((D, D))
    block = whole((N1, N2))
    line = whole((1, D))
    per = min(4, rows)
    row = rows_of(per)
    column = pl.BlockSpec((D, per * N2), lambda i: (0, i))
    sent = by_device(n, per, chans)
    one = pl.BlockSpec(memory_space=pltpu.SMEM)
    place = jnp.arange(GROUP * GROUP)
    swap = (
        place[None, :] == ((place % GROUP) * GROUP + place // GROUP)[:, None]
    ).astype(bf16)

    def cost(gflop, mib):
        scale = rows / 16
        return pl.CostEstimate(
            flops=int(gflop * 1e9 * scale), bytes_accessed=int(mib * 2**20 * scale), transcendentals=0
        )

    def shape(dims, dtype=bf16):
        return jax.ShapeDtypeStruct(dims, dtype)

    def transfer(array, order=None):
        groups = None if order is None else [order]
        return lax.all_to_all(
            array, "seq", split_axis=0, concat_axis=0, tiled=True, axis_index_groups=groups
        )

    orders = [interleaved(n), reversed_bits(n), strided(n), mirrored(n)]
    places = [np.concatenate([d * rows + np.arange(rows) for d in order]) for order in orders]
    picks = [
        (jnp.asarray(p)[:, None] == jnp.arange(N1)[None, :]).astype(bf16) for p in places
    ]
    unread = pl.BlockSpec(memory_space=pl.ANY)
    one_sent = pl.pallas_call(
        functools.partial(section_one_kernel, per, orders[0]),
        in_specs=[unread] * 3,
        out_specs=unread,
        out_shape=shape(sections),
        scratch_shapes=[
            pltpu.VMEM((local_rows, D), bf16),
            pltpu.VMEM((D, D), bf16),
            pltpu.VMEM((N2, N2), bf16),
            pltpu.VMEM(sections, bf16),
            pltpu.SemaphoreType.DMA((rows // per + 2,)),
            pltpu.SemaphoreType.DMA((rows // per,)),
        ],
        compiler_params=params(),
        cost_estimate=cost(3.2, 9),
    )(tokens, w_value, first_block)
    one_home = transfer(one_sent, orders[0])

    three_sent, value, d_mix, tokens_t, skip_term = pl.pallas_call(
        functools.partial(d_three_kernel, orders[1]),
        grid=(rows // per,),
        in_specs=[row, row, square, square, block],
        out_specs=[sent, row, row, column, line],
        out_shape=[
            shape(sections),
            shape((local_rows, D)),
            shape((local_rows, D)),
            shape((D, local_rows)),
            shape((1, D), f32),
        ],
        compiler_params=params(),
        cost_estimate=cost(5.4, 25),
    )(tokens, cotangent, w_value, w_gate, fourth_block)
    three_home = transfer(three_sent, orders[1])

    at_home = pl.BlockSpec((N1, GROUP, N2), lambda i: (0, i, 0))
    filters = pl.BlockSpec((GROUP, N1, N2), lambda i: (i, 0, 0))
    three_back, spectrum = pl.pallas_call(
        home_forward_kernel,
        grid=(chans // GROUP,),
        in_specs=[at_home, filters, block, block, block],
        out_specs=[at_home, filters],
        out_shape=[shape((N1, chans, N2)), shape((chans, N1, N2), f32)],
        scratch_shapes=[pltpu.VMEM((GROUP, N1, N2), bf16)],
        compiler_params=params(),
        cost_estimate=cost(4.3, 20),
    )(
        one_home.reshape(N1, chans, N2),
        kernel,
        dot_nt(second_block, picks[0]).astype(bf16),
        dot_nn(picks[2], third_block).astype(bf16),
        swap,
    )
    three_here = transfer(three_back.reshape(sections), orders[2])

    one_back, grad_kernel = pl.pallas_call(
        home_backward_kernel,
        grid=(chans // GROUP,),
        in_specs=[at_home, filters, filters, block, block, block],
        out_specs=[at_home, filters],
        out_shape=[shape((N1, chans, N2)), shape((chans, N1, N2))],
        scratch_shapes=[pltpu.VMEM((GROUP, N1, N2), bf16)],
        compiler_params=params(),
        cost_estimate=cost(4.3, 24),
    )(
        three_home.reshape(N1, chans, N2),
        kernel,
        spectrum,
        dot_nt(picks[3], second_block).astype(bf16),
        dot_nn(picks[1], third_block).T.astype(bf16),
        swap,
    )
    one_here = transfer(one_back.reshape(sections), orders[3])

    partial, gate_term = pl.pallas_call(
        functools.partial(gate_kernel, orders[2]),
        grid=(rows // per,),
        in_specs=[sent, column, row, row, block, square, line, one],
        out_specs=[row, square],
        out_shape=[shape((local_rows, D), f32), shape((D, D))],
        scratch_shapes=[pltpu.VMEM((D, D), f32), pltpu.VMEM((per * N2, D), bf16)],
        compiler_params=params(),
        cost_estimate=cost(5.4, 25),
    )(three_here, tokens_t, value, cotangent, fourth_block, w_gate.T, skip, factor)

    skip_lanes = jnp.broadcast_to((skip_term * factor[0, 0]).astype(bf16).T, (D, LANES))
    early = halve_over_seq(jnp.concatenate([gate_term, skip_lanes], axis=1), n)

    first_t = first_block.T
    in_vmem = pl.BlockSpec(memory_space=pltpu.VMEM)
    value_term = pl.pallas_call(
        functools.partial(value_kernel, per, orders[3]),
        in_specs=[unread, unread, unread, in_vmem, in_vmem, one, unread],
        out_specs=in_vmem,
        out_shape=shape((D, D)),
        scratch_shapes=[
            pltpu.VMEM(sections, bf16),
            pltpu.VMEM((D, local_rows), bf16),
            pltpu.VMEM((local_rows, D), bf16),
            pltpu.VMEM((local_rows, D), bf16),
            pltpu.VMEM((D, D), f32),
            pltpu.SemaphoreType.DMA((rows // per, 3)),
        ],
        compiler_params=params(),
        cost_estimate=cost(3.3, 13),
    )(one_here, tokens_t, d_mix, first_t, skip, factor, early)

    parts = transfer(value_term.reshape(n, D // n, D))
    grad_tokens = pl.pallas_call(
        functools.partial(tokens_kernel, orders[3]),
        grid=(rows // per,),
        in_specs=[sent, row, row, block, line, square],
        out_specs=row,
        out_shape=shape((local_rows, D)),
        compiler_params=params(),
        cost_estimate=cost(3.3, 20),
    )(one_here, d_mix, partial, first_t, skip, w_value.T)
    own, early = pl.pallas_call(
        sum_kernel,
        in_specs=[in_vmem, in_vmem, unread],
        out_specs=[in_vmem, in_vmem],
        out_shape=[shape(parts.shape), shape(early.shape)],
        compiler_params=params(),
        cost_estimate=cost(0.001, 1),
    )(parts, early, grad_tokens)
    value_total = transfer(own).reshape(D, D)
    early = double_over_seq(early, n)
    gate_total, skip_total = early[:, :D], early[:, D]
    return (
        grad_tokens,
        grad_kernel,
        jnp.stack([value_total, gate_total]).astype(f32),
        skip_total.astype(f32),
    )


def solution(mesh):
    in_specs = (
        P(("parts", "seq"), None),
        P(),
        P(),
        P(),
        P(),
        P(),
        P(),
        P("seq", None, None),
        P(),
        P(("parts", "seq"), None),
    )
    out_specs = (
        P(("parts", "seq"), None),
        P(("parts", "seq"), None, None),
        P("parts", None, None),
        P("parts"),
    )
    return jax.shard_map(
        on_device, mesh=mesh, in_specs=in_specs, out_specs=out_specs, check_vma=False
    )
```

```python
import functools

import functools

import jax
import jax.numpy as jnp
from jax import lax
from jax.experimental import pallas as pl
from jax.experimental.pallas import tpu as pltpu
from jax.sharding import PartitionSpec as P

D = 512
N1 = 256
N2 = 256
GROUP = 16
LANES = 128
VMEM_LIMIT = 56 * 1024 * 1024

f32 = jnp.float32
bf16 = jnp.bfloat16


def dot_nn(a, b):
    return jnp.dot(a, b, preferred_element_type=f32)


def dot_nt(a, b):
    return lax.dot_general(a, b, (((1,), (1,)), ((), ())), preferred_element_type=f32)


def params():
    return pltpu.CompilerParams(vmem_limit_bytes=VMEM_LIMIT)


def whole(shape):
    return pl.BlockSpec(shape, lambda i: (0,) * len(shape))


def rows_of(per):
    return pl.BlockSpec((per * N2, D), lambda i: (i, 0))


def by_device(n, per, chans):
    return pl.BlockSpec((n, per, chans, N2), lambda i: (0, i, 0, 0))


def row_slice(r):
    return slice(r * N2, (r + 1) * N2)


def section_one_kernel(
    per, tokens, w_value, first, out, tokens_v, w_v, first_v, out_v, arrive, leave
):
    n, rows, chans, _ = out.shape
    chunks = rows // per
    in_first = pltpu.make_async_copy(first, first_v, arrive.at[chunks])
    in_w = pltpu.make_async_copy(w_value, w_v, arrive.at[chunks + 1])
    in_tokens = [
        pltpu.make_async_copy(
            tokens.at[pl.ds(i * per * N2, per * N2)],
            tokens_v.at[pl.ds(i * per * N2, per * N2)],
            arrive.at[i],
        )
        for i in range(chunks)
    ]
    outs = [
        pltpu.make_async_copy(
            out_v.at[:, pl.ds(i * per, per)], out.at[:, pl.ds(i * per, per)], leave.at[i]
        )
        for i in range(chunks)
    ]
    in_w.start()
    in_tokens[0].start()
    in_first.start()
    for copy in in_tokens[1:]:
        copy.start()
    in_w.wait()
    for i in range(chunks):
        in_tokens[i].wait()
        value = dot_nn(tokens_v[i * per * N2 : (i + 1) * per * N2], w_v[...]).astype(bf16)
        if i == 0:
            in_first.wait()
            first_v[...] = first_v[...].T
        for r in range(per):
            section = dot_nn(value[row_slice(r)].T, first_v[...]).astype(bf16)
            out_v[:, i * per + r] = section.reshape(n, chans, N2)
        outs[i].start()
    for copy in outs:
        copy.wait()


def d_three_kernel(
    tokens,
    cotangent,
    w_value,
    w_gate,
    fourth,
    out,
    value_out,
    d_mix_out,
    tokens_t_out,
    skip_out,
):
    n, per, chans, _ = out.shape

    @pl.when(pl.program_id(0) == 0)
    def _():
        skip_out[...] = jnp.zeros_like(skip_out)

    for r in range(per):
        here = row_slice(r)
        value = dot_nn(tokens[here], w_value[...]).astype(bf16)
        gate = dot_nn(tokens[here], w_gate[...]).astype(bf16)
        d_mix = (cotangent[here].astype(f32) * gate.astype(f32)).astype(bf16)
        value_out[here] = value
        d_mix_out[here] = d_mix
        tokens_t_out[:, here] = tokens[here].T
        skip_out[...] += jnp.sum(
            d_mix.astype(f32) * value.astype(f32), axis=0, keepdims=True
        )
        section = dot_nn(d_mix.T, fourth[...]).astype(bf16)
        out[:, r] = section.reshape(n, chans, N2)


def turn_in(swap, arrived, by_channel):
    def body(i, _):
        rows = pl.ds(pl.multiple_of(i * GROUP, GROUP), GROUP)
        block = arrived[rows].reshape(GROUP * GROUP, N2)
        turned = dot_nn(swap[...], block).astype(bf16)
        by_channel[:, rows, :] = turned.reshape(GROUP, GROUP, N2)
        return 0

    lax.fori_loop(0, N1 // GROUP, body, 0, unroll=2)


def turn_out(swap, by_channel, out):
    def body(i, _):
        rows = pl.ds(pl.multiple_of(i * GROUP, GROUP), GROUP)
        block = by_channel[:, rows, :].reshape(GROUP * GROUP, N2)
        turned = dot_nn(swap[...], block).astype(bf16)
        out[rows] = turned.reshape(GROUP, GROUP, N2)
        return 0

    lax.fori_loop(0, N1 // GROUP, body, 0, unroll=2)


def home_forward_kernel(arrived, kernel, second, third, swap, out, spectrum_out, by_channel):
    turn_in(swap, arrived, by_channel)

    def body(c, _):
        spectrum = dot_nn(second[...], by_channel[c])
        spectrum_out[c] = spectrum
        filtered = (spectrum * kernel[c].astype(f32)).astype(bf16)
        by_channel[c] = dot_nn(third[...], filtered).astype(bf16)
        return 0

    lax.fori_loop(0, GROUP, body, 0, unroll=2)
    turn_out(swap, by_channel, out)


def home_backward_kernel(
    arrived, kernel, spectrum, second_t, third_t, swap, out, grad_kernel, by_channel
):
    turn_in(swap, arrived, by_channel)

    def body(c, _):
        d_freq = dot_nn(third_t[...], by_channel[c])
        grad_kernel[c] = (d_freq * spectrum[c]).astype(bf16)
        d_spec = (d_freq * kernel[c].astype(f32)).astype(bf16)
        by_channel[c] = dot_nn(second_t[...], d_spec).astype(bf16)
        return 0

    lax.fori_loop(0, GROUP, body, 0, unroll=2)
    turn_out(swap, by_channel, out)


def accumulate(total, term):
    @pl.when(pl.program_id(0) == 0)
    def _():
        total[...] = term

    @pl.when(pl.program_id(0) > 0)
    def _():
        total[...] += term


def finish(total, factor, grad_w):
    @pl.when(pl.program_id(0) == pl.num_programs(0) - 1)
    def _():
        grad_w[...] = (total[...] * factor[0, 0]).astype(bf16)


def gate_kernel(
    arrived,
    tokens_t,
    value,
    cotangent,
    fourth,
    w_gate_t,
    skip,
    factor,
    partial,
    grad_w,
    total,
    d_gate,
):
    for r in range(arrived.shape[1]):
        here = row_slice(r)
        conv = dot_nt(fourth[...], arrived[:, r].reshape(D, N2))
        mixed = conv + skip[...] * value[here].astype(f32)
        d_gate[here] = (cotangent[here].astype(f32) * mixed).astype(bf16)
        partial[here] = dot_nn(d_gate[here], w_gate_t[...]).astype(bf16)
    accumulate(total, dot_nn(tokens_t[...], d_gate[...]))
    finish(total, factor, grad_w)


def value_kernel(
    per,
    arrived,
    tokens_t,
    d_mix,
    first_t,
    skip,
    factor,
    _,
    grad_w,
    arrived_v,
    tokens_v,
    d_mix_v,
    d_value,
    total,
    arrive,
):
    rows = arrived.shape[1]
    chunks = rows // per

    def copies(i):
        lines = pl.ds(i * per, per)
        here = pl.ds(i * per * N2, per * N2)
        return [
            pltpu.make_async_copy(
                arrived.at[:, lines], arrived_v.at[:, lines], arrive.at[i, 0]
            ),
            pltpu.make_async_copy(d_mix.at[here], d_mix_v.at[here], arrive.at[i, 1]),
            pltpu.make_async_copy(
                tokens_t.at[:, here], tokens_v.at[:, here], arrive.at[i, 2]
            ),
        ]

    started = [copies(i) for i in range(chunks)]
    for group in started:
        for copy in group:
            copy.start()
    for i in range(chunks):
        started[i][0].wait()
        started[i][1].wait()
        for r in range(i * per, (i + 1) * per):
            here = row_slice(r)
            d_cube = dot_nt(first_t[...], arrived_v[:, r].reshape(D, N2))
            d_value[here] = (d_cube + skip[...] * d_mix_v[here].astype(f32)).astype(bf16)
        started[i][2].wait()
        here = slice(i * per * N2, (i + 1) * per * N2)
        term = dot_nn(tokens_v[:, here], d_value[here])
        if i == 0:
            total[...] = term
        elif i < chunks - 1:
            total[...] += term
        else:
            grad_w[...] = ((total[...] + term) * factor[0, 0]).astype(bf16)


def tokens_kernel(arrived, d_mix, partial, first_t, skip, w_value_t, *rest):
    grad_tokens, zero = rest[-2:]
    for r in range(arrived.shape[1]):
        here = row_slice(r)
        d_cube = dot_nt(first_t[...], arrived[:, r].reshape(D, N2))
        d_value = (d_cube + skip[...] * d_mix[here].astype(f32)).astype(bf16)
        grad_tokens[here] = (
            partial[here].astype(f32) + dot_nn(d_value, w_value_t[...])
        ).astype(bf16)
    zero[...] = jnp.zeros_like(zero)


def place_kernel(values, offsets, me, *refs):
    value_parts, gate_parts = refs[:values], refs[values : 2 * values]
    out, skip_out, column = refs[2 * values :]
    here = me[0, 0]
    for distance, part in enumerate(value_parts):
        size = part.shape[0]
        start = pl.multiple_of((here % values ^ distance) * size, size)
        out[0, pl.ds(start, size)] = part[...].astype(f32)
    for distance, part in enumerate(gate_parts):
        size = part.shape[0] // len(offsets)
        for i, offset in enumerate(offsets):
            start = pl.multiple_of((here ^ (distance | offset)) * size, size)
            block = part[i * size : (i + 1) * size].astype(f32)
            out[1, pl.ds(start, size)] = block[:, :D]
            column[pl.ds(start, size)] = block[:, D:]
    skip_out[...] = column[...].T[:1]


def from_partner(array, b, n):
    return lax.ppermute(array, "seq", [(i, i ^ (1 << b)) for i in range(n)])


def halves(part, axis, b):
    bit = (lax.axis_index("seq") >> b) & 1
    kept = lax.dynamic_index_in_dim(part, bit, axis, keepdims=False)
    sent = lax.dynamic_index_in_dim(part, 1 - bit, axis, keepdims=False)
    return kept, sent


def added(kept, got, zero=0.0):
    return (kept.astype(f32) + got.astype(f32) + zero).astype(bf16)


def doubled(part, n):
    other = from_partner(part, 1, n)
    return [part, from_partner(part, 0, n), other, from_partner(other, 0, n)]


def on_device(
    tokens,
    w_value,
    w_gate,
    first_block,
    second_block,
    third_block,
    fourth_block,
    kernel,
    skip_gain,
    cotangent,
):
    n = lax.axis_size("seq")
    rows = N1 // n
    chans = D // n
    local_rows = tokens.shape[0]
    sections = (n, rows, chans, N2)
    factor = (1.0 / jnp.sqrt(jnp.asarray(N1 * N2, f32))).reshape(1, 1)
    skip = skip_gain.reshape(1, D)
    square = whole((D, D))
    block = whole((N1, N2))
    line = whole((1, D))
    per = min(4, rows)
    row = rows_of(per)
    column = pl.BlockSpec((D, per * N2), lambda i: (0, i))
    sent = by_device(n, per, chans)
    one = pl.BlockSpec(memory_space=pltpu.SMEM)
    place = jnp.arange(GROUP * GROUP)
    swap = (
        place[None, :] == ((place % GROUP) * GROUP + place // GROUP)[:, None]
    ).astype(bf16)

    def cost(gflop, mib):
        scale = rows / 16
        return pl.CostEstimate(
            flops=int(gflop * 1e9 * scale), bytes_accessed=int(mib * 2**20 * scale), transcendentals=0
        )

    def shape(dims, dtype=bf16):
        return jax.ShapeDtypeStruct(dims, dtype)

    def transfer(array):
        return lax.all_to_all(array, "seq", split_axis=0, concat_axis=0, tiled=True)

    unread = pl.BlockSpec(memory_space=pl.ANY)
    one_sent = pl.pallas_call(
        functools.partial(section_one_kernel, per),
        in_specs=[unread] * 3,
        out_specs=unread,
        out_shape=shape(sections),
        scratch_shapes=[
            pltpu.VMEM((local_rows, D), bf16),
            pltpu.VMEM((D, D), bf16),
            pltpu.VMEM((N2, N2), bf16),
            pltpu.VMEM(sections, bf16),
            pltpu.SemaphoreType.DMA((rows // per + 2,)),
            pltpu.SemaphoreType.DMA((rows // per,)),
        ],
        compiler_params=params(),
        cost_estimate=cost(3.2, 9),
    )(tokens, w_value, first_block)
    one_home = transfer(one_sent)

    three_sent, value, d_mix, tokens_t, skip_term = pl.pallas_call(
        d_three_kernel,
        grid=(rows // per,),
        in_specs=[row, row, square, square, block],
        out_specs=[sent, row, row, column, line],
        out_shape=[
            shape(sections),
            shape((local_rows, D)),
            shape((local_rows, D)),
            shape((D, local_rows)),
            shape((1, D), f32),
        ],
        compiler_params=params(),
        cost_estimate=cost(5.4, 25),
    )(tokens, cotangent, w_value, w_gate, fourth_block)
    three_home = transfer(three_sent)

    at_home = pl.BlockSpec((N1, GROUP, N2), lambda i: (0, i, 0))
    filters = pl.BlockSpec((GROUP, N1, N2), lambda i: (i, 0, 0))
    three_back, spectrum = pl.pallas_call(
        home_forward_kernel,
        grid=(chans // GROUP,),
        in_specs=[at_home, filters, block, block, block],
        out_specs=[at_home, filters],
        out_shape=[shape((N1, chans, N2)), shape((chans, N1, N2), f32)],
        scratch_shapes=[pltpu.VMEM((GROUP, N1, N2), bf16)],
        compiler_params=params(),
        cost_estimate=cost(4.3, 20),
    )(one_home.reshape(N1, chans, N2), kernel, second_block, third_block, swap)
    three_here = transfer(three_back.reshape(sections))

    one_back, grad_kernel = pl.pallas_call(
        home_backward_kernel,
        grid=(chans // GROUP,),
        in_specs=[at_home, filters, filters, block, block, block],
        out_specs=[at_home, filters],
        out_shape=[shape((N1, chans, N2)), shape((chans, N1, N2))],
        scratch_shapes=[pltpu.VMEM((GROUP, N1, N2), bf16)],
        compiler_params=params(),
        cost_estimate=cost(4.3, 24),
    )(
        three_home.reshape(N1, chans, N2),
        kernel,
        spectrum,
        second_block.T,
        third_block.T,
        swap,
    )
    one_here = transfer(one_back.reshape(sections))

    partial, gate_term = pl.pallas_call(
        gate_kernel,
        grid=(rows // per,),
        in_specs=[sent, column, row, row, block, square, line, one],
        out_specs=[row, square],
        out_shape=[shape((local_rows, D)), shape((D, D))],
        scratch_shapes=[pltpu.VMEM((D, D), f32), pltpu.VMEM((per * N2, D), bf16)],
        compiler_params=params(),
        cost_estimate=cost(5.4, 25),
    )(three_here, tokens_t, value, cotangent, fourth_block, w_gate.T, skip, factor)

    skip_lanes = jnp.broadcast_to((skip_term * factor[0, 0]).astype(bf16).T, (D, LANES))
    gate_term = jnp.concatenate([gate_term, skip_lanes], axis=1)
    bits = n.bit_length() - 1
    gate_part = gate_term.reshape((2,) * bits + (D // n, D + LANES))
    for b in range(bits):
        early = gate_part
        kept, sent_half = halves(gate_part, bits - 1 - b, b)
        gate_part = added(kept, from_partner(sent_half, b, n))

    first_t = first_block.T
    in_vmem = pl.BlockSpec(memory_space=pltpu.VMEM)
    value_term = pl.pallas_call(
        functools.partial(value_kernel, per),
        in_specs=[unread, unread, unread, in_vmem, in_vmem, one, unread],
        out_specs=in_vmem,
        out_shape=shape((D, D)),
        scratch_shapes=[
            pltpu.VMEM(sections, bf16),
            pltpu.VMEM((D, local_rows), bf16),
            pltpu.VMEM((local_rows, D), bf16),
            pltpu.VMEM((local_rows, D), bf16),
            pltpu.VMEM((D, D), f32),
            pltpu.SemaphoreType.DMA((rows // per, 3)),
        ],
        compiler_params=params(),
        cost_estimate=cost(3.3, 13),
    )(one_here, tokens_t, d_mix, first_t, skip, factor, early)

    offsets = [0]
    for b in reversed(range(2, bits)):
        gate_part = jnp.concatenate([gate_part, from_partner(gate_part, b, n)])
        offsets += [offset | (1 << b) for offset in offsets]
    gate_parts = doubled(gate_part, n)

    quarters = 4
    pair = rows // quarters // 2 if rows > quarters else 1
    steps = rows // quarters // pair
    w_value_t = w_value.T

    def quarter(i, grad_tokens, after):
        turn = lambda g: g + i * steps
        lines = pl.BlockSpec((pair * N2, D), lambda g: (turn(g), 0))
        held = [] if grad_tokens is None else [grad_tokens]
        return pl.pallas_call(
            tokens_kernel,
            grid=(steps,),
            in_specs=[
                pl.BlockSpec((n, pair, chans, N2), lambda g: (0, turn(g), 0, 0)),
                lines,
                lines,
                block,
                line,
                square,
                unread,
            ]
            + [unread] * len(held),
            out_specs=[lines, whole((1, LANES))],
            out_shape=[shape((local_rows, D)), shape((1, LANES), f32)],
            input_output_aliases={7: 0} if held else {},
            compiler_params=params(),
            cost_estimate=cost(0.8, 4),
        )(one_here, d_mix, partial, first_t, skip, w_value_t, after, *held)

    value_part = value_term.reshape(2, 2, D // 4, D)
    grad_tokens = None
    for i, b in enumerate(range(bits)):
        if b < 2:
            kept, sent_half = halves(value_part, 1 - b, b)
        else:
            kept, sent_half = value_part, value_part
        got = from_partner(sent_half, b, n)
        zero = 0.0
        if i < quarters:
            grad_tokens, zeros = quarter(i, grad_tokens, value_part)
            zero = zeros[0, 0]
        value_part = added(kept, got, zero)
    value_parts = doubled(value_part, n)

    vmem_specs = [in_vmem] * 8
    grad_weights, skip_total = pl.pallas_call(
        functools.partial(place_kernel, 4, offsets),
        in_specs=[one] + vmem_specs,
        out_specs=[in_vmem, in_vmem],
        out_shape=[shape((2, D, D), f32), shape((1, D), f32)],
        scratch_shapes=[pltpu.VMEM((D, LANES), f32)],
        compiler_params=params(),
        cost_estimate=cost(0.001, 3),
    )(lax.axis_index("seq").reshape(1, 1), *value_parts, *gate_parts)
    return grad_tokens, grad_kernel, grad_weights, skip_total.reshape(D)


def solution(mesh):
    in_specs = (
        P(("parts", "seq"), None),
        P(),
        P(),
        P(),
        P(),
        P(),
        P(),
        P("seq", None, None),
        P(),
        P(("parts", "seq"), None),
    )
    out_specs = (
        P(("parts", "seq"), None),
        P(("parts", "seq"), None, None),
        P("parts", None, None),
        P("parts"),
    )
    return jax.shard_map(
        on_device, mesh=mesh, in_specs=in_specs, out_specs=out_specs, check_vma=False
    )
```

```python
import functools

import functools

import jax
import jax.numpy as jnp
from jax import lax
from jax.experimental import pallas as pl
from jax.experimental.pallas import tpu as pltpu
from jax.sharding import PartitionSpec as P

D = 512
N1 = 256
N2 = 256
GROUP = 16
LANES = 128
VMEM_LIMIT = 56 * 1024 * 1024

f32 = jnp.float32
bf16 = jnp.bfloat16


def dot_nn(a, b):
    return jnp.dot(a, b, preferred_element_type=f32)


def dot_nt(a, b):
    return lax.dot_general(a, b, (((1,), (1,)), ((), ())), preferred_element_type=f32)


def params():
    return pltpu.CompilerParams(vmem_limit_bytes=VMEM_LIMIT)


def whole(shape):
    return pl.BlockSpec(shape, lambda i: (0,) * len(shape))


def rows_of(per):
    return pl.BlockSpec((per * N2, D), lambda i: (i, 0))


def by_device(n, per, chans):
    return pl.BlockSpec((n, per, chans, N2), lambda i: (0, i, 0, 0))


def row_slice(r):
    return slice(r * N2, (r + 1) * N2)


def section_one_kernel(
    per, tokens, w_value, first, out, tokens_v, w_v, first_v, out_v, arrive, leave
):
    n, rows, chans, _ = out.shape
    chunks = rows // per
    in_first = pltpu.make_async_copy(first, first_v, arrive.at[chunks])
    in_w = pltpu.make_async_copy(w_value, w_v, arrive.at[chunks + 1])
    in_tokens = [
        pltpu.make_async_copy(
            tokens.at[pl.ds(i * per * N2, per * N2)],
            tokens_v.at[pl.ds(i * per * N2, per * N2)],
            arrive.at[i],
        )
        for i in range(chunks)
    ]
    outs = [
        pltpu.make_async_copy(
            out_v.at[:, pl.ds(i * per, per)], out.at[:, pl.ds(i * per, per)], leave.at[i]
        )
        for i in range(chunks)
    ]
    in_w.start()
    in_tokens[0].start()
    in_first.start()
    for copy in in_tokens[1:]:
        copy.start()
    in_w.wait()
    for i in range(chunks):
        in_tokens[i].wait()
        value = dot_nn(tokens_v[i * per * N2 : (i + 1) * per * N2], w_v[...]).astype(bf16)
        if i == 0:
            in_first.wait()
            first_v[...] = first_v[...].T
        for r in range(per):
            section = dot_nn(value[row_slice(r)].T, first_v[...]).astype(bf16)
            out_v[:, i * per + r] = section.reshape(n, chans, N2)
        outs[i].start()
    for copy in outs:
        copy.wait()


def d_three_kernel(
    tokens,
    cotangent,
    w_value,
    w_gate,
    fourth,
    out,
    value_out,
    d_mix_out,
    tokens_t_out,
    skip_out,
    w_value_t,
    w_gate_t,
):
    n, per, chans, _ = out.shape

    @pl.when(pl.program_id(0) == 0)
    def _():
        skip_out[...] = jnp.zeros_like(skip_out)
        w_value_t[...] = w_value[...].T
        w_gate_t[...] = w_gate[...].T

    for r in range(per):
        here = row_slice(r)
        value = dot_nn(tokens[here], w_value[...]).astype(bf16)
        gate = dot_nn(tokens[here], w_gate[...]).astype(bf16)
        d_mix = (cotangent[here].astype(f32) * gate.astype(f32)).astype(bf16)
        value_out[here] = value
        d_mix_out[here] = d_mix
        tokens_t_out[:, here] = tokens[here].T
        skip_out[...] += jnp.sum(
            d_mix.astype(f32) * value.astype(f32), axis=0, keepdims=True
        )
        section = dot_nn(d_mix.T, fourth[...]).astype(bf16)
        out[:, r] = section.reshape(n, chans, N2)


def turn_in(swap, arrived, by_channel):
    def body(i, _):
        rows = pl.ds(pl.multiple_of(i * GROUP, GROUP), GROUP)
        block = arrived[rows].reshape(GROUP * GROUP, N2)
        turned = dot_nn(swap[...], block).astype(bf16)
        by_channel[:, rows, :] = turned.reshape(GROUP, GROUP, N2)
        return 0

    lax.fori_loop(0, N1 // GROUP, body, 0, unroll=2)


def turn_out(swap, by_channel, out):
    def body(i, _):
        rows = pl.ds(pl.multiple_of(i * GROUP, GROUP), GROUP)
        block = by_channel[:, rows, :].reshape(GROUP * GROUP, N2)
        turned = dot_nn(swap[...], block).astype(bf16)
        out[rows] = turned.reshape(GROUP, GROUP, N2)
        return 0

    lax.fori_loop(0, N1 // GROUP, body, 0, unroll=2)


def home_forward_kernel(arrived, kernel, second, third, swap, out, spectrum_out, by_channel):
    turn_in(swap, arrived, by_channel)

    def body(c, _):
        spectrum = dot_nn(second[...], by_channel[c])
        spectrum_out[c] = spectrum
        filtered = (spectrum * kernel[c].astype(f32)).astype(bf16)
        by_channel[c] = dot_nn(third[...], filtered).astype(bf16)
        return 0

    lax.fori_loop(0, GROUP, body, 0, unroll=2)
    turn_out(swap, by_channel, out)


def home_backward_kernel(
    arrived, kernel, spectrum, second_t, third_t, swap, out, grad_kernel, by_channel
):
    turn_in(swap, arrived, by_channel)

    def body(c, _):
        d_freq = dot_nn(third_t[...], by_channel[c])
        grad_kernel[c] = (d_freq * spectrum[c]).astype(bf16)
        d_spec = (d_freq * kernel[c].astype(f32)).astype(bf16)
        by_channel[c] = dot_nn(second_t[...], d_spec).astype(bf16)
        return 0

    lax.fori_loop(0, GROUP, body, 0, unroll=2)
    turn_out(swap, by_channel, out)


def accumulate(total, term):
    @pl.when(pl.program_id(0) == 0)
    def _():
        total[...] = term

    @pl.when(pl.program_id(0) > 0)
    def _():
        total[...] += term


def finish(total, factor, grad_w):
    @pl.when(pl.program_id(0) == pl.num_programs(0) - 1)
    def _():
        grad_w[...] = (total[...] * factor[0, 0]).astype(bf16)


def gate_kernel(
    arrived,
    tokens_t,
    value,
    cotangent,
    fourth,
    w_gate_t,
    skip,
    factor,
    partial,
    grad_w,
    total,
    d_gate,
):
    for r in range(arrived.shape[1]):
        here = row_slice(r)
        conv = dot_nt(fourth[...], arrived[:, r].reshape(D, N2))
        mixed = conv + skip[...] * value[here].astype(f32)
        d_gate[here] = (cotangent[here].astype(f32) * mixed).astype(bf16)
        partial[here] = dot_nn(d_gate[here], w_gate_t[...]).astype(bf16)
    accumulate(total, dot_nn(tokens_t[...], d_gate[...]))
    finish(total, factor, grad_w)


def value_kernel(
    per,
    arrived,
    tokens_t,
    d_mix,
    first_t,
    skip,
    factor,
    bit,
    _,
    kept,
    given,
    d_value_out,
    arrived_v,
    tokens_v,
    d_mix_v,
    d_value,
    total,
    arrive,
    leave,
):
    rows = arrived.shape[1]
    chunks = rows // per

    def copies(i):
        lines = pl.ds(i * per, per)
        here = pl.ds(i * per * N2, per * N2)
        return [
            pltpu.make_async_copy(
                arrived.at[:, lines], arrived_v.at[:, lines], arrive.at[i, 0]
            ),
            pltpu.make_async_copy(d_mix.at[here], d_mix_v.at[here], arrive.at[i, 1]),
            pltpu.make_async_copy(
                tokens_t.at[:, here], tokens_v.at[:, here], arrive.at[i, 2]
            ),
        ]

    started = [copies(i) for i in range(chunks)]
    for group in started:
        for copy in group:
            copy.start()
    outs = []
    for i in range(chunks):
        started[i][0].wait()
        started[i][1].wait()
        for r in range(i * per, (i + 1) * per):
            here = row_slice(r)
            d_cube = dot_nt(first_t[...], arrived_v[:, r].reshape(D, N2))
            d_value[here] = (d_cube + skip[...] * d_mix_v[here].astype(f32)).astype(bf16)
        here = pl.ds(i * per * N2, per * N2)
        outs.append(pltpu.make_async_copy(d_value.at[here], d_value_out.at[here], leave.at[i]))
        outs[i].start()
        started[i][2].wait()
        here = slice(i * per * N2, (i + 1) * per * N2)
        term = dot_nn(tokens_v[:, here], d_value[here])
        if i == 0:
            total[...] = term
        else:
            total[...] += term
    size = kept.shape[1]
    for high in range(2):
        for part, low in ((kept, bit[0, 0]), (given, 1 - bit[0, 0])):
            start = pl.multiple_of((2 * high + low) * size, size)
            part[high] = (total[pl.ds(start, size)] * factor[0, 0]).astype(bf16)
    for copy in outs:
        copy.wait()


def tokens_kernel(d_value, partial, w_value_t, *rest):
    grad_tokens, zero = rest[-2:]
    for r in range(d_value.shape[0] // N2):
        here = row_slice(r)
        grad_tokens[here] = (
            partial[here].astype(f32) + dot_nn(d_value[here], w_value_t[...])
        ).astype(bf16)
    zero[...] = jnp.zeros_like(zero)


def place_gate_kernel(offsets, me, *refs):
    parts, (out, skip_out), held = refs[:4], refs[4:6], refs[6:10]
    wide, column, arrive, leave = refs[10:]
    copies = [
        pltpu.make_async_copy(parts[i], held[i], arrive.at[i]) for i in range(4)
    ]
    for copy in copies:
        copy.start()
    for distance in range(4):
        copies[distance].wait()
        size = held[distance].shape[0] // len(offsets)
        for i, offset in enumerate(offsets):
            start = pl.multiple_of((me[0, 0] ^ (distance | offset)) * size, size)
            block = held[distance][i * size : (i + 1) * size].astype(f32)
            wide[pl.ds(start, size)] = block[:, :D]
            column[pl.ds(start, size)] = block[:, D:]
    copy = pltpu.make_async_copy(wide, out.at[1], leave)
    copy.start()
    skip_out[...] = column[...].T[:1]
    copy.wait()


def place_value_kernel(me, *refs):
    parts, out, held, wide = refs[:4], refs[5], refs[6:10], refs[10:14]
    arrive, leave = refs[14:]
    ins = [pltpu.make_async_copy(parts[i], held[i], arrive.at[i]) for i in range(4)]
    for copy in ins:
        copy.start()
    outs = []
    for i in range(4):
        ins[i].wait()
        wide[i][...] = held[i][...].astype(f32)
        size = D // 4
        start = pl.multiple_of(((me[0, 0] % 4) ^ i) * size, size)
        outs.append(
            pltpu.make_async_copy(wide[i], out.at[0, pl.ds(start, size)], leave.at[i])
        )
        outs[i].start()
    for copy in outs:
        copy.wait()


def from_partner(array, b, n):
    return lax.ppermute(array, "seq", [(i, i ^ (1 << b)) for i in range(n)])


def halves(part, axis, b):
    bit = (lax.axis_index("seq") >> b) & 1
    kept = lax.dynamic_index_in_dim(part, bit, axis, keepdims=False)
    sent = lax.dynamic_index_in_dim(part, 1 - bit, axis, keepdims=False)
    return kept, sent


def added(kept, got, zero=0.0):
    return (kept.astype(f32) + got.astype(f32) + zero).astype(bf16)


def doubled(part, n):
    other = from_partner(part, 1, n)
    return [part, from_partner(part, 0, n), other, from_partner(other, 0, n)]


def on_device(
    tokens,
    w_value,
    w_gate,
    first_block,
    second_block,
    third_block,
    fourth_block,
    kernel,
    skip_gain,
    cotangent,
):
    n = lax.axis_size("seq")
    rows = N1 // n
    chans = D // n
    local_rows = tokens.shape[0]
    sections = (n, rows, chans, N2)
    factor = (1.0 / jnp.sqrt(jnp.asarray(N1 * N2, f32))).reshape(1, 1)
    skip = skip_gain.reshape(1, D)
    square = whole((D, D))
    block = whole((N1, N2))
    line = whole((1, D))
    per = min(4, rows)
    row = rows_of(per)
    column = pl.BlockSpec((D, per * N2), lambda i: (0, i))
    sent = by_device(n, per, chans)
    one = pl.BlockSpec(memory_space=pltpu.SMEM)
    place = jnp.arange(GROUP * GROUP)
    swap = (
        place[None, :] == ((place % GROUP) * GROUP + place // GROUP)[:, None]
    ).astype(bf16)

    def cost(gflop, mib):
        scale = rows / 16
        return pl.CostEstimate(
            flops=int(gflop * 1e9 * scale), bytes_accessed=int(mib * 2**20 * scale), transcendentals=0
        )

    def shape(dims, dtype=bf16):
        return jax.ShapeDtypeStruct(dims, dtype)

    def transfer(array):
        return lax.all_to_all(array, "seq", split_axis=0, concat_axis=0, tiled=True)

    unread = pl.BlockSpec(memory_space=pl.ANY)
    one_sent = pl.pallas_call(
        functools.partial(section_one_kernel, per),
        in_specs=[unread] * 3,
        out_specs=unread,
        out_shape=shape(sections),
        scratch_shapes=[
            pltpu.VMEM((local_rows, D), bf16),
            pltpu.VMEM((D, D), bf16),
            pltpu.VMEM((N2, N2), bf16),
            pltpu.VMEM(sections, bf16),
            pltpu.SemaphoreType.DMA((rows // per + 2,)),
            pltpu.SemaphoreType.DMA((rows // per,)),
        ],
        compiler_params=params(),
        cost_estimate=cost(3.2, 9),
    )(tokens, w_value, first_block)
    one_home = transfer(one_sent)

    three_sent, value, d_mix, tokens_t, skip_term, w_value_t, w_gate_t = pl.pallas_call(
        d_three_kernel,
        grid=(rows // per,),
        in_specs=[row, row, square, square, block],
        out_specs=[sent, row, row, column, line, square, square],
        out_shape=[
            shape(sections),
            shape((local_rows, D)),
            shape((local_rows, D)),
            shape((D, local_rows)),
            shape((1, D), f32),
            shape((D, D)),
            shape((D, D)),
        ],
        compiler_params=params(),
        cost_estimate=cost(5.4, 25),
    )(tokens, cotangent, w_value, w_gate, fourth_block)
    three_home = transfer(three_sent)

    at_home = pl.BlockSpec((N1, GROUP, N2), lambda i: (0, i, 0))
    filters = pl.BlockSpec((GROUP, N1, N2), lambda i: (i, 0, 0))
    three_back, spectrum = pl.pallas_call(
        home_forward_kernel,
        grid=(chans // GROUP,),
        in_specs=[at_home, filters, block, block, block],
        out_specs=[at_home, filters],
        out_shape=[shape((N1, chans, N2)), shape((chans, N1, N2), f32)],
        scratch_shapes=[pltpu.VMEM((GROUP, N1, N2), bf16)],
        compiler_params=params(),
        cost_estimate=cost(4.3, 20),
    )(one_home.reshape(N1, chans, N2), kernel, second_block, third_block, swap)
    three_here = transfer(three_back.reshape(sections))

    one_back, grad_kernel = pl.pallas_call(
        home_backward_kernel,
        grid=(chans // GROUP,),
        in_specs=[at_home, filters, filters, block, block, block],
        out_specs=[at_home, filters],
        out_shape=[shape((N1, chans, N2)), shape((chans, N1, N2))],
        scratch_shapes=[pltpu.VMEM((GROUP, N1, N2), bf16)],
        compiler_params=params(),
        cost_estimate=cost(4.3, 24),
    )(
        three_home.reshape(N1, chans, N2),
        kernel,
        spectrum,
        second_block.T,
        third_block.T,
        swap,
    )
    one_here = transfer(one_back.reshape(sections))

    partial, gate_term = pl.pallas_call(
        gate_kernel,
        grid=(rows // per,),
        in_specs=[sent, column, row, row, block, square, line, one],
        out_specs=[row, square],
        out_shape=[shape((local_rows, D)), shape((D, D))],
        scratch_shapes=[pltpu.VMEM((D, D), f32), pltpu.VMEM((per * N2, D), bf16)],
        compiler_params=params(),
        cost_estimate=cost(5.4, 25),
    )(three_here, tokens_t, value, cotangent, fourth_block, w_gate_t, skip, factor)

    skip_lanes = jnp.broadcast_to((skip_term * factor[0, 0]).astype(bf16).T, (D, LANES))
    gate_term = jnp.concatenate([gate_term, skip_lanes], axis=1)
    bits = n.bit_length() - 1
    gate_part = gate_term.reshape((2,) * bits + (D // n, D + LANES))
    for b in range(bits):
        kept, given = halves(gate_part, bits - 1 - b, b)
        gate_part = added(kept, from_partner(given, b, n))

    first_t = first_block.T
    in_vmem = pl.BlockSpec(memory_space=pltpu.VMEM)
    me = lax.axis_index("seq").reshape(1, 1)
    half = (2, D // 4, D)
    kept, given, d_value = pl.pallas_call(
        functools.partial(value_kernel, per),
        in_specs=[unread, unread, unread, in_vmem, in_vmem, one, one, unread],
        out_specs=[in_vmem, in_vmem, unread],
        out_shape=[shape(half), shape(half), shape((local_rows, D))],
        scratch_shapes=[
            pltpu.VMEM(sections, bf16),
            pltpu.VMEM((D, local_rows), bf16),
            pltpu.VMEM((local_rows, D), bf16),
            pltpu.VMEM((local_rows, D), bf16),
            pltpu.VMEM((D, D), f32),
            pltpu.SemaphoreType.DMA((rows // per, 3)),
            pltpu.SemaphoreType.DMA((rows // per,)),
        ],
        compiler_params=params(),
        cost_estimate=cost(3.3, 17),
    )(one_here, tokens_t, d_mix, first_t, skip, factor, me & 1, gate_part)

    offsets = [0]
    gate_after = []
    for b in reversed(range(2, bits)):
        gate_part = jnp.concatenate([gate_part, from_partner(gate_part, b, n)])
        gate_after.append(gate_part)
        offsets += [offset | (1 << b) for offset in offsets]
    gate_parts = doubled(gate_part, n)
    gate_after = gate_after[-2:] + gate_parts[2:]

    quarters = 4
    pair = max(rows // quarters // 2, 1)
    steps = rows // quarters // pair

    def quarter(i, grad_tokens, after):
        lines = pl.BlockSpec((pair * N2, D), lambda g: (g + i * steps, 0))
        held = [] if grad_tokens is None else [grad_tokens]
        return pl.pallas_call(
            tokens_kernel,
            grid=(steps,),
            in_specs=[lines, lines, square, unread, unread] + [unread] * len(held),
            out_specs=[lines, line],
            out_shape=[shape((local_rows, D)), shape((1, D), f32)],
            input_output_aliases={5: 0} if held else {},
            compiler_params=params(),
            cost_estimate=cost(0.53, 3.5),
        )(d_value, partial, w_value_t, after, gate_after[i], *held)

    grad_tokens = None
    for b in range(bits):
        if b == 1:
            kept, given = halves(value_part, 0, b)
        elif b > 1:
            kept, given = value_part, value_part
        got = from_partner(given, b, n)
        zeros = 0.0
        if b < quarters:
            grad_tokens, zeros = quarter(b, grad_tokens, given)
        value_part = added(kept, got, zeros)
    value_parts = doubled(value_part, n)

    placed = shape((2, D, D), f32)
    gate_block = (D // 4, D + LANES)
    grad_weights, skip_total = pl.pallas_call(
        functools.partial(place_gate_kernel, offsets),
        in_specs=[one] + [unread] * 4,
        out_specs=[unread, in_vmem],
        out_shape=[placed, shape((1, D), f32)],
        scratch_shapes=[pltpu.VMEM(gate_block, bf16)] * 4
        + [
            pltpu.VMEM((D, D), f32),
            pltpu.VMEM((D, LANES), f32),
            pltpu.SemaphoreType.DMA((4,)),
            pltpu.SemaphoreType.DMA,
        ],
        compiler_params=params(),
        cost_estimate=cost(0.001, 2),
    )(me, *gate_parts)
    grad_weights = pl.pallas_call(
        place_value_kernel,
        in_specs=[one] + [unread] * 5,
        out_specs=unread,
        out_shape=placed,
        input_output_aliases={5: 0},
        scratch_shapes=[pltpu.VMEM((D // 4, D), bf16)] * 4
        + [pltpu.VMEM((D // 4, D), f32)] * 4
        + [pltpu.SemaphoreType.DMA((4,)), pltpu.SemaphoreType.DMA((4,))],
        compiler_params=params(),
        cost_estimate=cost(0.001, 2),
    )(me, *value_parts, grad_weights)
    return grad_tokens, grad_kernel, grad_weights, skip_total.reshape(D)


def solution(mesh):
    in_specs = (
        P(("parts", "seq"), None),
        P(),
        P(),
        P(),
        P(),
        P(),
        P(),
        P("seq", None, None),
        P(),
        P(("parts", "seq"), None),
    )
    out_specs = (
        P(("parts", "seq"), None),
        P(("parts", "seq"), None, None),
        P("parts", None, None),
        P("parts"),
    )
    return jax.shard_map(
        on_device, mesh=mesh, in_specs=in_specs, out_specs=out_specs, check_vma=False
    )
```

```python
import functools

import functools

import jax
import jax.numpy as jnp
from jax import lax
from jax.experimental import pallas as pl
from jax.experimental.pallas import tpu as pltpu
from jax.sharding import PartitionSpec as P

D = 512
N1 = 256
N2 = 256
GROUP = 16
LANES = 128
VMEM_LIMIT = 56 * 1024 * 1024

f32 = jnp.float32
bf16 = jnp.bfloat16


def dot_nn(a, b):
    return jnp.dot(a, b, preferred_element_type=f32)


def dot_nt(a, b):
    return lax.dot_general(a, b, (((1,), (1,)), ((), ())), preferred_element_type=f32)


def params():
    return pltpu.CompilerParams(vmem_limit_bytes=VMEM_LIMIT)


def whole(shape):
    return pl.BlockSpec(shape, lambda i: (0,) * len(shape))


def rows_of(per):
    return pl.BlockSpec((per * N2, D), lambda i: (i, 0))


def by_device(n, per, chans):
    return pl.BlockSpec((n, per, chans, N2), lambda i: (0, i, 0, 0))


def row_slice(r):
    return slice(r * N2, (r + 1) * N2)


def section_one_kernel(
    per, tokens, w_value, first, out, tokens_v, w_v, first_v, out_v, arrive, leave
):
    n, rows, chans, _ = out.shape
    chunks = rows // per
    in_first = pltpu.make_async_copy(first, first_v, arrive.at[chunks])
    in_w = pltpu.make_async_copy(w_value, w_v, arrive.at[chunks + 1])
    in_tokens = [
        pltpu.make_async_copy(
            tokens.at[pl.ds(i * per * N2, per * N2)],
            tokens_v.at[pl.ds(i * per * N2, per * N2)],
            arrive.at[i],
        )
        for i in range(chunks)
    ]
    outs = [
        pltpu.make_async_copy(
            out_v.at[:, pl.ds(i * per, per)], out.at[:, pl.ds(i * per, per)], leave.at[i]
        )
        for i in range(chunks)
    ]
    in_w.start()
    in_tokens[0].start()
    in_first.start()
    for copy in in_tokens[1:]:
        copy.start()
    in_w.wait()
    for i in range(chunks):
        in_tokens[i].wait()
        value = dot_nn(tokens_v[i * per * N2 : (i + 1) * per * N2], w_v[...]).astype(bf16)
        if i == 0:
            in_first.wait()
            first_v[...] = first_v[...].T
        for r in range(per):
            section = dot_nn(value[row_slice(r)].T, first_v[...]).astype(bf16)
            out_v[:, i * per + r] = section.reshape(n, chans, N2)
        outs[i].start()
    for copy in outs:
        copy.wait()


def d_three_kernel(
    tokens,
    cotangent,
    w_value,
    w_gate,
    fourth,
    out,
    value_out,
    d_mix_out,
    tokens_t_out,
    skip_out,
    w_value_t,
    w_gate_t,
):
    n, per, chans, _ = out.shape

    @pl.when(pl.program_id(0) == 0)
    def _():
        skip_out[...] = jnp.zeros_like(skip_out)
        w_value_t[...] = w_value[...].T
        w_gate_t[...] = w_gate[...].T

    for r in range(per):
        here = row_slice(r)
        value = dot_nn(tokens[here], w_value[...]).astype(bf16)
        gate = dot_nn(tokens[here], w_gate[...]).astype(bf16)
        d_mix = (cotangent[here].astype(f32) * gate.astype(f32)).astype(bf16)
        value_out[here] = value
        d_mix_out[here] = d_mix
        tokens_t_out[:, here] = tokens[here].T
        skip_out[...] += jnp.sum(
            d_mix.astype(f32) * value.astype(f32), axis=0, keepdims=True
        )
        section = dot_nn(d_mix.T, fourth[...]).astype(bf16)
        out[:, r] = section.reshape(n, chans, N2)


def turn_in(swap, arrived, by_channel):
    def body(i, _):
        rows = pl.ds(pl.multiple_of(i * GROUP, GROUP), GROUP)
        block = arrived[rows].reshape(GROUP * GROUP, N2)
        turned = dot_nn(swap[...], block).astype(bf16)
        by_channel[:, rows, :] = turned.reshape(GROUP, GROUP, N2)
        return 0

    lax.fori_loop(0, N1 // GROUP, body, 0, unroll=2)


def turn_out(swap, by_channel, out):
    def body(i, _):
        rows = pl.ds(pl.multiple_of(i * GROUP, GROUP), GROUP)
        block = by_channel[:, rows, :].reshape(GROUP * GROUP, N2)
        turned = dot_nn(swap[...], block).astype(bf16)
        out[rows] = turned.reshape(GROUP, GROUP, N2)
        return 0

    lax.fori_loop(0, N1 // GROUP, body, 0, unroll=2)


def home_forward_kernel(arrived, kernel, second, third, swap, out, spectrum_out, by_channel):
    turn_in(swap, arrived, by_channel)

    def body(c, _):
        spectrum = dot_nn(second[...], by_channel[c])
        spectrum_out[c] = spectrum
        filtered = (spectrum * kernel[c].astype(f32)).astype(bf16)
        by_channel[c] = dot_nn(third[...], filtered).astype(bf16)
        return 0

    lax.fori_loop(0, GROUP, body, 0, unroll=2)
    turn_out(swap, by_channel, out)


def home_backward_kernel(
    arrived, kernel, spectrum, second_t, third_t, swap, out, grad_kernel, by_channel
):
    turn_in(swap, arrived, by_channel)

    def body(c, _):
        d_freq = dot_nn(third_t[...], by_channel[c])
        grad_kernel[c] = (d_freq * spectrum[c]).astype(bf16)
        d_spec = (d_freq * kernel[c].astype(f32)).astype(bf16)
        by_channel[c] = dot_nn(second_t[...], d_spec).astype(bf16)
        return 0

    lax.fori_loop(0, GROUP, body, 0, unroll=2)
    turn_out(swap, by_channel, out)


def accumulate(total, term):
    @pl.when(pl.program_id(0) == 0)
    def _():
        total[...] = term

    @pl.when(pl.program_id(0) > 0)
    def _():
        total[...] += term


def finish(total, factor, grad_w):
    @pl.when(pl.program_id(0) == pl.num_programs(0) - 1)
    def _():
        grad_w[...] = (total[...] * factor[0, 0]).astype(bf16)


def gate_kernel(
    arrived,
    tokens_t,
    value,
    cotangent,
    fourth,
    w_gate_t,
    skip,
    factor,
    partial,
    grad_w,
    total,
    d_gate,
):
    for r in range(arrived.shape[1]):
        here = row_slice(r)
        conv = dot_nt(fourth[...], arrived[:, r].reshape(D, N2))
        mixed = conv + skip[...] * value[here].astype(f32)
        d_gate[here] = (cotangent[here].astype(f32) * mixed).astype(bf16)
        partial[here] = dot_nn(d_gate[here], w_gate_t[...]).astype(bf16)
    accumulate(total, dot_nn(tokens_t[...], d_gate[...]))
    finish(total, factor, grad_w)


def value_kernel(
    per,
    arrived,
    tokens_t,
    d_mix,
    first_t,
    skip,
    factor,
    bit,
    _,
    kept,
    given,
    d_value_out,
    arrived_v,
    tokens_v,
    d_mix_v,
    d_value,
    total,
    arrive,
    leave,
):
    rows = arrived.shape[1]
    chunks = rows // per

    def copies(i):
        lines = pl.ds(i * per, per)
        here = pl.ds(i * per * N2, per * N2)
        return [
            pltpu.make_async_copy(
                arrived.at[:, lines], arrived_v.at[:, lines], arrive.at[i, 0]
            ),
            pltpu.make_async_copy(d_mix.at[here], d_mix_v.at[here], arrive.at[i, 1]),
            pltpu.make_async_copy(
                tokens_t.at[:, here], tokens_v.at[:, here], arrive.at[i, 2]
            ),
        ]

    started = [copies(i) for i in range(chunks)]
    for group in started:
        for copy in group:
            copy.start()
    outs = []
    for i in range(chunks):
        started[i][0].wait()
        started[i][1].wait()
        for r in range(i * per, (i + 1) * per):
            here = row_slice(r)
            d_cube = dot_nt(first_t[...], arrived_v[:, r].reshape(D, N2))
            d_value[here] = (d_cube + skip[...] * d_mix_v[here].astype(f32)).astype(bf16)
        here = pl.ds(i * per * N2, per * N2)
        outs.append(pltpu.make_async_copy(d_value.at[here], d_value_out.at[here], leave.at[i]))
        outs[i].start()
        started[i][2].wait()
        here = slice(i * per * N2, (i + 1) * per * N2)
        term = dot_nn(tokens_v[:, here], d_value[here])
        if i == 0:
            total[...] = term
        else:
            total[...] += term
    size = kept.shape[1]
    for high in range(2):
        for part, low in ((kept, bit[0, 0]), (given, 1 - bit[0, 0])):
            start = pl.multiple_of((2 * high + low) * size, size)
            part[high] = (total[pl.ds(start, size)] * factor[0, 0]).astype(bf16)
    for copy in outs:
        copy.wait()


def tokens_kernel(d_value, partial, w_value_t, *rest):
    grad_tokens, zero = rest[-2:]
    for r in range(d_value.shape[0] // N2):
        here = row_slice(r)
        grad_tokens[here] = (
            partial[here].astype(f32) + dot_nn(d_value[here], w_value_t[...])
        ).astype(bf16)
    zero[...] = jnp.zeros_like(zero)


def place_kernel(distances, me, *refs):
    count = len(distances)
    parts, refs = refs[:count], refs[count:]
    out, skip_out, *refs = refs[-(2 + 3 * count + 2) :]
    held, wides, columns = refs[:count], refs[count : 2 * count], refs[2 * count : 3 * count]
    arrive, leave = refs[-2:]
    size = D // 4
    ins = [pltpu.make_async_copy(parts[i], held[i], arrive.at[i]) for i in range(count)]
    for copy in ins:
        copy.start()
    outs = []
    for i, distance in enumerate(distances):
        ins[i].wait()
        start = pl.multiple_of(((me[0, 0] % 4) ^ distance) * size, size)
        wides[i][0] = held[i][:, :D].astype(f32)
        wides[i][1] = held[i][:, D : 2 * D].astype(f32)
        columns[i][...] = held[i][:, 2 * D :].astype(f32)
        columns[i][...] = columns[i][...].T
        outs += [
            pltpu.make_async_copy(wides[i], out.at[:, pl.ds(start, size)], leave.at[i, 0]),
            pltpu.make_async_copy(
                columns[i].at[pl.ds(0, 8)],
                skip_out.at[:, pl.ds(start, size)],
                leave.at[i, 1],
            ),
        ]
        outs[-2].start()
        outs[-1].start()
    for copy in outs:
        copy.wait()


def from_partner(array, b, n):
    return lax.ppermute(array, "seq", [(i, i ^ (1 << b)) for i in range(n)])


def halves(part, axis, b):
    bit = (lax.axis_index("seq") >> b) & 1
    kept = lax.dynamic_index_in_dim(part, bit, axis, keepdims=False)
    sent = lax.dynamic_index_in_dim(part, 1 - bit, axis, keepdims=False)
    return kept, sent


def added(kept, got, zero=0.0):
    return (kept.astype(f32) + got.astype(f32) + zero).astype(bf16)


def on_device(
    tokens,
    w_value,
    w_gate,
    first_block,
    second_block,
    third_block,
    fourth_block,
    kernel,
    skip_gain,
    cotangent,
):
    n = lax.axis_size("seq")
    rows = N1 // n
    chans = D // n
    local_rows = tokens.shape[0]
    sections = (n, rows, chans, N2)
    factor = (1.0 / jnp.sqrt(jnp.asarray(N1 * N2, f32))).reshape(1, 1)
    skip = skip_gain.reshape(1, D)
    square = whole((D, D))
    block = whole((N1, N2))
    line = whole((1, D))
    per = min(4, rows)
    row = rows_of(per)
    column = pl.BlockSpec((D, per * N2), lambda i: (0, i))
    sent = by_device(n, per, chans)
    one = pl.BlockSpec(memory_space=pltpu.SMEM)
    place = jnp.arange(GROUP * GROUP)
    swap = (
        place[None, :] == ((place % GROUP) * GROUP + place // GROUP)[:, None]
    ).astype(bf16)

    def cost(gflop, mib):
        scale = rows / 16
        return pl.CostEstimate(
            flops=int(gflop * 1e9 * scale), bytes_accessed=int(mib * 2**20 * scale), transcendentals=0
        )

    def shape(dims, dtype=bf16):
        return jax.ShapeDtypeStruct(dims, dtype)

    def transfer(array):
        return lax.all_to_all(array, "seq", split_axis=0, concat_axis=0, tiled=True)

    unread = pl.BlockSpec(memory_space=pl.ANY)
    one_sent = pl.pallas_call(
        functools.partial(section_one_kernel, per),
        in_specs=[unread] * 3,
        out_specs=unread,
        out_shape=shape(sections),
        scratch_shapes=[
            pltpu.VMEM((local_rows, D), bf16),
            pltpu.VMEM((D, D), bf16),
            pltpu.VMEM((N2, N2), bf16),
            pltpu.VMEM(sections, bf16),
            pltpu.SemaphoreType.DMA((rows // per + 2,)),
            pltpu.SemaphoreType.DMA((rows // per,)),
        ],
        compiler_params=params(),
        cost_estimate=cost(3.2, 9),
    )(tokens, w_value, first_block)
    one_home = transfer(one_sent)

    three_sent, value, d_mix, tokens_t, skip_term, w_value_t, w_gate_t = pl.pallas_call(
        d_three_kernel,
        grid=(rows // per,),
        in_specs=[row, row, square, square, block],
        out_specs=[sent, row, row, column, line, square, square],
        out_shape=[
            shape(sections),
            shape((local_rows, D)),
            shape((local_rows, D)),
            shape((D, local_rows)),
            shape((1, D), f32),
            shape((D, D)),
            shape((D, D)),
        ],
        compiler_params=params(),
        cost_estimate=cost(5.4, 25),
    )(tokens, cotangent, w_value, w_gate, fourth_block)
    three_home = transfer(three_sent)

    at_home = pl.BlockSpec((N1, GROUP, N2), lambda i: (0, i, 0))
    filters = pl.BlockSpec((GROUP, N1, N2), lambda i: (i, 0, 0))
    three_back, spectrum = pl.pallas_call(
        home_forward_kernel,
        grid=(chans // GROUP,),
        in_specs=[at_home, filters, block, block, block],
        out_specs=[at_home, filters],
        out_shape=[shape((N1, chans, N2)), shape((chans, N1, N2), f32)],
        scratch_shapes=[pltpu.VMEM((GROUP, N1, N2), bf16)],
        compiler_params=params(),
        cost_estimate=cost(4.3, 20),
    )(one_home.reshape(N1, chans, N2), kernel, second_block, third_block, swap)
    three_here = transfer(three_back.reshape(sections))

    one_back, grad_kernel = pl.pallas_call(
        home_backward_kernel,
        grid=(chans // GROUP,),
        in_specs=[at_home, filters, filters, block, block, block],
        out_specs=[at_home, filters],
        out_shape=[shape((N1, chans, N2)), shape((chans, N1, N2))],
        scratch_shapes=[pltpu.VMEM((GROUP, N1, N2), bf16)],
        compiler_params=params(),
        cost_estimate=cost(4.3, 24),
    )(
        three_home.reshape(N1, chans, N2),
        kernel,
        spectrum,
        second_block.T,
        third_block.T,
        swap,
    )
    one_here = transfer(one_back.reshape(sections))

    partial, gate_term = pl.pallas_call(
        gate_kernel,
        grid=(rows // per,),
        in_specs=[sent, column, row, row, block, square, line, one],
        out_specs=[row, square],
        out_shape=[shape((local_rows, D)), shape((D, D))],
        scratch_shapes=[pltpu.VMEM((D, D), f32), pltpu.VMEM((per * N2, D), bf16)],
        compiler_params=params(),
        cost_estimate=cost(5.4, 25),
    )(three_here, tokens_t, value, cotangent, fourth_block, w_gate_t, skip, factor)

    skip_lanes = jnp.broadcast_to((skip_term * factor[0, 0]).astype(bf16).T, (D, LANES))
    gate_term = jnp.concatenate([gate_term, skip_lanes], axis=1)
    bits = n.bit_length() - 1
    gate_part = gate_term.reshape(2, 2, D // 4, D + LANES)
    for b in range(bits):
        kept, given = halves(gate_part, 1 - b, b) if b < 2 else (gate_part, gate_part)
        gate_part = added(kept, from_partner(given, b, n))

    first_t = first_block.T
    in_vmem = pl.BlockSpec(memory_space=pltpu.VMEM)
    me = lax.axis_index("seq").reshape(1, 1)
    half = (2, D // 4, D)
    kept, given, d_value = pl.pallas_call(
        functools.partial(value_kernel, per),
        in_specs=[unread, unread, unread, in_vmem, in_vmem, one, one, unread],
        out_specs=[in_vmem, in_vmem, unread],
        out_shape=[shape(half), shape(half), shape((local_rows, D))],
        scratch_shapes=[
            pltpu.VMEM(sections, bf16),
            pltpu.VMEM((D, local_rows), bf16),
            pltpu.VMEM((local_rows, D), bf16),
            pltpu.VMEM((local_rows, D), bf16),
            pltpu.VMEM((D, D), f32),
            pltpu.SemaphoreType.DMA((rows // per, 3)),
            pltpu.SemaphoreType.DMA((rows // per,)),
        ],
        compiler_params=params(),
        cost_estimate=cost(3.3, 17),
    )(one_here, tokens_t, d_mix, first_t, skip, factor, me & 1, gate_part)

    quarters = 4
    pair = max(rows // quarters // 2, 1)
    steps = rows // quarters // pair

    def quarter(i, grad_tokens, after):
        lines = pl.BlockSpec((pair * N2, D), lambda g: (g + i * steps, 0))
        held = [] if grad_tokens is None else [grad_tokens]
        return pl.pallas_call(
            tokens_kernel,
            grid=(steps,),
            in_specs=[lines, lines, square, unread] + [unread] * len(held),
            out_specs=[lines, line],
            out_shape=[shape((local_rows, D)), shape((1, D), f32)],
            input_output_aliases={4: 0} if held else {},
            compiler_params=params(),
            cost_estimate=cost(0.53, 3.5),
        )(d_value, partial, w_value_t, after, *held)

    grad_tokens = None
    for b in range(bits):
        if b == 1:
            kept, given = halves(value_part, 0, b)
        elif b > 1:
            kept, given = value_part, value_part
        got = from_partner(given, b, n)
        zeros = 0.0
        if b < quarters:
            grad_tokens, zeros = quarter(b, grad_tokens, given)
        value_part = added(kept, got, zeros)
    both = jnp.concatenate([value_part, gate_part], axis=1)
    other = from_partner(both, 1, n)
    near = from_partner(both, 0, n)
    far = from_partner(other, 0, n)

    def place(parts, distances, held):
        count = len(parts)
        block = (D // 4, 2 * D + LANES)
        return pl.pallas_call(
            functools.partial(place_kernel, distances),
            in_specs=[one] + [unread] * (count + len(held)),
            out_specs=[unread, unread],
            out_shape=[shape((2, D, D), f32), shape((8, D), f32)],
            input_output_aliases={1 + count: 0, 2 + count: 1} if held else {},
            scratch_shapes=[pltpu.VMEM(block, bf16)] * count
            + [pltpu.VMEM((2, D // 4, D), f32)] * count
            + [pltpu.VMEM((LANES, D // 4), f32)] * count
            + [pltpu.SemaphoreType.DMA((count,)), pltpu.SemaphoreType.DMA((count, 2))],
            compiler_params=params(),
            cost_estimate=cost(0.001, count),
        )(me, *parts, *held)

    placed = place([both, near, other], [0, 1, 2], [])
    grad_weights, skip_total = place([far], [3], placed)
    return grad_tokens, grad_kernel, grad_weights, skip_total[0]


def solution(mesh):
    in_specs = (
        P(("parts", "seq"), None),
        P(),
        P(),
        P(),
        P(),
        P(),
        P(),
        P("seq", None, None),
        P(),
        P(("parts", "seq"), None),
    )
    out_specs = (
        P(("parts", "seq"), None),
        P(("parts", "seq"), None, None),
        P("parts", None, None),
        P("parts"),
    )
    return jax.shard_map(
        on_device, mesh=mesh, in_specs=in_specs, out_specs=out_specs, check_vma=False
    )
```

```python
import functools

import functools

import jax
import jax.numpy as jnp
from jax import lax
from jax.experimental import pallas as pl
from jax.experimental.pallas import tpu as pltpu
from jax.sharding import PartitionSpec as P

D = 512
N1 = 256
N2 = 256
GROUP = 16
LANES = 128
VMEM_LIMIT = 56 * 1024 * 1024

f32 = jnp.float32
bf16 = jnp.bfloat16


def dot_nn(a, b):
    return jnp.dot(a, b, preferred_element_type=f32)


def dot_nt(a, b):
    return lax.dot_general(a, b, (((1,), (1,)), ((), ())), preferred_element_type=f32)


def params():
    return pltpu.CompilerParams(vmem_limit_bytes=VMEM_LIMIT)


def whole(shape):
    return pl.BlockSpec(shape, lambda i: (0,) * len(shape))


def rows_of(per):
    return pl.BlockSpec((per * N2, D), lambda i: (i, 0))


def by_device(n, per, chans):
    return pl.BlockSpec((n, per, chans, N2), lambda i: (0, i, 0, 0))


def row_slice(r):
    return slice(r * N2, (r + 1) * N2)


def section_one_kernel(
    per, tokens, w_value, first, out, tokens_v, w_v, first_v, out_v, arrive, leave
):
    n, rows, chans, _ = out.shape
    chunks = rows // per
    in_first = pltpu.make_async_copy(first, first_v, arrive.at[chunks])
    in_w = pltpu.make_async_copy(w_value, w_v, arrive.at[chunks + 1])
    in_tokens = [
        pltpu.make_async_copy(
            tokens.at[pl.ds(i * per * N2, per * N2)],
            tokens_v.at[pl.ds(i * per * N2, per * N2)],
            arrive.at[i],
        )
        for i in range(chunks)
    ]
    outs = [
        pltpu.make_async_copy(
            out_v.at[:, pl.ds(i * per, per)], out.at[:, pl.ds(i * per, per)], leave.at[i]
        )
        for i in range(chunks)
    ]
    in_w.start()
    in_tokens[0].start()
    in_first.start()
    for copy in in_tokens[1:]:
        copy.start()
    in_w.wait()
    for i in range(chunks):
        in_tokens[i].wait()
        value = dot_nn(tokens_v[i * per * N2 : (i + 1) * per * N2], w_v[...]).astype(bf16)
        if i == 0:
            in_first.wait()
            first_v[...] = first_v[...].T
        for r in range(per):
            section = dot_nn(value[row_slice(r)].T, first_v[...]).astype(bf16)
            out_v[:, i * per + r] = section.reshape(n, chans, N2)
        outs[i].start()
    for copy in outs:
        copy.wait()


def d_three_kernel(
    tokens,
    cotangent,
    w_value,
    w_gate,
    fourth,
    out,
    value_out,
    d_mix_out,
    tokens_t_out,
    skip_out,
    w_value_t,
    w_gate_t,
):
    n, per, chans, _ = out.shape

    @pl.when(pl.program_id(0) == 0)
    def _():
        skip_out[...] = jnp.zeros_like(skip_out)
        w_value_t[...] = w_value[...].T
        w_gate_t[...] = w_gate[...].T

    for r in range(per):
        here = row_slice(r)
        value = dot_nn(tokens[here], w_value[...]).astype(bf16)
        gate = dot_nn(tokens[here], w_gate[...]).astype(bf16)
        d_mix = (cotangent[here].astype(f32) * gate.astype(f32)).astype(bf16)
        value_out[here] = value
        d_mix_out[here] = d_mix
        tokens_t_out[:, here] = tokens[here].T
        skip_out[...] += jnp.sum(
            d_mix.astype(f32) * value.astype(f32), axis=0, keepdims=True
        )
        section = dot_nn(d_mix.T, fourth[...]).astype(bf16)
        out[:, r] = section.reshape(n, chans, N2)


def turn_in(swap, arrived, by_channel):
    def body(i, _):
        rows = pl.ds(pl.multiple_of(i * GROUP, GROUP), GROUP)
        block = arrived[rows].reshape(GROUP * GROUP, N2)
        turned = dot_nn(swap[...], block).astype(bf16)
        by_channel[:, rows, :] = turned.reshape(GROUP, GROUP, N2)
        return 0

    lax.fori_loop(0, N1 // GROUP, body, 0, unroll=2)


def turn_out(swap, by_channel, out):
    def body(i, _):
        rows = pl.ds(pl.multiple_of(i * GROUP, GROUP), GROUP)
        block = by_channel[:, rows, :].reshape(GROUP * GROUP, N2)
        turned = dot_nn(swap[...], block).astype(bf16)
        out[rows] = turned.reshape(GROUP, GROUP, N2)
        return 0

    lax.fori_loop(0, N1 // GROUP, body, 0, unroll=2)


def home_forward_kernel(arrived, kernel, second, third, swap, out, spectrum_out, by_channel):
    turn_in(swap, arrived, by_channel)

    def body(c, _):
        spectrum = dot_nn(second[...], by_channel[c])
        spectrum_out[c] = spectrum
        filtered = (spectrum * kernel[c].astype(f32)).astype(bf16)
        by_channel[c] = dot_nn(third[...], filtered).astype(bf16)
        return 0

    lax.fori_loop(0, GROUP, body, 0, unroll=2)
    turn_out(swap, by_channel, out)


def home_backward_kernel(
    arrived, kernel, spectrum, second_t, third_t, swap, out, grad_kernel, by_channel
):
    turn_in(swap, arrived, by_channel)

    def body(c, _):
        d_freq = dot_nn(third_t[...], by_channel[c])
        grad_kernel[c] = (d_freq * spectrum[c]).astype(bf16)
        d_spec = (d_freq * kernel[c].astype(f32)).astype(bf16)
        by_channel[c] = dot_nn(second_t[...], d_spec).astype(bf16)
        return 0

    lax.fori_loop(0, GROUP, body, 0, unroll=2)
    turn_out(swap, by_channel, out)


def accumulate(total, term):
    @pl.when(pl.program_id(0) == 0)
    def _():
        total[...] = term

    @pl.when(pl.program_id(0) > 0)
    def _():
        total[...] += term


def finish(total, factor, grad_w):
    @pl.when(pl.program_id(0) == pl.num_programs(0) - 1)
    def _():
        grad_w[...] = (total[...] * factor[0, 0]).astype(bf16)


def gate_kernel(
    arrived,
    tokens_t,
    value,
    cotangent,
    fourth,
    w_gate_t,
    skip,
    factor,
    partial,
    grad_w,
    total,
    d_gate,
):
    for r in range(arrived.shape[1]):
        here = row_slice(r)
        conv = dot_nt(fourth[...], arrived[:, r].reshape(D, N2))
        mixed = conv + skip[...] * value[here].astype(f32)
        d_gate[here] = (cotangent[here].astype(f32) * mixed).astype(bf16)
        partial[here] = dot_nn(d_gate[here], w_gate_t[...]).astype(bf16)
    accumulate(total, dot_nn(tokens_t[...], d_gate[...]))
    finish(total, factor, grad_w)


def value_kernel(
    per,
    arrived,
    tokens_t,
    d_mix,
    first_t,
    skip,
    factor,
    bit,
    _,
    kept,
    given,
    d_value_out,
    arrived_v,
    tokens_v,
    d_mix_v,
    d_value,
    total,
    arrive,
    leave,
):
    rows = arrived.shape[1]
    chunks = rows // per

    def copies(i):
        lines = pl.ds(i * per, per)
        here = pl.ds(i * per * N2, per * N2)
        return [
            pltpu.make_async_copy(
                arrived.at[:, lines], arrived_v.at[:, lines], arrive.at[i, 0]
            ),
            pltpu.make_async_copy(d_mix.at[here], d_mix_v.at[here], arrive.at[i, 1]),
            pltpu.make_async_copy(
                tokens_t.at[:, here], tokens_v.at[:, here], arrive.at[i, 2]
            ),
        ]

    started = [copies(i) for i in range(chunks)]
    for group in started:
        for copy in group:
            copy.start()
    outs = []
    for i in range(chunks):
        started[i][0].wait()
        started[i][1].wait()
        for r in range(i * per, (i + 1) * per):
            here = row_slice(r)
            d_cube = dot_nt(first_t[...], arrived_v[:, r].reshape(D, N2))
            d_value[here] = (d_cube + skip[...] * d_mix_v[here].astype(f32)).astype(bf16)
        here = pl.ds(i * per * N2, per * N2)
        outs.append(pltpu.make_async_copy(d_value.at[here], d_value_out.at[here], leave.at[i]))
        outs[i].start()
        started[i][2].wait()
        here = slice(i * per * N2, (i + 1) * per * N2)
        term = dot_nn(tokens_v[:, here], d_value[here])
        if i == 0:
            total[...] = term
        else:
            total[...] += term
    size = kept.shape[1]
    for high in range(2):
        for part, low in ((kept, bit[0, 0]), (given, 1 - bit[0, 0])):
            start = pl.multiple_of((2 * high + low) * size, size)
            part[high] = (total[pl.ds(start, size)] * factor[0, 0]).astype(bf16)
    for copy in outs:
        copy.wait()


def tokens_kernel(d_value, partial, w_value_t, *rest):
    grad_tokens = rest[-1]
    for r in range(d_value.shape[0] // N2):
        here = row_slice(r)
        grad_tokens[here] = (
            partial[here].astype(f32) + dot_nn(d_value[here], w_value_t[...])
        ).astype(bf16)


def from_partner(array, b, n):
    return lax.ppermute(array, "seq", [(i, i ^ (1 << b)) for i in range(n)])


def halves(part, axis, b):
    bit = (lax.axis_index("seq") >> b) & 1
    kept = lax.dynamic_index_in_dim(part, bit, axis, keepdims=False)
    sent = lax.dynamic_index_in_dim(part, 1 - bit, axis, keepdims=False)
    return kept, sent


def added(kept, got):
    return (kept.astype(f32) + got.astype(f32)).astype(bf16)


def doubled(part, axis, b, n):
    bit = (lax.axis_index("seq") >> b) & 1
    mine = jnp.expand_dims(part, axis)
    other = jnp.expand_dims(from_partner(part, b, n), axis)
    around = jnp.concatenate([mine, other, mine], axis)
    return lax.dynamic_slice_in_dim(around, bit, 2, axis)


def on_device(
    tokens,
    w_value,
    w_gate,
    first_block,
    second_block,
    third_block,
    fourth_block,
    kernel,
    skip_gain,
    cotangent,
):
    n = lax.axis_size("seq")
    rows = N1 // n
    chans = D // n
    local_rows = tokens.shape[0]
    sections = (n, rows, chans, N2)
    factor = (1.0 / jnp.sqrt(jnp.asarray(N1 * N2, f32))).reshape(1, 1)
    skip = skip_gain.reshape(1, D)
    square = whole((D, D))
    block = whole((N1, N2))
    line = whole((1, D))
    per = min(4, rows)
    row = rows_of(per)
    column = pl.BlockSpec((D, per * N2), lambda i: (0, i))
    sent = by_device(n, per, chans)
    one = pl.BlockSpec(memory_space=pltpu.SMEM)
    place = jnp.arange(GROUP * GROUP)
    swap = (
        place[None, :] == ((place % GROUP) * GROUP + place // GROUP)[:, None]
    ).astype(bf16)

    def cost(gflop, mib):
        scale = rows / 16
        return pl.CostEstimate(
            flops=int(gflop * 1e9 * scale), bytes_accessed=int(mib * 2**20 * scale), transcendentals=0
        )

    def shape(dims, dtype=bf16):
        return jax.ShapeDtypeStruct(dims, dtype)

    def transfer(array):
        return lax.all_to_all(array, "seq", split_axis=0, concat_axis=0, tiled=True)

    unread = pl.BlockSpec(memory_space=pl.ANY)
    one_sent = pl.pallas_call(
        functools.partial(section_one_kernel, per),
        in_specs=[unread] * 3,
        out_specs=unread,
        out_shape=shape(sections),
        scratch_shapes=[
            pltpu.VMEM((local_rows, D), bf16),
            pltpu.VMEM((D, D), bf16),
            pltpu.VMEM((N2, N2), bf16),
            pltpu.VMEM(sections, bf16),
            pltpu.SemaphoreType.DMA((rows // per + 2,)),
            pltpu.SemaphoreType.DMA((rows // per,)),
        ],
        compiler_params=params(),
        cost_estimate=cost(3.2, 9),
    )(tokens, w_value, first_block)
    one_home = transfer(one_sent)

    three_sent, value, d_mix, tokens_t, skip_term, w_value_t, w_gate_t = pl.pallas_call(
        d_three_kernel,
        grid=(rows // per,),
        in_specs=[row, row, square, square, block],
        out_specs=[sent, row, row, column, line, square, square],
        out_shape=[
            shape(sections),
            shape((local_rows, D)),
            shape((local_rows, D)),
            shape((D, local_rows)),
            shape((1, D), f32),
            shape((D, D)),
            shape((D, D)),
        ],
        compiler_params=params(),
        cost_estimate=cost(5.4, 25),
    )(tokens, cotangent, w_value, w_gate, fourth_block)
    three_home = transfer(three_sent)

    at_home = pl.BlockSpec((N1, GROUP, N2), lambda i: (0, i, 0))
    filters = pl.BlockSpec((GROUP, N1, N2), lambda i: (i, 0, 0))
    three_back, spectrum = pl.pallas_call(
        home_forward_kernel,
        grid=(chans // GROUP,),
        in_specs=[at_home, filters, block, block, block],
        out_specs=[at_home, filters],
        out_shape=[shape((N1, chans, N2)), shape((chans, N1, N2), f32)],
        scratch_shapes=[pltpu.VMEM((GROUP, N1, N2), bf16)],
        compiler_params=params(),
        cost_estimate=cost(4.3, 20),
    )(one_home.reshape(N1, chans, N2), kernel, second_block, third_block, swap)
    three_here = transfer(three_back.reshape(sections))

    one_back, grad_kernel = pl.pallas_call(
        home_backward_kernel,
        grid=(chans // GROUP,),
        in_specs=[at_home, filters, filters, block, block, block],
        out_specs=[at_home, filters],
        out_shape=[shape((N1, chans, N2)), shape((chans, N1, N2))],
        scratch_shapes=[pltpu.VMEM((GROUP, N1, N2), bf16)],
        compiler_params=params(),
        cost_estimate=cost(4.3, 24),
    )(
        three_home.reshape(N1, chans, N2),
        kernel,
        spectrum,
        second_block.T,
        third_block.T,
        swap,
    )
    one_here = transfer(one_back.reshape(sections))

    partial, gate_term = pl.pallas_call(
        gate_kernel,
        grid=(rows // per,),
        in_specs=[sent, column, row, row, block, square, line, one],
        out_specs=[row, square],
        out_shape=[shape((local_rows, D)), shape((D, D))],
        scratch_shapes=[pltpu.VMEM((D, D), f32), pltpu.VMEM((per * N2, D), bf16)],
        compiler_params=params(),
        cost_estimate=cost(5.4, 25),
    )(three_here, tokens_t, value, cotangent, fourth_block, w_gate_t, skip, factor)

    skip_lanes = jnp.broadcast_to((skip_term * factor[0, 0]).astype(bf16).T, (D, LANES))
    gate_term = jnp.concatenate([gate_term, skip_lanes], axis=1)
    bits = n.bit_length() - 1
    gate_part = gate_term.reshape((2,) * bits + (D // n, D + LANES))
    for b in range(bits):
        kept, given = halves(gate_part, bits - 1 - b, b)
        gate_part = added(kept, from_partner(given, b, n))

    first_t = first_block.T
    in_vmem = pl.BlockSpec(memory_space=pltpu.VMEM)
    me = lax.axis_index("seq").reshape(1, 1)
    half = (2, D // 4, D)
    kept, given, d_value = pl.pallas_call(
        functools.partial(value_kernel, per),
        in_specs=[unread, unread, unread, in_vmem, in_vmem, one, one, unread],
        out_specs=[in_vmem, in_vmem, unread],
        out_shape=[shape(half), shape(half), shape((local_rows, D))],
        scratch_shapes=[
            pltpu.VMEM(sections, bf16),
            pltpu.VMEM((D, local_rows), bf16),
            pltpu.VMEM((local_rows, D), bf16),
            pltpu.VMEM((local_rows, D), bf16),
            pltpu.VMEM((D, D), f32),
            pltpu.SemaphoreType.DMA((rows // per, 3)),
            pltpu.SemaphoreType.DMA((rows // per,)),
        ],
        compiler_params=params(),
        cost_estimate=cost(3.3, 17),
    )(one_here, tokens_t, d_mix, first_t, skip, factor, me & 1, gate_part)

    for b in reversed(range(bits)):
        gate_part = doubled(gate_part, bits - 1 - b, b, n)
    gate_total = gate_part.reshape(D, D + LANES)

    quarters = 4
    pair = max(rows // quarters // 2, 1)
    steps = rows // quarters // pair

    def quarter(i, grad_tokens, after):
        lines = pl.BlockSpec((pair * N2, D), lambda g: (g + i * steps, 0))
        held = [] if grad_tokens is None else [grad_tokens]
        return pl.pallas_call(
            tokens_kernel,
            grid=(steps,),
            in_specs=[lines, lines, square, unread] + [unread] * len(held),
            out_specs=lines,
            out_shape=shape((local_rows, D)),
            input_output_aliases={4: 0} if held else {},
            compiler_params=params(),
            cost_estimate=cost(0.53, 3.5),
        )(d_value, partial, w_value_t, after, *held)

    grad_tokens = None
    for b in range(bits):
        if b == 1:
            kept, given = halves(value_part, 0, b)
        elif b > 1:
            kept, given = value_part, value_part
        got = from_partner(given, b, n)
        if b < quarters:
            grad_tokens = quarter(b, grad_tokens, given)
        value_part = added(kept, got)
    for b in (1, 0):
        value_part = doubled(value_part, 1 - b, b, n)
    grad_weights = jnp.stack([value_part.reshape(D, D), gate_total[:, :D]]).astype(f32)
    return grad_tokens, grad_kernel, grad_weights, gate_total[:, D].astype(f32)


def solution(mesh):
    in_specs = (
        P(("parts", "seq"), None),
        P(),
        P(),
        P(),
        P(),
        P(),
        P(),
        P("seq", None, None),
        P(),
        P(("parts", "seq"), None),
    )
    out_specs = (
        P(("parts", "seq"), None),
        P(("parts", "seq"), None, None),
        P("parts", None, None),
        P("parts"),
    )
    return jax.shard_map(
        on_device, mesh=mesh, in_specs=in_specs, out_specs=out_specs, check_vma=False
    )
```

```python
import functools

import functools

import jax
import jax.numpy as jnp
from jax import lax
from jax.experimental import pallas as pl
from jax.experimental.pallas import tpu as pltpu
from jax.sharding import PartitionSpec as P

D = 512
N1 = 256
N2 = 256
GROUP = 16
LANES = 128
VMEM_LIMIT = 56 * 1024 * 1024

f32 = jnp.float32
bf16 = jnp.bfloat16


def dot_nn(a, b):
    return jnp.dot(a, b, preferred_element_type=f32)


def dot_nt(a, b):
    return lax.dot_general(a, b, (((1,), (1,)), ((), ())), preferred_element_type=f32)


def params():
    return pltpu.CompilerParams(vmem_limit_bytes=VMEM_LIMIT)


def whole(shape):
    return pl.BlockSpec(shape, lambda i: (0,) * len(shape))


def rows_of(per):
    return pl.BlockSpec((per * N2, D), lambda i: (i, 0))


def by_device(n, per, chans):
    return pl.BlockSpec((n, per, chans, N2), lambda i: (0, i, 0, 0))


def row_slice(r):
    return slice(r * N2, (r + 1) * N2)


def section_one_kernel(
    per, tokens, w_value, first, out, tokens_v, w_v, first_v, out_v, arrive, leave
):
    n, rows, chans, _ = out.shape
    chunks = rows // per
    in_first = pltpu.make_async_copy(first, first_v, arrive.at[chunks])
    in_w = pltpu.make_async_copy(w_value, w_v, arrive.at[chunks + 1])
    in_tokens = [
        pltpu.make_async_copy(
            tokens.at[pl.ds(i * per * N2, per * N2)],
            tokens_v.at[pl.ds(i * per * N2, per * N2)],
            arrive.at[i],
        )
        for i in range(chunks)
    ]
    outs = [
        pltpu.make_async_copy(
            out_v.at[:, pl.ds(i * per, per)], out.at[:, pl.ds(i * per, per)], leave.at[i]
        )
        for i in range(chunks)
    ]
    in_w.start()
    in_tokens[0].start()
    in_first.start()
    for copy in in_tokens[1:]:
        copy.start()
    in_w.wait()
    for i in range(chunks):
        in_tokens[i].wait()
        value = dot_nn(tokens_v[i * per * N2 : (i + 1) * per * N2], w_v[...]).astype(bf16)
        if i == 0:
            in_first.wait()
            first_v[...] = first_v[...].T
        for r in range(per):
            section = dot_nn(value[row_slice(r)].T, first_v[...]).astype(bf16)
            out_v[:, i * per + r] = section.reshape(n, chans, N2)
        outs[i].start()
    for copy in outs:
        copy.wait()


def d_three_kernel(
    tokens,
    cotangent,
    w_value,
    w_gate,
    fourth,
    out,
    value_out,
    d_mix_out,
    tokens_t_out,
    skip_out,
    w_value_t,
    w_gate_t,
):
    n, per, chans, _ = out.shape

    @pl.when(pl.program_id(0) == 0)
    def _():
        skip_out[...] = jnp.zeros_like(skip_out)
        w_value_t[...] = w_value[...].T
        w_gate_t[...] = w_gate[...].T

    for r in range(per):
        here = row_slice(r)
        value = dot_nn(tokens[here], w_value[...]).astype(bf16)
        gate = dot_nn(tokens[here], w_gate[...]).astype(bf16)
        d_mix = (cotangent[here].astype(f32) * gate.astype(f32)).astype(bf16)
        value_out[here] = value
        d_mix_out[here] = d_mix
        tokens_t_out[:, here] = tokens[here].T
        skip_out[...] += jnp.sum(
            d_mix.astype(f32) * value.astype(f32), axis=0, keepdims=True
        )
        section = dot_nn(d_mix.T, fourth[...]).astype(bf16)
        out[:, r] = section.reshape(n, chans, N2)


def turn_in(swap, arrived, by_channel):
    def body(i, _):
        rows = pl.ds(pl.multiple_of(i * GROUP, GROUP), GROUP)
        block = arrived[rows].reshape(GROUP * GROUP, N2)
        turned = dot_nn(swap[...], block).astype(bf16)
        by_channel[:, rows, :] = turned.reshape(GROUP, GROUP, N2)
        return 0

    lax.fori_loop(0, N1 // GROUP, body, 0, unroll=2)


def turn_out(swap, by_channel, out):
    def body(i, _):
        rows = pl.ds(pl.multiple_of(i * GROUP, GROUP), GROUP)
        block = by_channel[:, rows, :].reshape(GROUP * GROUP, N2)
        turned = dot_nn(swap[...], block).astype(bf16)
        out[rows] = turned.reshape(GROUP, GROUP, N2)
        return 0

    lax.fori_loop(0, N1 // GROUP, body, 0, unroll=2)


def home_forward_kernel(arrived, kernel, second, third, swap, out, spectrum_out, by_channel):
    turn_in(swap, arrived, by_channel)

    def body(c, _):
        spectrum = dot_nn(second[...], by_channel[c])
        spectrum_out[c] = spectrum
        filtered = (spectrum * kernel[c].astype(f32)).astype(bf16)
        by_channel[c] = dot_nn(third[...], filtered).astype(bf16)
        return 0

    lax.fori_loop(0, GROUP, body, 0, unroll=2)
    turn_out(swap, by_channel, out)


def home_backward_kernel(
    arrived, kernel, spectrum, second_t, third_t, swap, out, grad_kernel, by_channel
):
    turn_in(swap, arrived, by_channel)

    def body(c, _):
        d_freq = dot_nn(third_t[...], by_channel[c])
        grad_kernel[c] = (d_freq * spectrum[c]).astype(bf16)
        d_spec = (d_freq * kernel[c].astype(f32)).astype(bf16)
        by_channel[c] = dot_nn(second_t[...], d_spec).astype(bf16)
        return 0

    lax.fori_loop(0, GROUP, body, 0, unroll=2)
    turn_out(swap, by_channel, out)


def accumulate(total, term):
    @pl.when(pl.program_id(0) == 0)
    def _():
        total[...] = term

    @pl.when(pl.program_id(0) > 0)
    def _():
        total[...] += term


def finish(total, factor, grad_w):
    @pl.when(pl.program_id(0) == pl.num_programs(0) - 1)
    def _():
        grad_w[...] = (total[...] * factor[0, 0]).astype(bf16)


def gate_kernel(
    arrived,
    tokens_t,
    value,
    cotangent,
    fourth,
    w_gate_t,
    skip,
    factor,
    partial,
    grad_w,
    total,
    d_gate,
):
    for r in range(arrived.shape[1]):
        here = row_slice(r)
        conv = dot_nt(fourth[...], arrived[:, r].reshape(D, N2))
        mixed = conv + skip[...] * value[here].astype(f32)
        d_gate[here] = (cotangent[here].astype(f32) * mixed).astype(bf16)
        partial[here] = dot_nn(d_gate[here], w_gate_t[...]).astype(bf16)
    accumulate(total, dot_nn(tokens_t[...], d_gate[...]))
    finish(total, factor, grad_w)


def value_kernel(
    per,
    arrived,
    tokens_t,
    d_mix,
    first_t,
    skip,
    factor,
    bit,
    _,
    kept,
    given,
    d_value_out,
    arrived_v,
    tokens_v,
    d_mix_v,
    d_value,
    total,
    arrive,
    leave,
):
    rows = arrived.shape[1]
    chunks = rows // per

    def copies(i):
        lines = pl.ds(i * per, per)
        here = pl.ds(i * per * N2, per * N2)
        return [
            pltpu.make_async_copy(
                arrived.at[:, lines], arrived_v.at[:, lines], arrive.at[i, 0]
            ),
            pltpu.make_async_copy(d_mix.at[here], d_mix_v.at[here], arrive.at[i, 1]),
            pltpu.make_async_copy(
                tokens_t.at[:, here], tokens_v.at[:, here], arrive.at[i, 2]
            ),
        ]

    started = [copies(i) for i in range(chunks)]
    for group in started:
        for copy in group:
            copy.start()
    outs = []
    for i in range(chunks):
        started[i][0].wait()
        started[i][1].wait()
        for r in range(i * per, (i + 1) * per):
            here = row_slice(r)
            d_cube = dot_nt(first_t[...], arrived_v[:, r].reshape(D, N2))
            d_value[here] = (d_cube + skip[...] * d_mix_v[here].astype(f32)).astype(bf16)
        here = pl.ds(i * per * N2, per * N2)
        outs.append(pltpu.make_async_copy(d_value.at[here], d_value_out.at[here], leave.at[i]))
        outs[i].start()
        started[i][2].wait()
    total[...] = dot_nn(tokens_v[...], d_value[...])
    size = kept.shape[1]
    for high in range(2):
        for part, low in ((kept, bit[0, 0]), (given, 1 - bit[0, 0])):
            start = pl.multiple_of((2 * high + low) * size, size)
            part[high] = (total[pl.ds(start, size)] * factor[0, 0]).astype(bf16)
    for copy in outs:
        copy.wait()


def tokens_kernel(d_value, partial, w_value_t, *rest):
    grad_tokens = rest[-1]
    for r in range(d_value.shape[0] // N2):
        here = row_slice(r)
        grad_tokens[here] = (
            partial[here].astype(f32) + dot_nn(d_value[here], w_value_t[...])
        ).astype(bf16)


def from_partner(array, b, n):
    return lax.ppermute(array, "seq", [(i, i ^ (1 << b)) for i in range(n)])


def halves(part, axis, b):
    bit = (lax.axis_index("seq") >> b) & 1
    kept = lax.dynamic_index_in_dim(part, bit, axis, keepdims=False)
    sent = lax.dynamic_index_in_dim(part, 1 - bit, axis, keepdims=False)
    return kept, sent


def added(kept, got):
    return (kept.astype(f32) + got.astype(f32)).astype(bf16)


def doubled(part, axis, b, n):
    bit = (lax.axis_index("seq") >> b) & 1
    mine = jnp.expand_dims(part, axis)
    other = jnp.expand_dims(from_partner(part, b, n), axis)
    around = jnp.concatenate([mine, other, mine], axis)
    return lax.dynamic_slice_in_dim(around, bit, 2, axis)


def on_device(
    tokens,
    w_value,
    w_gate,
    first_block,
    second_block,
    third_block,
    fourth_block,
    kernel,
    skip_gain,
    cotangent,
):
    n = lax.axis_size("seq")
    rows = N1 // n
    chans = D // n
    local_rows = tokens.shape[0]
    sections = (n, rows, chans, N2)
    factor = (1.0 / jnp.sqrt(jnp.asarray(N1 * N2, f32))).reshape(1, 1)
    skip = skip_gain.reshape(1, D)
    square = whole((D, D))
    block = whole((N1, N2))
    line = whole((1, D))
    per = min(4, rows)
    row = rows_of(per)
    column = pl.BlockSpec((D, per * N2), lambda i: (0, i))
    sent = by_device(n, per, chans)
    one = pl.BlockSpec(memory_space=pltpu.SMEM)
    place = jnp.arange(GROUP * GROUP)
    swap = (
        place[None, :] == ((place % GROUP) * GROUP + place // GROUP)[:, None]
    ).astype(bf16)

    def cost(gflop, mib):
        scale = rows / 16
        return pl.CostEstimate(
            flops=int(gflop * 1e9 * scale), bytes_accessed=int(mib * 2**20 * scale), transcendentals=0
        )

    def shape(dims, dtype=bf16):
        return jax.ShapeDtypeStruct(dims, dtype)

    def transfer(array):
        return lax.all_to_all(array, "seq", split_axis=0, concat_axis=0, tiled=True)

    unread = pl.BlockSpec(memory_space=pl.ANY)
    one_sent = pl.pallas_call(
        functools.partial(section_one_kernel, per),
        in_specs=[unread] * 3,
        out_specs=unread,
        out_shape=shape(sections),
        scratch_shapes=[
            pltpu.VMEM((local_rows, D), bf16),
            pltpu.VMEM((D, D), bf16),
            pltpu.VMEM((N2, N2), bf16),
            pltpu.VMEM(sections, bf16),
            pltpu.SemaphoreType.DMA((rows // per + 2,)),
            pltpu.SemaphoreType.DMA((rows // per,)),
        ],
        compiler_params=params(),
        cost_estimate=cost(3.2, 9),
    )(tokens, w_value, first_block)
    one_home = transfer(one_sent)

    three_sent, value, d_mix, tokens_t, skip_term, w_value_t, w_gate_t = pl.pallas_call(
        d_three_kernel,
        grid=(rows // per,),
        in_specs=[row, row, square, square, block],
        out_specs=[sent, row, row, column, line, square, square],
        out_shape=[
            shape(sections),
            shape((local_rows, D)),
            shape((local_rows, D)),
            shape((D, local_rows)),
            shape((1, D), f32),
            shape((D, D)),
            shape((D, D)),
        ],
        compiler_params=params(),
        cost_estimate=cost(5.4, 25),
    )(tokens, cotangent, w_value, w_gate, fourth_block)
    three_home = transfer(three_sent)

    at_home = pl.BlockSpec((N1, GROUP, N2), lambda i: (0, i, 0))
    filters = pl.BlockSpec((GROUP, N1, N2), lambda i: (i, 0, 0))
    three_back, spectrum = pl.pallas_call(
        home_forward_kernel,
        grid=(chans // GROUP,),
        in_specs=[at_home, filters, block, block, block],
        out_specs=[at_home, filters],
        out_shape=[shape((N1, chans, N2)), shape((chans, N1, N2), f32)],
        scratch_shapes=[pltpu.VMEM((GROUP, N1, N2), bf16)],
        compiler_params=params(),
        cost_estimate=cost(4.3, 20),
    )(one_home.reshape(N1, chans, N2), kernel, second_block, third_block, swap)
    three_here = transfer(three_back.reshape(sections))

    one_back, grad_kernel = pl.pallas_call(
        home_backward_kernel,
        grid=(chans // GROUP,),
        in_specs=[at_home, filters, filters, block, block, block],
        out_specs=[at_home, filters],
        out_shape=[shape((N1, chans, N2)), shape((chans, N1, N2))],
        scratch_shapes=[pltpu.VMEM((GROUP, N1, N2), bf16)],
        compiler_params=params(),
        cost_estimate=cost(4.3, 24),
    )(
        three_home.reshape(N1, chans, N2),
        kernel,
        spectrum,
        second_block.T,
        third_block.T,
        swap,
    )
    one_here = transfer(one_back.reshape(sections))

    partial, gate_term = pl.pallas_call(
        gate_kernel,
        grid=(rows // per,),
        in_specs=[sent, column, row, row, block, square, line, one],
        out_specs=[row, square],
        out_shape=[shape((local_rows, D)), shape((D, D))],
        scratch_shapes=[pltpu.VMEM((D, D), f32), pltpu.VMEM((per * N2, D), bf16)],
        compiler_params=params(),
        cost_estimate=cost(5.4, 25),
    )(three_here, tokens_t, value, cotangent, fourth_block, w_gate_t, skip, factor)

    skip_lanes = jnp.broadcast_to((skip_term * factor[0, 0]).astype(bf16).T, (D, LANES))
    gate_term = jnp.concatenate([gate_term, skip_lanes], axis=1)
    bits = n.bit_length() - 1
    gate_part = gate_term.reshape((2,) * bits + (D // n, D + LANES))
    for b in range(bits):
        early = gate_part
        kept, given = halves(gate_part, bits - 1 - b, b)
        gate_part = added(kept, from_partner(given, b, n))

    first_t = first_block.T
    in_vmem = pl.BlockSpec(memory_space=pltpu.VMEM)
    me = lax.axis_index("seq").reshape(1, 1)
    half = (2, D // 4, D)
    kept, given, d_value = pl.pallas_call(
        functools.partial(value_kernel, per),
        in_specs=[unread, unread, unread, in_vmem, in_vmem, one, one, unread],
        out_specs=[in_vmem, in_vmem, unread],
        out_shape=[shape(half), shape(half), shape((local_rows, D))],
        scratch_shapes=[
            pltpu.VMEM(sections, bf16),
            pltpu.VMEM((D, local_rows), bf16),
            pltpu.VMEM((local_rows, D), bf16),
            pltpu.VMEM((local_rows, D), bf16),
            pltpu.VMEM((D, D), f32),
            pltpu.SemaphoreType.DMA((rows // per, 3)),
            pltpu.SemaphoreType.DMA((rows // per,)),
        ],
        compiler_params=params(),
        cost_estimate=cost(3.3, 17),
    )(one_here, tokens_t, d_mix, first_t, skip, factor, me & 1, early)

    for b in reversed(range(bits)):
        gate_part = doubled(gate_part, bits - 1 - b, b, n)
    gate_total = gate_part.reshape(D, D + LANES)

    quarters = 4
    pair = max(rows // quarters // 2, 1)
    steps = rows // quarters // pair

    def quarter(i, grad_tokens, after):
        lines = pl.BlockSpec((pair * N2, D), lambda g: (g + i * steps, 0))
        held = [] if grad_tokens is None else [grad_tokens]
        return pl.pallas_call(
            tokens_kernel,
            grid=(steps,),
            in_specs=[lines, lines, square, unread] + [unread] * len(held),
            out_specs=lines,
            out_shape=shape((local_rows, D)),
            input_output_aliases={4: 0} if held else {},
            compiler_params=params(),
            cost_estimate=cost(0.53, 3.5),
        )(d_value, partial, w_value_t, after, *held)

    grad_tokens = None
    for b in range(bits):
        if b == 1:
            kept, given = halves(value_part, 0, b)
        elif b > 1:
            kept, given = value_part, value_part
        got = from_partner(given, b, n)
        if 0 < b < quarters:
            grad_tokens = quarter(b - 1, grad_tokens, given)
        value_part = added(kept, got)
    grad_tokens = quarter(quarters - 1, grad_tokens, value_part)
    for b in (1, 0):
        value_part = doubled(value_part, 1 - b, b, n)
    grad_weights = jnp.broadcast_to(gate_total[None, :, :D].astype(f32), (2, D, D))
    grad_weights = lax.dynamic_update_slice(
        grad_weights, value_part.reshape(1, D, D).astype(f32), (0, 0, 0)
    )
    return grad_tokens, grad_kernel, grad_weights, gate_total[:, D].astype(f32)


def solution(mesh):
    in_specs = (
        P(("parts", "seq"), None),
        P(),
        P(),
        P(),
        P(),
        P(),
        P(),
        P("seq", None, None),
        P(),
        P(("parts", "seq"), None),
    )
    out_specs = (
        P(("parts", "seq"), None),
        P(("parts", "seq"), None, None),
        P("parts", None, None),
        P("parts"),
    )
    return jax.shard_map(
        on_device, mesh=mesh, in_specs=in_specs, out_specs=out_specs, check_vma=False
    )
```

```python
import functools

import functools

import jax
import jax.numpy as jnp
from jax import lax
from jax.experimental import pallas as pl
from jax.experimental.pallas import tpu as pltpu
from jax.sharding import PartitionSpec as P

D = 512
N1 = 256
N2 = 256
GROUP = 16
LANES = 128
VMEM_LIMIT = 56 * 1024 * 1024

f32 = jnp.float32
bf16 = jnp.bfloat16


def dot_nn(a, b):
    return jnp.dot(a, b, preferred_element_type=f32)


def dot_nt(a, b):
    return lax.dot_general(a, b, (((1,), (1,)), ((), ())), preferred_element_type=f32)


def params():
    return pltpu.CompilerParams(vmem_limit_bytes=VMEM_LIMIT)


def whole(shape):
    return pl.BlockSpec(shape, lambda i: (0,) * len(shape))


def rows_of(per):
    return pl.BlockSpec((per * N2, D), lambda i: (i, 0))


def by_device(n, per, chans):
    return pl.BlockSpec((n, per, chans, N2), lambda i: (0, i, 0, 0))


def row_slice(r):
    return slice(r * N2, (r + 1) * N2)


def section_one_kernel(
    per, tokens, w_value, first, out, tokens_v, w_v, first_v, out_v, arrive, leave
):
    n, rows, chans, _ = out.shape
    chunks = rows // per
    in_first = pltpu.make_async_copy(first, first_v, arrive.at[chunks])
    in_w = pltpu.make_async_copy(w_value, w_v, arrive.at[chunks + 1])
    in_tokens = [
        pltpu.make_async_copy(
            tokens.at[pl.ds(i * per * N2, per * N2)],
            tokens_v.at[pl.ds(i * per * N2, per * N2)],
            arrive.at[i],
        )
        for i in range(chunks)
    ]
    outs = [
        pltpu.make_async_copy(
            out_v.at[:, pl.ds(i * per, per)], out.at[:, pl.ds(i * per, per)], leave.at[i]
        )
        for i in range(chunks)
    ]
    in_w.start()
    in_tokens[0].start()
    in_first.start()
    in_tokens[1].start()
    in_w.wait()
    for i in range(chunks):
        in_tokens[i].wait()
        if i + 2 < chunks:
            in_tokens[i + 2].start()
        value = dot_nn(tokens_v[i * per * N2 : (i + 1) * per * N2], w_v[...]).astype(bf16)
        if i == 0:
            in_first.wait()
            first_v[...] = first_v[...].T
        for r in range(per):
            section = dot_nn(value[row_slice(r)].T, first_v[...]).astype(bf16)
            out_v[:, i * per + r] = section.reshape(n, chans, N2)
        outs[i].start()
    for copy in outs:
        copy.wait()


def d_three_kernel(
    tokens,
    cotangent,
    w_value,
    w_gate,
    fourth,
    out,
    value_out,
    d_mix_out,
    tokens_t_out,
    skip_out,
    w_value_t,
    w_gate_t,
):
    n, per, chans, _ = out.shape

    @pl.when(pl.program_id(0) == 0)
    def _():
        skip_out[...] = jnp.zeros_like(skip_out)
        w_value_t[...] = w_value[...].T
        w_gate_t[...] = w_gate[...].T

    for r in range(per):
        here = row_slice(r)
        value = dot_nn(tokens[here], w_value[...]).astype(bf16)
        gate = dot_nn(tokens[here], w_gate[...]).astype(bf16)
        d_mix = (cotangent[here].astype(f32) * gate.astype(f32)).astype(bf16)
        value_out[here] = value
        d_mix_out[here] = d_mix
        tokens_t_out[:, here] = tokens[here].T
        skip_out[...] += jnp.sum(
            d_mix.astype(f32) * value.astype(f32), axis=0, keepdims=True
        )
        section = dot_nn(d_mix.T, fourth[...]).astype(bf16)
        out[:, r] = section.reshape(n, chans, N2)


def turn_in(swap, arrived, by_channel):
    def body(i, _):
        rows = pl.ds(pl.multiple_of(i * GROUP, GROUP), GROUP)
        block = arrived[rows].reshape(GROUP * GROUP, N2)
        turned = dot_nn(swap[...], block).astype(bf16)
        by_channel[:, rows, :] = turned.reshape(GROUP, GROUP, N2)
        return 0

    lax.fori_loop(0, N1 // GROUP, body, 0, unroll=2)


def turn_out(swap, by_channel, out):
    def body(i, _):
        rows = pl.ds(pl.multiple_of(i * GROUP, GROUP), GROUP)
        block = by_channel[:, rows, :].reshape(GROUP * GROUP, N2)
        turned = dot_nn(swap[...], block).astype(bf16)
        out[rows] = turned.reshape(GROUP, GROUP, N2)
        return 0

    lax.fori_loop(0, N1 // GROUP, body, 0, unroll=2)


def home_forward_kernel(arrived, kernel, second, third, swap, out, spectrum_out, by_channel):
    turn_in(swap, arrived, by_channel)

    def body(c, _):
        spectrum = dot_nn(second[...], by_channel[c])
        spectrum_out[c] = spectrum
        filtered = (spectrum * kernel[c].astype(f32)).astype(bf16)
        by_channel[c] = dot_nn(third[...], filtered).astype(bf16)
        return 0

    lax.fori_loop(0, GROUP, body, 0, unroll=2)
    turn_out(swap, by_channel, out)


def home_backward_kernel(
    arrived, kernel, spectrum, second_t, third_t, swap, out, grad_kernel, by_channel
):
    turn_in(swap, arrived, by_channel)

    def body(c, _):
        d_freq = dot_nn(third_t[...], by_channel[c])
        grad_kernel[c] = (d_freq * spectrum[c]).astype(bf16)
        d_spec = (d_freq * kernel[c].astype(f32)).astype(bf16)
        by_channel[c] = dot_nn(second_t[...], d_spec).astype(bf16)
        return 0

    lax.fori_loop(0, GROUP, body, 0, unroll=2)
    turn_out(swap, by_channel, out)


def accumulate(total, term):
    @pl.when(pl.program_id(0) == 0)
    def _():
        total[...] = term

    @pl.when(pl.program_id(0) > 0)
    def _():
        total[...] += term


def finish(total, factor, grad_w):
    @pl.when(pl.program_id(0) == pl.num_programs(0) - 1)
    def _():
        grad_w[...] = (total[...] * factor[0, 0]).astype(bf16)


def gate_kernel(
    arrived,
    tokens_t,
    value,
    cotangent,
    fourth,
    w_gate_t,
    skip,
    factor,
    partial,
    grad_w,
    total,
    d_gate,
):
    for r in range(arrived.shape[1]):
        here = row_slice(r)
        conv = dot_nt(fourth[...], arrived[:, r].reshape(D, N2))
        mixed = conv + skip[...] * value[here].astype(f32)
        d_gate[here] = (cotangent[here].astype(f32) * mixed).astype(bf16)
        partial[here] = dot_nn(d_gate[here], w_gate_t[...]).astype(bf16)
    accumulate(total, dot_nn(tokens_t[...], d_gate[...]))
    finish(total, factor, grad_w)


def value_kernel(
    per,
    arrived,
    tokens_t,
    d_mix,
    first_t,
    skip,
    factor,
    bit,
    gate_part,
    kept,
    given,
    d_value_out,
    gate_out,
    arrived_v,
    tokens_v,
    d_mix_v,
    d_value,
    total,
    arrive,
    leave,
    hand_on,
):
    rows = arrived.shape[1]
    chunks = rows // per
    gate_copy = pltpu.make_async_copy(gate_part, gate_out, hand_on)

    def copies(i):
        lines = pl.ds(i * per, per)
        here = pl.ds(i * per * N2, per * N2)
        return [
            pltpu.make_async_copy(
                arrived.at[:, lines], arrived_v.at[:, lines], arrive.at[i, 0]
            ),
            pltpu.make_async_copy(d_mix.at[here], d_mix_v.at[here], arrive.at[i, 1]),
            pltpu.make_async_copy(
                tokens_t.at[:, here], tokens_v.at[:, here], arrive.at[i, 2]
            ),
        ]

    started = [copies(i) for i in range(chunks)]

    def start(i):
        if i < chunks:
            for copy in started[i]:
                copy.start()

    start(0)
    start(1)
    gate_copy.start()
    outs = []
    for i in range(chunks):
        started[i][0].wait()
        started[i][1].wait()
        start(i + 2)
        for r in range(i * per, (i + 1) * per):
            here = row_slice(r)
            d_cube = dot_nt(first_t[...], arrived_v[:, r].reshape(D, N2))
            d_value[here] = (d_cube + skip[...] * d_mix_v[here].astype(f32)).astype(bf16)
        here = pl.ds(i * per * N2, per * N2)
        outs.append(pltpu.make_async_copy(d_value.at[here], d_value_out.at[here], leave.at[i]))
        outs[i].start()
        started[i][2].wait()
        here = slice(i * per * N2, (i + 1) * per * N2)
        term = dot_nn(tokens_v[:, here], d_value[here])
        if i == 0:
            total[...] = term
        else:
            total[...] += term
    size = kept.shape[1]
    for high in range(2):
        for part, low in ((kept, bit[0, 0]), (given, 1 - bit[0, 0])):
            place = pl.multiple_of((2 * high + low) * size, size)
            part[high] = (total[pl.ds(place, size)] * factor[0, 0]).astype(bf16)
    for copy in outs:
        copy.wait()
    gate_copy.wait()


def tokens_kernel(d_value, partial, w_value_t, *rest):
    grad_tokens = rest[-1]
    for r in range(d_value.shape[0] // N2):
        here = row_slice(r)
        grad_tokens[here] = (
            partial[here].astype(f32) + dot_nn(d_value[here], w_value_t[...])
        ).astype(bf16)


def from_partner(array, b, n):
    return lax.ppermute(array, "seq", [(i, i ^ (1 << b)) for i in range(n)])


def halves(part, axis, b):
    bit = (lax.axis_index("seq") >> b) & 1
    kept = lax.dynamic_index_in_dim(part, bit, axis, keepdims=False)
    sent = lax.dynamic_index_in_dim(part, 1 - bit, axis, keepdims=False)
    return kept, sent


def added(kept, got):
    return (kept.astype(f32) + got.astype(f32)).astype(bf16)


def doubled(part, axis, b, n):
    bit = (lax.axis_index("seq") >> b) & 1
    mine = jnp.expand_dims(part, axis)
    other = jnp.expand_dims(from_partner(part, b, n), axis)
    around = jnp.concatenate([mine, other, mine], axis)
    return lax.dynamic_slice_in_dim(around, bit, 2, axis)


def on_device(
    tokens,
    w_value,
    w_gate,
    first_block,
    second_block,
    third_block,
    fourth_block,
    kernel,
    skip_gain,
    cotangent,
):
    n = lax.axis_size("seq")
    rows = N1 // n
    chans = D // n
    local_rows = tokens.shape[0]
    sections = (n, rows, chans, N2)
    factor = (1.0 / jnp.sqrt(jnp.asarray(N1 * N2, f32))).reshape(1, 1)
    skip = skip_gain.reshape(1, D)
    square = whole((D, D))
    block = whole((N1, N2))
    line = whole((1, D))
    per = min(4, rows)
    row = rows_of(per)
    column = pl.BlockSpec((D, per * N2), lambda i: (0, i))
    sent = by_device(n, per, chans)
    one = pl.BlockSpec(memory_space=pltpu.SMEM)
    place = jnp.arange(GROUP * GROUP)
    swap = (
        place[None, :] == ((place % GROUP) * GROUP + place // GROUP)[:, None]
    ).astype(bf16)

    def cost(gflop, mib):
        scale = rows / 16
        return pl.CostEstimate(
            flops=int(gflop * 1e9 * scale), bytes_accessed=int(mib * 2**20 * scale), transcendentals=0
        )

    def shape(dims, dtype=bf16):
        return jax.ShapeDtypeStruct(dims, dtype)

    def transfer(array):
        return lax.all_to_all(array, "seq", split_axis=0, concat_axis=0, tiled=True)

    unread = pl.BlockSpec(memory_space=pl.ANY)
    one_sent = pl.pallas_call(
        functools.partial(section_one_kernel, per),
        in_specs=[unread] * 3,
        out_specs=unread,
        out_shape=shape(sections),
        scratch_shapes=[
            pltpu.VMEM((local_rows, D), bf16),
            pltpu.VMEM((D, D), bf16),
            pltpu.VMEM((N2, N2), bf16),
            pltpu.VMEM(sections, bf16),
            pltpu.SemaphoreType.DMA((rows // per + 2,)),
            pltpu.SemaphoreType.DMA((rows // per,)),
        ],
        compiler_params=params(),
        cost_estimate=cost(3.2, 9),
    )(tokens, w_value, first_block)
    one_home = transfer(one_sent)

    three_sent, value, d_mix, tokens_t, skip_term, w_value_t, w_gate_t = pl.pallas_call(
        d_three_kernel,
        grid=(rows // per,),
        in_specs=[row, row, square, square, block],
        out_specs=[sent, row, row, column, line, square, square],
        out_shape=[
            shape(sections),
            shape((local_rows, D)),
            shape((local_rows, D)),
            shape((D, local_rows)),
            shape((1, D), f32),
            shape((D, D)),
            shape((D, D)),
        ],
        compiler_params=params(),
        cost_estimate=cost(5.4, 25),
    )(tokens, cotangent, w_value, w_gate, fourth_block)
    three_home = transfer(three_sent)

    at_home = pl.BlockSpec((N1, GROUP, N2), lambda i: (0, i, 0))
    filters = pl.BlockSpec((GROUP, N1, N2), lambda i: (i, 0, 0))
    three_back, spectrum = pl.pallas_call(
        home_forward_kernel,
        grid=(chans // GROUP,),
        in_specs=[at_home, filters, block, block, block],
        out_specs=[at_home, filters],
        out_shape=[shape((N1, chans, N2)), shape((chans, N1, N2), f32)],
        scratch_shapes=[pltpu.VMEM((GROUP, N1, N2), bf16)],
        compiler_params=params(),
        cost_estimate=cost(4.3, 20),
    )(one_home.reshape(N1, chans, N2), kernel, second_block, third_block, swap)
    three_here = transfer(three_back.reshape(sections))

    one_back, grad_kernel = pl.pallas_call(
        home_backward_kernel,
        grid=(chans // GROUP,),
        in_specs=[at_home, filters, filters, block, block, block],
        out_specs=[at_home, filters],
        out_shape=[shape((N1, chans, N2)), shape((chans, N1, N2))],
        scratch_shapes=[pltpu.VMEM((GROUP, N1, N2), bf16)],
        compiler_params=params(),
        cost_estimate=cost(4.3, 24),
    )(
        three_home.reshape(N1, chans, N2),
        kernel,
        spectrum,
        second_block.T,
        third_block.T,
        swap,
    )
    one_here = transfer(one_back.reshape(sections))

    partial, gate_term = pl.pallas_call(
        gate_kernel,
        grid=(rows // per,),
        in_specs=[sent, column, row, row, block, square, line, one],
        out_specs=[row, square],
        out_shape=[shape((local_rows, D)), shape((D, D))],
        scratch_shapes=[pltpu.VMEM((D, D), f32), pltpu.VMEM((per * N2, D), bf16)],
        compiler_params=params(),
        cost_estimate=cost(5.4, 25),
    )(three_here, tokens_t, value, cotangent, fourth_block, w_gate_t, skip, factor)

    skip_lanes = jnp.broadcast_to((skip_term * factor[0, 0]).astype(bf16).T, (D, LANES))
    gate_term = jnp.concatenate([gate_term, skip_lanes], axis=1)
    bits = n.bit_length() - 1
    gate_part = gate_term.reshape((2,) * bits + (D // n, D + LANES))
    for b in range(bits):
        kept, given = halves(gate_part, bits - 1 - b, b)
        gate_part = added(kept, from_partner(given, b, n))

    first_t = first_block.T
    in_vmem = pl.BlockSpec(memory_space=pltpu.VMEM)
    me = lax.axis_index("seq").reshape(1, 1)
    half = (2, D // 4, D)
    kept, given, d_value, gate_part = pl.pallas_call(
        functools.partial(value_kernel, per),
        in_specs=[unread, unread, unread, in_vmem, in_vmem, one, one, unread],
        out_specs=[in_vmem, in_vmem, unread, unread],
        out_shape=[shape(half), shape(half), shape((local_rows, D)), shape(gate_part.shape)],
        scratch_shapes=[
            pltpu.VMEM(sections, bf16),
            pltpu.VMEM((D, local_rows), bf16),
            pltpu.VMEM((local_rows, D), bf16),
            pltpu.VMEM((local_rows, D), bf16),
            pltpu.VMEM((D, D), f32),
            pltpu.SemaphoreType.DMA((rows // per, 3)),
            pltpu.SemaphoreType.DMA((rows // per,)),
            pltpu.SemaphoreType.DMA,
        ],
        compiler_params=params(),
        cost_estimate=cost(3.3, 17),
    )(one_here, tokens_t, d_mix, first_t, skip, factor, me & 1, gate_part)

    for b in reversed(range(bits)):
        gate_part = doubled(gate_part, bits - 1 - b, b, n)
    gate_total = gate_part.reshape(D, D + LANES)

    unit = rows // 8
    pieces = [1, 2, 3, 2]

    def piece(i, grad_tokens, after):
        first = sum(pieces[:i])
        lines = pl.BlockSpec((unit * N2, D), lambda g: (g + first, 0))
        held = [] if grad_tokens is None else [grad_tokens]
        return pl.pallas_call(
            tokens_kernel,
            grid=(pieces[i],),
            in_specs=[lines, lines, square, unread] + [unread] * len(held),
            out_specs=lines,
            out_shape=shape((local_rows, D)),
            input_output_aliases={4: 0} if held else {},
            compiler_params=params(),
            cost_estimate=cost(0.265 * pieces[i], 1.5 * pieces[i]),
        )(d_value, partial, w_value_t, after, *held)

    grad_tokens = None
    for b in range(bits):
        if b == 1:
            kept, given = halves(value_part, 0, b)
        elif b > 1:
            kept, given = value_part, value_part
        got = from_partner(given, b, n)
        if b < len(pieces):
            grad_tokens = piece(b, grad_tokens, given)
        value_part = added(kept, got)
    for b in (1, 0):
        value_part = doubled(value_part, 1 - b, b, n)
    grad_weights = jnp.stack([value_part.reshape(D, D), gate_total[:, :D]]).astype(f32)
    return grad_tokens, grad_kernel, grad_weights, gate_total[:, D].astype(f32)


def solution(mesh):
    in_specs = (
        P(("parts", "seq"), None),
        P(),
        P(),
        P(),
        P(),
        P(),
        P(),
        P("seq", None, None),
        P(),
        P(("parts", "seq"), None),
    )
    out_specs = (
        P(("parts", "seq"), None),
        P(("parts", "seq"), None, None),
        P("parts", None, None),
        P("parts"),
    )
    return jax.shard_map(
        on_device, mesh=mesh, in_specs=in_specs, out_specs=out_specs, check_vma=False
    )
```

```python
import functools

import functools

import jax
import jax.numpy as jnp
from jax import lax
from jax.experimental import pallas as pl
from jax.experimental.pallas import tpu as pltpu
from jax.sharding import PartitionSpec as P

D = 512
N1 = 256
N2 = 256
GROUP = 16
LANES = 128
VMEM_LIMIT = 56 * 1024 * 1024

f32 = jnp.float32
bf16 = jnp.bfloat16


def dot_nn(a, b):
    return jnp.dot(a, b, preferred_element_type=f32)


def dot_nt(a, b):
    return lax.dot_general(a, b, (((1,), (1,)), ((), ())), preferred_element_type=f32)


def params():
    return pltpu.CompilerParams(vmem_limit_bytes=VMEM_LIMIT)


def whole(shape):
    return pl.BlockSpec(shape, lambda i: (0,) * len(shape))


def rows_of(per):
    return pl.BlockSpec((per * N2, D), lambda i: (i, 0))


def by_device(n, per, chans):
    return pl.BlockSpec((n, per, chans, N2), lambda i: (0, i, 0, 0))


def row_slice(r):
    return slice(r * N2, (r + 1) * N2)


def section_one_kernel(
    per, tokens, w_value, first, out, tokens_v, w_v, first_v, out_v, arrive, leave
):
    n, rows, chans, _ = out.shape
    chunks = rows // per
    in_first = pltpu.make_async_copy(first, first_v, arrive.at[chunks])
    in_w = pltpu.make_async_copy(w_value, w_v, arrive.at[chunks + 1])
    in_tokens = [
        pltpu.make_async_copy(
            tokens.at[pl.ds(i * per * N2, per * N2)],
            tokens_v.at[pl.ds(i * per * N2, per * N2)],
            arrive.at[i],
        )
        for i in range(chunks)
    ]
    outs = [
        pltpu.make_async_copy(
            out_v.at[:, pl.ds(i * per, per)], out.at[:, pl.ds(i * per, per)], leave.at[i]
        )
        for i in range(chunks)
    ]
    in_w.start()
    in_tokens[0].start()
    in_first.start()
    for copy in in_tokens[1:]:
        copy.start()
    in_w.wait()
    for i in range(chunks):
        in_tokens[i].wait()
        value = dot_nn(tokens_v[i * per * N2 : (i + 1) * per * N2], w_v[...]).astype(bf16)
        if i == 0:
            in_first.wait()
            first_v[...] = first_v[...].T
        for r in range(per):
            section = dot_nn(value[row_slice(r)].T, first_v[...]).astype(bf16)
            out_v[:, i * per + r] = section.reshape(n, chans, N2)
        outs[i].start()
    for copy in outs:
        copy.wait()


def d_three_kernel(
    tokens,
    cotangent,
    w_value,
    w_gate,
    first,
    fourth,
    skip,
    out,
    value_out,
    d_mix_out,
    tokens_t_out,
    turned_out,
    direct_out,
    skip_out,
    w_value_t,
    w_gate_t,
):
    n, per, chans, _ = out.shape

    @pl.when(pl.program_id(0) == 0)
    def _():
        skip_out[...] = jnp.zeros_like(skip_out)
        direct_out[...] = jnp.zeros_like(direct_out)
        w_value_t[...] = w_value[...].T
        w_gate_t[...] = w_gate[...].T

    for r in range(per):
        here = row_slice(r)
        value = dot_nn(tokens[here], w_value[...]).astype(bf16)
        gate = dot_nn(tokens[here], w_gate[...]).astype(bf16)
        d_mix = (cotangent[here].astype(f32) * gate.astype(f32)).astype(bf16)
        value_out[here] = value
        d_mix_out[here] = d_mix
        tokens_t_out[:, here] = tokens[here].T
        turned_out[here] = dot_nn(first[...], tokens[here]).astype(bf16)
        skip_out[...] += jnp.sum(
            d_mix.astype(f32) * value.astype(f32), axis=0, keepdims=True
        )
        section = dot_nn(d_mix.T, fourth[...]).astype(bf16)
        out[:, r] = section.reshape(n, chans, N2)
    direct_out[...] += dot_nn(tokens_t_out[...], d_mix_out[...])

    @pl.when(pl.program_id(0) == pl.num_programs(0) - 1)
    def _():
        direct_out[...] = direct_out[...] * skip[...]


def turn_in(swap, arrived, by_channel):
    def body(i, _):
        rows = pl.ds(pl.multiple_of(i * GROUP, GROUP), GROUP)
        block = arrived[rows].reshape(GROUP * GROUP, N2)
        turned = dot_nn(swap[...], block).astype(bf16)
        by_channel[:, rows, :] = turned.reshape(GROUP, GROUP, N2)
        return 0

    lax.fori_loop(0, N1 // GROUP, body, 0, unroll=2)


def turn_out(swap, by_channel, out):
    def body(i, _):
        rows = pl.ds(pl.multiple_of(i * GROUP, GROUP), GROUP)
        block = by_channel[:, rows, :].reshape(GROUP * GROUP, N2)
        turned = dot_nn(swap[...], block).astype(bf16)
        out[rows] = turned.reshape(GROUP, GROUP, N2)
        return 0

    lax.fori_loop(0, N1 // GROUP, body, 0, unroll=2)


def home_forward_kernel(arrived, kernel, second, third, swap, out, spectrum_out, by_channel):
    turn_in(swap, arrived, by_channel)

    def body(c, _):
        spectrum = dot_nn(second[...], by_channel[c])
        spectrum_out[c] = spectrum
        filtered = (spectrum * kernel[c].astype(f32)).astype(bf16)
        by_channel[c] = dot_nn(third[...], filtered).astype(bf16)
        return 0

    lax.fori_loop(0, GROUP, body, 0, unroll=2)
    turn_out(swap, by_channel, out)


def home_backward_kernel(
    arrived, kernel, spectrum, second_t, third_t, swap, out, grad_kernel, by_channel
):
    turn_in(swap, arrived, by_channel)

    def body(c, _):
        d_freq = dot_nn(third_t[...], by_channel[c])
        grad_kernel[c] = (d_freq * spectrum[c]).astype(bf16)
        d_spec = (d_freq * kernel[c].astype(f32)).astype(bf16)
        by_channel[c] = dot_nn(second_t[...], d_spec).astype(bf16)
        return 0

    lax.fori_loop(0, GROUP, body, 0, unroll=2)
    turn_out(swap, by_channel, out)


def accumulate(total, term):
    @pl.when(pl.program_id(0) == 0)
    def _():
        total[...] = term

    @pl.when(pl.program_id(0) > 0)
    def _():
        total[...] += term


def finish(total, factor, grad_w):
    @pl.when(pl.program_id(0) == pl.num_programs(0) - 1)
    def _():
        grad_w[...] = (total[...] * factor[0, 0]).astype(bf16)


def gate_kernel(
    arrived,
    tokens_t,
    value,
    cotangent,
    d_mix,
    fourth,
    w_gate_t,
    w_value_t,
    skip,
    factor,
    partial,
    grad_w,
    total,
    d_gate,
):
    for r in range(arrived.shape[1]):
        here = row_slice(r)
        conv = dot_nt(fourth[...], arrived[:, r].reshape(D, N2))
        mixed = conv + skip[...] * value[here].astype(f32)
        d_gate[here] = (cotangent[here].astype(f32) * mixed).astype(bf16)
        direct = (skip[...] * d_mix[here].astype(f32)).astype(bf16)
        partial[here] = (
            dot_nn(d_gate[here], w_gate_t[...]) + dot_nn(direct, w_value_t[...])
        ).astype(bf16)
    accumulate(total, dot_nn(tokens_t[...], d_gate[...]))
    finish(total, factor, grad_w)


def value_kernel(
    per,
    arrived,
    turned,
    direct,
    factor,
    bit,
    _,
    kept,
    given,
    arrived_v,
    turned_v,
    direct_v,
    total,
    arrive,
):
    rows = arrived.shape[1]
    chunks = rows // per
    in_direct = pltpu.make_async_copy(direct, direct_v, arrive.at[chunks, 0])

    def copies(i):
        lines = pl.ds(i * per, per)
        here = pl.ds(i * per * N2, per * N2)
        return [
            pltpu.make_async_copy(
                arrived.at[:, lines], arrived_v.at[:, lines], arrive.at[i, 0]
            ),
            pltpu.make_async_copy(turned.at[here], turned_v.at[here], arrive.at[i, 1]),
        ]

    started = [copies(i) for i in range(chunks)]
    for group in started:
        for copy in group:
            copy.start()
    in_direct.start()
    for i in range(chunks):
        for copy in started[i]:
            copy.wait()
        side = jnp.concatenate(
            [arrived_v[:, r].reshape(D, N2) for r in range(i * per, (i + 1) * per)], axis=1
        )
        term = dot_nn(side, turned_v[i * per * N2 : (i + 1) * per * N2])
        if i == 0:
            total[...] = term
        else:
            total[...] += term
    in_direct.wait()
    size = kept.shape[1]
    total[...] = total[...].T
    for high in range(2):
        for part, low in ((kept, bit[0, 0]), (given, 1 - bit[0, 0])):
            place = pl.ds(pl.multiple_of((2 * high + low) * size, size), size)
            part[high] = ((total[place] + direct_v[place]) * factor[0, 0]).astype(bf16)


def tokens_kernel(arrived, partial, first_t, w_value_t, *rest):
    grad_tokens = rest[-1]
    for r in range(arrived.shape[1]):
        here = row_slice(r)
        d_cube = dot_nt(first_t[...], arrived[:, r].reshape(D, N2)).astype(bf16)
        grad_tokens[here] = (
            partial[here].astype(f32) + dot_nn(d_cube, w_value_t[...])
        ).astype(bf16)


def from_partner(array, b, n):
    return lax.ppermute(array, "seq", [(i, i ^ (1 << b)) for i in range(n)])


def halves(part, axis, b):
    bit = (lax.axis_index("seq") >> b) & 1
    kept = lax.dynamic_index_in_dim(part, bit, axis, keepdims=False)
    sent = lax.dynamic_index_in_dim(part, 1 - bit, axis, keepdims=False)
    return kept, sent


def added(kept, got):
    return (kept.astype(f32) + got.astype(f32)).astype(bf16)


def doubled(part, axis, b, n):
    bit = (lax.axis_index("seq") >> b) & 1
    mine = jnp.expand_dims(part, axis)
    other = jnp.expand_dims(from_partner(part, b, n), axis)
    around = jnp.concatenate([mine, other, mine], axis)
    return lax.dynamic_slice_in_dim(around, bit, 2, axis)


def on_device(
    tokens,
    w_value,
    w_gate,
    first_block,
    second_block,
    third_block,
    fourth_block,
    kernel,
    skip_gain,
    cotangent,
):
    n = lax.axis_size("seq")
    rows = N1 // n
    chans = D // n
    local_rows = tokens.shape[0]
    sections = (n, rows, chans, N2)
    factor = (1.0 / jnp.sqrt(jnp.asarray(N1 * N2, f32))).reshape(1, 1)
    skip = skip_gain.reshape(1, D)
    square = whole((D, D))
    block = whole((N1, N2))
    line = whole((1, D))
    per = min(4, rows)
    row = rows_of(per)
    column = pl.BlockSpec((D, per * N2), lambda i: (0, i))
    sent = by_device(n, per, chans)
    one = pl.BlockSpec(memory_space=pltpu.SMEM)
    place = jnp.arange(GROUP * GROUP)
    swap = (
        place[None, :] == ((place % GROUP) * GROUP + place // GROUP)[:, None]
    ).astype(bf16)

    def cost(gflop, mib):
        scale = rows / 16
        return pl.CostEstimate(
            flops=int(gflop * 1e9 * scale), bytes_accessed=int(mib * 2**20 * scale), transcendentals=0
        )

    def shape(dims, dtype=bf16):
        return jax.ShapeDtypeStruct(dims, dtype)

    def transfer(array):
        return lax.all_to_all(array, "seq", split_axis=0, concat_axis=0, tiled=True)

    unread = pl.BlockSpec(memory_space=pl.ANY)
    one_sent = pl.pallas_call(
        functools.partial(section_one_kernel, per),
        in_specs=[unread] * 3,
        out_specs=unread,
        out_shape=shape(sections),
        scratch_shapes=[
            pltpu.VMEM((local_rows, D), bf16),
            pltpu.VMEM((D, D), bf16),
            pltpu.VMEM((N2, N2), bf16),
            pltpu.VMEM(sections, bf16),
            pltpu.SemaphoreType.DMA((rows // per + 2,)),
            pltpu.SemaphoreType.DMA((rows // per,)),
        ],
        compiler_params=params(),
        cost_estimate=cost(3.2, 9),
    )(tokens, w_value, first_block)
    one_home = transfer(one_sent)

    three_sent, value, d_mix, tokens_t, turned, direct, skip_term, w_value_t, w_gate_t = pl.pallas_call(
        d_three_kernel,
        grid=(rows // per,),
        in_specs=[row, row, square, square, block, block, line],
        out_specs=[sent, row, row, column, row, square, line, square, square],
        out_shape=[
            shape(sections),
            shape((local_rows, D)),
            shape((local_rows, D)),
            shape((D, local_rows)),
            shape((local_rows, D)),
            shape((D, D), f32),
            shape((1, D), f32),
            shape((D, D)),
            shape((D, D)),
        ],
        compiler_params=params(),
        cost_estimate=cost(8.6, 30),
    )(tokens, cotangent, w_value, w_gate, first_block, fourth_block, skip)
    three_home = transfer(three_sent)

    at_home = pl.BlockSpec((N1, GROUP, N2), lambda i: (0, i, 0))
    filters = pl.BlockSpec((GROUP, N1, N2), lambda i: (i, 0, 0))
    three_back, spectrum = pl.pallas_call(
        home_forward_kernel,
        grid=(chans // GROUP,),
        in_specs=[at_home, filters, block, block, block],
        out_specs=[at_home, filters],
        out_shape=[shape((N1, chans, N2)), shape((chans, N1, N2), f32)],
        scratch_shapes=[pltpu.VMEM((GROUP, N1, N2), bf16)],
        compiler_params=params(),
        cost_estimate=cost(4.3, 20),
    )(one_home.reshape(N1, chans, N2), kernel, second_block, third_block, swap)
    three_here = transfer(three_back.reshape(sections))

    one_back, grad_kernel = pl.pallas_call(
        home_backward_kernel,
        grid=(chans // GROUP,),
        in_specs=[at_home, filters, filters, block, block, block],
        out_specs=[at_home, filters],
        out_shape=[shape((N1, chans, N2)), shape((chans, N1, N2))],
        scratch_shapes=[pltpu.VMEM((GROUP, N1, N2), bf16)],
        compiler_params=params(),
        cost_estimate=cost(4.3, 24),
    )(
        three_home.reshape(N1, chans, N2),
        kernel,
        spectrum,
        second_block.T,
        third_block.T,
        swap,
    )
    one_here = transfer(one_back.reshape(sections))

    partial, gate_term = pl.pallas_call(
        gate_kernel,
        grid=(rows // per,),
        in_specs=[sent, column, row, row, row, block, square, square, line, one],
        out_specs=[row, square],
        out_shape=[shape((local_rows, D)), shape((D, D))],
        scratch_shapes=[pltpu.VMEM((D, D), f32), pltpu.VMEM((per * N2, D), bf16)],
        compiler_params=params(),
        cost_estimate=cost(5.4, 25),
    )(
        three_here,
        tokens_t,
        value,
        cotangent,
        d_mix,
        fourth_block,
        w_gate_t,
        w_value_t,
        skip,
        factor,
    )

    skip_lanes = jnp.broadcast_to((skip_term * factor[0, 0]).astype(bf16).T, (D, LANES))
    gate_term = jnp.concatenate([gate_term, skip_lanes], axis=1)
    bits = n.bit_length() - 1
    gate_part = gate_term.reshape((2,) * bits + (D // n, D + LANES))
    for b in range(bits):
        kept, given = halves(gate_part, bits - 1 - b, b)
        gate_part = added(kept, from_partner(given, b, n))

    first_t = first_block.T
    in_vmem = pl.BlockSpec(memory_space=pltpu.VMEM)
    me = lax.axis_index("seq").reshape(1, 1)
    half = (2, D // 4, D)
    kept, given = pl.pallas_call(
        functools.partial(value_kernel, per),
        in_specs=[unread, unread, unread, one, one, unread],
        out_specs=[in_vmem, in_vmem],
        out_shape=[shape(half), shape(half)],
        scratch_shapes=[
            pltpu.VMEM(sections, bf16),
            pltpu.VMEM((local_rows, D), bf16),
            pltpu.VMEM((D, D), f32),
            pltpu.VMEM((D, D), f32),
            pltpu.SemaphoreType.DMA((rows // per + 1, 2)),
        ],
        compiler_params=params(),
        cost_estimate=cost(2.2, 9.5),
    )(one_here, turned, direct, factor, me & 1, gate_part)

    for b in reversed(range(bits)):
        gate_part = doubled(gate_part, bits - 1 - b, b, n)
    gate_total = gate_part.reshape(D, D + LANES)

    unit = rows // 8
    pieces = [1, 2, 3, 2]

    def piece(i, grad_tokens, after):
        first = sum(pieces[:i])
        lines = pl.BlockSpec((unit * N2, D), lambda g: (g + first, 0))
        held = [] if grad_tokens is None else [grad_tokens]
        return pl.pallas_call(
            tokens_kernel,
            grid=(pieces[i],),
            in_specs=[
                pl.BlockSpec((n, unit, chans, N2), lambda g: (0, g + first, 0, 0)),
                lines,
                block,
                square,
                unread,
            ]
            + [unread] * len(held),
            out_specs=lines,
            out_shape=shape((local_rows, D)),
            input_output_aliases={5: 0} if held else {},
            compiler_params=params(),
            cost_estimate=cost(0.4 * pieces[i], 1.5 * pieces[i]),
        )(one_here, partial, first_t, w_value_t, after, *held)

    grad_tokens = None
    for b in range(bits):
        if b == 1:
            kept, given = halves(value_part, 0, b)
        elif b > 1:
            kept, given = value_part, value_part
        got = from_partner(given, b, n)
        if b < len(pieces):
            grad_tokens = piece(b, grad_tokens, given)
        value_part = added(kept, got)
    for b in (1, 0):
        value_part = doubled(value_part, 1 - b, b, n)
    grad_weights = jnp.stack([value_part.reshape(D, D), gate_total[:, :D]]).astype(f32)
    return grad_tokens, grad_kernel, grad_weights, gate_total[:, D].astype(f32)


def solution(mesh):
    in_specs = (
        P(("parts", "seq"), None),
        P(),
        P(),
        P(),
        P(),
        P(),
        P(),
        P("seq", None, None),
        P(),
        P(("parts", "seq"), None),
    )
    out_specs = (
        P(("parts", "seq"), None),
        P(("parts", "seq"), None, None),
        P("parts", None, None),
        P("parts"),
    )
    return jax.shard_map(
        on_device, mesh=mesh, in_specs=in_specs, out_specs=out_specs, check_vma=False
    )
```

```python
import functools

import functools

import jax
import jax.numpy as jnp
from jax import lax
from jax.experimental import pallas as pl
from jax.experimental.pallas import tpu as pltpu
from jax.sharding import PartitionSpec as P

D = 512
N1 = 256
N2 = 256
GROUP = 16
LANES = 128
VMEM_LIMIT = 56 * 1024 * 1024

f32 = jnp.float32
bf16 = jnp.bfloat16


def dot_nn(a, b):
    return jnp.dot(a, b, preferred_element_type=f32)


def dot_nt(a, b):
    return lax.dot_general(a, b, (((1,), (1,)), ((), ())), preferred_element_type=f32)


def params():
    return pltpu.CompilerParams(vmem_limit_bytes=VMEM_LIMIT)


def whole(shape):
    return pl.BlockSpec(shape, lambda i: (0,) * len(shape))


def rows_of(per):
    return pl.BlockSpec((per * N2, D), lambda i: (i, 0))


def by_device(n, per, chans):
    return pl.BlockSpec((n, per, chans, N2), lambda i: (0, i, 0, 0))


def row_slice(r):
    return slice(r * N2, (r + 1) * N2)


def send_value_kernel(per, tokens, w_value, out, tokens_v, w_v, out_v, arrive, leave):
    rows = out.shape[1]
    n, _, chans, _ = out.shape
    chunks = rows // per
    in_w = pltpu.make_async_copy(w_value, w_v, arrive.at[chunks])
    in_tokens = [
        pltpu.make_async_copy(
            tokens.at[pl.ds(i * per * N2, per * N2)],
            tokens_v.at[pl.ds(i * per * N2, per * N2)],
            arrive.at[i],
        )
        for i in range(chunks)
    ]
    outs = [
        pltpu.make_async_copy(
            out_v.at[:, pl.ds(i * per, per)], out.at[:, pl.ds(i * per, per)], leave.at[i]
        )
        for i in range(chunks)
    ]
    in_w.start()
    for copy in in_tokens:
        copy.start()
    in_w.wait()
    for i in range(chunks):
        in_tokens[i].wait()
        value = dot_nn(tokens_v[i * per * N2 : (i + 1) * per * N2], w_v[...]).astype(bf16)
        for r in range(per):
            out_v[:, i * per + r] = value[row_slice(r)].T.reshape(n, chans, N2)
        outs[i].start()
    for copy in outs:
        copy.wait()


def d_three_kernel(
    tokens,
    cotangent,
    w_value,
    w_gate,
    first,
    fourth,
    skip,
    out,
    value_out,
    d_mix_out,
    tokens_t_out,
    turned_out,
    direct_out,
    skip_out,
    w_value_t,
    w_gate_t,
):
    n, per, chans, _ = out.shape

    @pl.when(pl.program_id(0) == 0)
    def _():
        skip_out[...] = jnp.zeros_like(skip_out)
        direct_out[...] = jnp.zeros_like(direct_out)
        w_value_t[...] = w_value[...].T
        w_gate_t[...] = w_gate[...].T

    for r in range(per):
        here = row_slice(r)
        value = dot_nn(tokens[here], w_value[...]).astype(bf16)
        gate = dot_nn(tokens[here], w_gate[...]).astype(bf16)
        d_mix = (cotangent[here].astype(f32) * gate.astype(f32)).astype(bf16)
        value_out[here] = value
        d_mix_out[here] = d_mix
        tokens_t_out[:, here] = tokens[here].T
        turned_out[here] = dot_nn(first[...], tokens[here]).astype(bf16)
        skip_out[...] += jnp.sum(
            d_mix.astype(f32) * value.astype(f32), axis=0, keepdims=True
        )
        section = dot_nn(d_mix.T, fourth[...]).astype(bf16)
        out[:, r] = section.reshape(n, chans, N2)
    direct_out[...] += dot_nn(tokens_t_out[...], d_mix_out[...])

    @pl.when(pl.program_id(0) == pl.num_programs(0) - 1)
    def _():
        direct_out[...] = direct_out[...] * skip[...]


def turn_in(swap, arrived, by_channel):
    def body(i, _):
        rows = pl.ds(pl.multiple_of(i * GROUP, GROUP), GROUP)
        block = arrived[rows].reshape(GROUP * GROUP, N2)
        turned = dot_nn(swap[...], block).astype(bf16)
        by_channel[:, rows, :] = turned.reshape(GROUP, GROUP, N2)
        return 0

    lax.fori_loop(0, N1 // GROUP, body, 0, unroll=2)


def turn_out(swap, by_channel, out):
    def body(i, _):
        rows = pl.ds(pl.multiple_of(i * GROUP, GROUP), GROUP)
        block = by_channel[:, rows, :].reshape(GROUP * GROUP, N2)
        turned = dot_nn(swap[...], block).astype(bf16)
        out[rows] = turned.reshape(GROUP, GROUP, N2)
        return 0

    lax.fori_loop(0, N1 // GROUP, body, 0, unroll=2)


def home_forward_kernel(
    arrived, kernel, first_t, second, third, swap, out, spectrum_out, by_channel
):
    turn_in(swap, arrived, by_channel)

    def body(c, _):
        section = dot_nn(by_channel[c], first_t[...]).astype(bf16)
        spectrum = dot_nn(second[...], section)
        spectrum_out[c] = spectrum
        filtered = (spectrum * kernel[c].astype(f32)).astype(bf16)
        by_channel[c] = dot_nn(third[...], filtered).astype(bf16)
        return 0

    lax.fori_loop(0, GROUP, body, 0, unroll=2)
    turn_out(swap, by_channel, out)


def home_backward_kernel(
    arrived, kernel, spectrum, second_t, third_t, swap, out, grad_kernel, by_channel
):
    turn_in(swap, arrived, by_channel)

    def body(c, _):
        d_freq = dot_nn(third_t[...], by_channel[c])
        grad_kernel[c] = (d_freq * spectrum[c]).astype(bf16)
        d_spec = (d_freq * kernel[c].astype(f32)).astype(bf16)
        by_channel[c] = dot_nn(second_t[...], d_spec).astype(bf16)
        return 0

    lax.fori_loop(0, GROUP, body, 0, unroll=2)
    turn_out(swap, by_channel, out)


def accumulate(total, term):
    @pl.when(pl.program_id(0) == 0)
    def _():
        total[...] = term

    @pl.when(pl.program_id(0) > 0)
    def _():
        total[...] += term


def finish(total, factor, grad_w):
    @pl.when(pl.program_id(0) == pl.num_programs(0) - 1)
    def _():
        grad_w[...] = (total[...] * factor[0, 0]).astype(bf16)


def gate_kernel(
    arrived,
    tokens_t,
    value,
    cotangent,
    d_mix,
    fourth,
    w_gate_t,
    w_value_t,
    skip,
    factor,
    partial,
    grad_w,
    total,
    d_gate,
):
    for r in range(arrived.shape[1]):
        here = row_slice(r)
        conv = dot_nt(fourth[...], arrived[:, r].reshape(D, N2))
        mixed = conv + skip[...] * value[here].astype(f32)
        d_gate[here] = (cotangent[here].astype(f32) * mixed).astype(bf16)
        direct = (skip[...] * d_mix[here].astype(f32)).astype(bf16)
        partial[here] = (
            dot_nn(d_gate[here], w_gate_t[...]) + dot_nn(direct, w_value_t[...])
        ).astype(bf16)
    accumulate(total, dot_nn(tokens_t[...], d_gate[...]))
    finish(total, factor, grad_w)


def value_kernel(
    per,
    arrived,
    turned,
    direct,
    factor,
    bit,
    _,
    kept,
    given,
    arrived_v,
    turned_v,
    direct_v,
    total,
    arrive,
):
    rows = arrived.shape[1]
    chunks = rows // per
    in_direct = pltpu.make_async_copy(direct, direct_v, arrive.at[chunks, 0])

    def copies(i):
        lines = pl.ds(i * per, per)
        here = pl.ds(i * per * N2, per * N2)
        return [
            pltpu.make_async_copy(
                arrived.at[:, lines], arrived_v.at[:, lines], arrive.at[i, 0]
            ),
            pltpu.make_async_copy(turned.at[here], turned_v.at[here], arrive.at[i, 1]),
        ]

    started = [copies(i) for i in range(chunks)]
    for group in started:
        for copy in group:
            copy.start()
    in_direct.start()
    for i in range(chunks):
        for copy in started[i]:
            copy.wait()
        side = jnp.concatenate(
            [arrived_v[:, r].reshape(D, N2) for r in range(i * per, (i + 1) * per)], axis=1
        )
        term = dot_nn(side, turned_v[i * per * N2 : (i + 1) * per * N2])
        if i == 0:
            total[...] = term
        else:
            total[...] += term
    in_direct.wait()
    size = kept.shape[1]
    total[...] = total[...].T
    for high in range(2):
        for part, low in ((kept, bit[0, 0]), (given, 1 - bit[0, 0])):
            place = pl.ds(pl.multiple_of((2 * high + low) * size, size), size)
            part[high] = ((total[place] + direct_v[place]) * factor[0, 0]).astype(bf16)


def tokens_kernel(arrived, partial, first_t, w_value_t, *rest):
    grad_tokens = rest[-1]
    for r in range(arrived.shape[1]):
        here = row_slice(r)
        d_cube = dot_nt(first_t[...], arrived[:, r].reshape(D, N2)).astype(bf16)
        grad_tokens[here] = (
            partial[here].astype(f32) + dot_nn(d_cube, w_value_t[...])
        ).astype(bf16)


def from_partner(array, b, n):
    return lax.ppermute(array, "seq", [(i, i ^ (1 << b)) for i in range(n)])


def halves(part, axis, b):
    bit = (lax.axis_index("seq") >> b) & 1
    kept = lax.dynamic_index_in_dim(part, bit, axis, keepdims=False)
    sent = lax.dynamic_index_in_dim(part, 1 - bit, axis, keepdims=False)
    return kept, sent


def added(kept, got):
    return (kept.astype(f32) + got.astype(f32)).astype(bf16)


def doubled(part, axis, b, n):
    bit = (lax.axis_index("seq") >> b) & 1
    mine = jnp.expand_dims(part, axis)
    other = jnp.expand_dims(from_partner(part, b, n), axis)
    around = jnp.concatenate([mine, other, mine], axis)
    return lax.dynamic_slice_in_dim(around, bit, 2, axis)


def on_device(
    tokens,
    w_value,
    w_gate,
    first_block,
    second_block,
    third_block,
    fourth_block,
    kernel,
    skip_gain,
    cotangent,
):
    n = lax.axis_size("seq")
    rows = N1 // n
    chans = D // n
    local_rows = tokens.shape[0]
    sections = (n, rows, chans, N2)
    factor = (1.0 / jnp.sqrt(jnp.asarray(N1 * N2, f32))).reshape(1, 1)
    skip = skip_gain.reshape(1, D)
    square = whole((D, D))
    block = whole((N1, N2))
    line = whole((1, D))
    per = min(4, rows)
    row = rows_of(per)
    column = pl.BlockSpec((D, per * N2), lambda i: (0, i))
    sent = by_device(n, per, chans)
    one = pl.BlockSpec(memory_space=pltpu.SMEM)
    place = jnp.arange(GROUP * GROUP)
    swap = (
        place[None, :] == ((place % GROUP) * GROUP + place // GROUP)[:, None]
    ).astype(bf16)

    def cost(gflop, mib):
        scale = rows / 16
        return pl.CostEstimate(
            flops=int(gflop * 1e9 * scale), bytes_accessed=int(mib * 2**20 * scale), transcendentals=0
        )

    def shape(dims, dtype=bf16):
        return jax.ShapeDtypeStruct(dims, dtype)

    def transfer(array):
        return lax.all_to_all(array, "seq", split_axis=0, concat_axis=0, tiled=True)

    unread = pl.BlockSpec(memory_space=pl.ANY)
    one_sent = pl.pallas_call(
        functools.partial(send_value_kernel, per),
        in_specs=[unread] * 2,
        out_specs=unread,
        out_shape=shape(sections),
        scratch_shapes=[
            pltpu.VMEM((local_rows, D), bf16),
            pltpu.VMEM((D, D), bf16),
            pltpu.VMEM(sections, bf16),
            pltpu.SemaphoreType.DMA((rows // per + 1,)),
            pltpu.SemaphoreType.DMA((rows // per,)),
        ],
        compiler_params=params(),
        cost_estimate=cost(2.1, 9),
    )(tokens, w_value)
    one_home = transfer(one_sent)

    three_sent, value, d_mix, tokens_t, turned, direct, skip_term, w_value_t, w_gate_t = pl.pallas_call(
        d_three_kernel,
        grid=(rows // per,),
        in_specs=[row, row, square, square, block, block, line],
        out_specs=[sent, row, row, column, row, square, line, square, square],
        out_shape=[
            shape(sections),
            shape((local_rows, D)),
            shape((local_rows, D)),
            shape((D, local_rows)),
            shape((local_rows, D)),
            shape((D, D), f32),
            shape((1, D), f32),
            shape((D, D)),
            shape((D, D)),
        ],
        compiler_params=params(),
        cost_estimate=cost(8.6, 30),
    )(tokens, cotangent, w_value, w_gate, first_block, fourth_block, skip)
    three_home = transfer(three_sent)

    first_t = first_block.T
    at_home = pl.BlockSpec((N1, GROUP, N2), lambda i: (0, i, 0))
    filters = pl.BlockSpec((GROUP, N1, N2), lambda i: (i, 0, 0))
    three_back, spectrum = pl.pallas_call(
        home_forward_kernel,
        grid=(chans // GROUP,),
        in_specs=[at_home, filters, block, block, block, block],
        out_specs=[at_home, filters],
        out_shape=[shape((N1, chans, N2)), shape((chans, N1, N2), f32)],
        scratch_shapes=[pltpu.VMEM((GROUP, N1, N2), bf16)],
        compiler_params=params(),
        cost_estimate=cost(5.4, 20),
    )(
        one_home.reshape(N1, chans, N2),
        kernel,
        first_t,
        second_block,
        third_block,
        swap,
    )
    three_here = transfer(three_back.reshape(sections))

    one_back, grad_kernel = pl.pallas_call(
        home_backward_kernel,
        grid=(chans // GROUP,),
        in_specs=[at_home, filters, filters, block, block, block],
        out_specs=[at_home, filters],
        out_shape=[shape((N1, chans, N2)), shape((chans, N1, N2))],
        scratch_shapes=[pltpu.VMEM((GROUP, N1, N2), bf16)],
        compiler_params=params(),
        cost_estimate=cost(4.3, 24),
    )(
        three_home.reshape(N1, chans, N2),
        kernel,
        spectrum,
        second_block.T,
        third_block.T,
        swap,
    )
    one_here = transfer(one_back.reshape(sections))

    partial, gate_term = pl.pallas_call(
        gate_kernel,
        grid=(rows // per,),
        in_specs=[sent, column, row, row, row, block, square, square, line, one],
        out_specs=[row, square],
        out_shape=[shape((local_rows, D)), shape((D, D))],
        scratch_shapes=[pltpu.VMEM((D, D), f32), pltpu.VMEM((per * N2, D), bf16)],
        compiler_params=params(),
        cost_estimate=cost(5.4, 25),
    )(
        three_here,
        tokens_t,
        value,
        cotangent,
        d_mix,
        fourth_block,
        w_gate_t,
        w_value_t,
        skip,
        factor,
    )

    skip_lanes = jnp.broadcast_to((skip_term * factor[0, 0]).astype(bf16).T, (D, LANES))
    gate_term = jnp.concatenate([gate_term, skip_lanes], axis=1)
    bits = n.bit_length() - 1
    gate_part = gate_term.reshape((2,) * bits + (D // n, D + LANES))
    for b in range(bits):
        kept, given = halves(gate_part, bits - 1 - b, b)
        gate_part = added(kept, from_partner(given, b, n))

    in_vmem = pl.BlockSpec(memory_space=pltpu.VMEM)
    me = lax.axis_index("seq").reshape(1, 1)
    half = (2, D // 4, D)
    kept, given = pl.pallas_call(
        functools.partial(value_kernel, per),
        in_specs=[unread, unread, unread, one, one, unread],
        out_specs=[in_vmem, in_vmem],
        out_shape=[shape(half), shape(half)],
        scratch_shapes=[
            pltpu.VMEM(sections, bf16),
            pltpu.VMEM((local_rows, D), bf16),
            pltpu.VMEM((D, D), f32),
            pltpu.VMEM((D, D), f32),
            pltpu.SemaphoreType.DMA((rows // per + 1, 2)),
        ],
        compiler_params=params(),
        cost_estimate=cost(2.2, 9.5),
    )(one_here, turned, direct, factor, me & 1, gate_part)

    for b in reversed(range(bits)):
        gate_part = doubled(gate_part, bits - 1 - b, b, n)
    gate_total = gate_part.reshape(D, D + LANES)

    unit = rows // 8
    pieces = [3, 3, 2]

    def piece(i, grad_tokens, after):
        first = sum(pieces[:i])
        lines = pl.BlockSpec((unit * N2, D), lambda g: (g + first, 0))
        held = [] if grad_tokens is None else [grad_tokens]
        return pl.pallas_call(
            tokens_kernel,
            grid=(pieces[i],),
            in_specs=[
                pl.BlockSpec((n, unit, chans, N2), lambda g: (0, g + first, 0, 0)),
                lines,
                block,
                square,
                unread,
            ]
            + [unread] * len(held),
            out_specs=lines,
            out_shape=shape((local_rows, D)),
            input_output_aliases={5: 0} if held else {},
            compiler_params=params(),
            cost_estimate=cost(0.4 * pieces[i], 1.5 * pieces[i]),
        )(one_here, partial, first_t, w_value_t, after, *held)

    grad_tokens = None
    for b in range(bits):
        if b == 1:
            kept, given = halves(value_part, 0, b)
        elif b > 1:
            kept, given = value_part, value_part
        got = from_partner(given, b, n)
        if 0 < b <= len(pieces):
            grad_tokens = piece(b - 1, grad_tokens, given)
        value_part = added(kept, got)
    for b in (1, 0):
        value_part = doubled(value_part, 1 - b, b, n)
    grad_weights = jnp.stack([value_part.reshape(D, D), gate_total[:, :D]]).astype(f32)
    return grad_tokens, grad_kernel, grad_weights, gate_total[:, D].astype(f32)


def solution(mesh):
    in_specs = (
        P(("parts", "seq"), None),
        P(),
        P(),
        P(),
        P(),
        P(),
        P(),
        P("seq", None, None),
        P(),
        P(("parts", "seq"), None),
    )
    out_specs = (
        P(("parts", "seq"), None),
        P(("parts", "seq"), None, None),
        P("parts", None, None),
        P("parts"),
    )
    return jax.shard_map(
        on_device, mesh=mesh, in_specs=in_specs, out_specs=out_specs, check_vma=False
    )
```

```python
import functools

import functools

import jax
import jax.numpy as jnp
from jax import lax
from jax.experimental import pallas as pl
from jax.experimental.pallas import tpu as pltpu
from jax.sharding import PartitionSpec as P

D = 512
N1 = 256
N2 = 256
GROUP = 16
LANES = 128
VMEM_LIMIT = 56 * 1024 * 1024

f32 = jnp.float32
bf16 = jnp.bfloat16


def dot_nn(a, b):
    return jnp.dot(a, b, preferred_element_type=f32)


def dot_nt(a, b):
    return lax.dot_general(a, b, (((1,), (1,)), ((), ())), preferred_element_type=f32)


def params():
    return pltpu.CompilerParams(vmem_limit_bytes=VMEM_LIMIT)


def whole(shape):
    return pl.BlockSpec(shape, lambda i: (0,) * len(shape))


def rows_of(per):
    return pl.BlockSpec((per * N2, D), lambda i: (i, 0))


def by_device(n, per, chans):
    return pl.BlockSpec((n, per, chans, N2), lambda i: (0, i, 0, 0))


def row_slice(r):
    return slice(r * N2, (r + 1) * N2)


def send_value_kernel(per, tokens, w_value, out, tokens_v, w_v, out_v, arrive, leave):
    rows = out.shape[1]
    n, _, chans, _ = out.shape
    chunks = rows // per
    in_w = pltpu.make_async_copy(w_value, w_v, arrive.at[chunks])
    in_tokens = [
        pltpu.make_async_copy(
            tokens.at[pl.ds(i * per * N2, per * N2)],
            tokens_v.at[pl.ds(i * per * N2, per * N2)],
            arrive.at[i],
        )
        for i in range(chunks)
    ]
    outs = [
        pltpu.make_async_copy(
            out_v.at[:, pl.ds(i * per, per)], out.at[:, pl.ds(i * per, per)], leave.at[i]
        )
        for i in range(chunks)
    ]
    in_w.start()
    for copy in in_tokens:
        copy.start()
    in_w.wait()
    for i in range(chunks):
        in_tokens[i].wait()
        value = dot_nn(tokens_v[i * per * N2 : (i + 1) * per * N2], w_v[...]).astype(bf16)
        for r in range(per):
            out_v[:, i * per + r] = value[row_slice(r)].T.reshape(n, chans, N2)
        outs[i].start()
    for copy in outs:
        copy.wait()


def d_three_kernel(
    tokens,
    cotangent,
    w_value,
    w_gate,
    first,
    fourth,
    skip,
    out,
    value_out,
    d_mix_out,
    tokens_t_out,
    turned_out,
    direct_out,
    skip_out,
    w_value_t,
    w_gate_t,
):
    n, per, chans, _ = out.shape

    @pl.when(pl.program_id(0) == 0)
    def _():
        skip_out[...] = jnp.zeros_like(skip_out)
        direct_out[...] = jnp.zeros_like(direct_out)
        w_value_t[...] = w_value[...].T
        w_gate_t[...] = w_gate[...].T

    for r in range(per):
        here = row_slice(r)
        value = dot_nn(tokens[here], w_value[...]).astype(bf16)
        gate = dot_nn(tokens[here], w_gate[...]).astype(bf16)
        d_mix = (cotangent[here].astype(f32) * gate.astype(f32)).astype(bf16)
        value_out[here] = value
        d_mix_out[here] = d_mix
        tokens_t_out[:, here] = tokens[here].T
        turned_out[here] = dot_nn(first[...], tokens[here]).astype(bf16)
        skip_out[...] += jnp.sum(
            d_mix.astype(f32) * value.astype(f32), axis=0, keepdims=True
        )
        section = dot_nn(d_mix.T, fourth[...]).astype(bf16)
        out[:, r] = section.reshape(n, chans, N2)
    direct_out[...] += dot_nn(tokens_t_out[...], d_mix_out[...])

    @pl.when(pl.program_id(0) == pl.num_programs(0) - 1)
    def _():
        direct_out[...] = direct_out[...] * skip[...]


def turn_in(swap, arrived, by_channel):
    def body(i, _):
        rows = pl.ds(pl.multiple_of(i * GROUP, GROUP), GROUP)
        block = arrived[rows].reshape(GROUP * GROUP, N2)
        turned = dot_nn(swap[...], block).astype(bf16)
        by_channel[:, rows, :] = turned.reshape(GROUP, GROUP, N2)
        return 0

    lax.fori_loop(0, N1 // GROUP, body, 0, unroll=2)


def turn_out(swap, by_channel, out):
    def body(i, _):
        rows = pl.ds(pl.multiple_of(i * GROUP, GROUP), GROUP)
        block = by_channel[:, rows, :].reshape(GROUP * GROUP, N2)
        turned = dot_nn(swap[...], block).astype(bf16)
        out[rows] = turned.reshape(GROUP, GROUP, N2)
        return 0

    lax.fori_loop(0, N1 // GROUP, body, 0, unroll=2)


def home_forward_kernel(
    arrived, kernel, first_t, second, third, swap, out, spectrum_out, by_channel
):
    turn_in(swap, arrived, by_channel)

    def body(c, _):
        section = dot_nn(by_channel[c], first_t[...]).astype(bf16)
        spectrum = dot_nn(second[...], section)
        spectrum_out[c] = spectrum
        filtered = (spectrum * kernel[c].astype(f32)).astype(bf16)
        by_channel[c] = dot_nn(third[...], filtered).astype(bf16)
        return 0

    lax.fori_loop(0, GROUP, body, 0, unroll=2)
    turn_out(swap, by_channel, out)


def home_backward_kernel(
    arrived, kernel, spectrum, second_t, third_t, swap, out, grad_kernel, by_channel
):
    turn_in(swap, arrived, by_channel)

    def body(c, _):
        d_freq = dot_nn(third_t[...], by_channel[c])
        grad_kernel[c] = (d_freq * spectrum[c]).astype(bf16)
        d_spec = (d_freq * kernel[c].astype(f32)).astype(bf16)
        by_channel[c] = dot_nn(second_t[...], d_spec).astype(bf16)
        return 0

    lax.fori_loop(0, GROUP, body, 0, unroll=2)
    turn_out(swap, by_channel, out)


def accumulate(total, term):
    @pl.when(pl.program_id(0) == 0)
    def _():
        total[...] = term

    @pl.when(pl.program_id(0) > 0)
    def _():
        total[...] += term


def finish(total, factor, grad_w):
    @pl.when(pl.program_id(0) == pl.num_programs(0) - 1)
    def _():
        grad_w[...] = (total[...] * factor[0, 0]).astype(bf16)


def gate_kernel(
    arrived,
    tokens_t,
    value,
    cotangent,
    d_mix,
    fourth,
    w_gate_t,
    w_value_t,
    skip,
    factor,
    partial,
    grad_w,
    total,
    d_gate,
):
    for r in range(arrived.shape[1]):
        here = row_slice(r)
        conv = dot_nt(fourth[...], arrived[:, r].reshape(D, N2))
        mixed = conv + skip[...] * value[here].astype(f32)
        d_gate[here] = (cotangent[here].astype(f32) * mixed).astype(bf16)
        direct = (skip[...] * d_mix[here].astype(f32)).astype(bf16)
        partial[here] = (
            dot_nn(d_gate[here], w_gate_t[...]) + dot_nn(direct, w_value_t[...])
        ).astype(bf16)
    accumulate(total, dot_nn(tokens_t[...], d_gate[...]))
    finish(total, factor, grad_w)


def value_kernel(
    per,
    arrived,
    turned,
    direct,
    factor,
    bit,
    _,
    kept,
    given,
    arrived_v,
    turned_v,
    direct_v,
    total,
    arrive,
):
    rows = arrived.shape[1]
    chunks = rows // per
    in_direct = pltpu.make_async_copy(direct, direct_v, arrive.at[chunks, 0])

    def copies(i):
        lines = pl.ds(i * per, per)
        here = pl.ds(i * per * N2, per * N2)
        return [
            pltpu.make_async_copy(
                arrived.at[:, lines], arrived_v.at[:, lines], arrive.at[i, 0]
            ),
            pltpu.make_async_copy(turned.at[here], turned_v.at[here], arrive.at[i, 1]),
        ]

    started = [copies(i) for i in range(chunks)]
    for group in started:
        for copy in group:
            copy.start()
    in_direct.start()
    for i in range(chunks):
        for copy in started[i]:
            copy.wait()
        side = jnp.concatenate(
            [arrived_v[:, r].reshape(D, N2) for r in range(i * per, (i + 1) * per)], axis=1
        )
        term = dot_nn(side, turned_v[i * per * N2 : (i + 1) * per * N2])
        if i == 0:
            total[...] = term
        else:
            total[...] += term
    in_direct.wait()
    size = kept.shape[1]
    total[...] = total[...].T
    for high in range(2):
        for part, low in ((kept, bit[0, 0]), (given, 1 - bit[0, 0])):
            place = pl.ds(pl.multiple_of((2 * high + low) * size, size), size)
            part[high] = ((total[place] + direct_v[place]) * factor[0, 0]).astype(bf16)


def tokens_kernel(arrived, partial, first_t, w_value_t, *rest):
    grad_tokens = rest[-1]
    for r in range(arrived.shape[1]):
        here = row_slice(r)
        d_cube = dot_nt(first_t[...], arrived[:, r].reshape(D, N2)).astype(bf16)
        grad_tokens[here] = (
            partial[here].astype(f32) + dot_nn(d_cube, w_value_t[...])
        ).astype(bf16)


def from_partner(array, b, n):
    return lax.ppermute(array, "seq", [(i, i ^ (1 << b)) for i in range(n)])


def halves(part, axis, b):
    bit = (lax.axis_index("seq") >> b) & 1
    kept = lax.dynamic_index_in_dim(part, bit, axis, keepdims=False)
    sent = lax.dynamic_index_in_dim(part, 1 - bit, axis, keepdims=False)
    return kept, sent


def added(kept, got):
    return (kept.astype(f32) + got.astype(f32)).astype(bf16)


def doubled(part, axis, b, n):
    bit = (lax.axis_index("seq") >> b) & 1
    mine = jnp.expand_dims(part, axis)
    other = jnp.expand_dims(from_partner(part, b, n), axis)
    around = jnp.concatenate([mine, other, mine], axis)
    return lax.dynamic_slice_in_dim(around, bit, 2, axis)


def on_device(
    tokens,
    w_value,
    w_gate,
    first_block,
    second_block,
    third_block,
    fourth_block,
    kernel,
    skip_gain,
    cotangent,
):
    n = lax.axis_size("seq")
    rows = N1 // n
    chans = D // n
    local_rows = tokens.shape[0]
    sections = (n, rows, chans, N2)
    factor = (1.0 / jnp.sqrt(jnp.asarray(N1 * N2, f32))).reshape(1, 1)
    skip = skip_gain.reshape(1, D)
    square = whole((D, D))
    block = whole((N1, N2))
    line = whole((1, D))
    per = min(4, rows)
    row = rows_of(per)
    column = pl.BlockSpec((D, per * N2), lambda i: (0, i))
    sent = by_device(n, per, chans)
    one = pl.BlockSpec(memory_space=pltpu.SMEM)
    place = jnp.arange(GROUP * GROUP)
    swap = (
        place[None, :] == ((place % GROUP) * GROUP + place // GROUP)[:, None]
    ).astype(bf16)

    def cost(gflop, mib):
        scale = rows / 16
        return pl.CostEstimate(
            flops=int(gflop * 1e9 * scale), bytes_accessed=int(mib * 2**20 * scale), transcendentals=0
        )

    def shape(dims, dtype=bf16):
        return jax.ShapeDtypeStruct(dims, dtype)

    def transfer(array):
        return lax.all_to_all(array, "seq", split_axis=0, concat_axis=0, tiled=True)

    unread = pl.BlockSpec(memory_space=pl.ANY)
    one_sent = pl.pallas_call(
        functools.partial(send_value_kernel, min(2, rows)),
        in_specs=[unread] * 2,
        out_specs=unread,
        out_shape=shape(sections),
        scratch_shapes=[
            pltpu.VMEM((local_rows, D), bf16),
            pltpu.VMEM((D, D), bf16),
            pltpu.VMEM(sections, bf16),
            pltpu.SemaphoreType.DMA((rows // min(2, rows) + 1,)),
            pltpu.SemaphoreType.DMA((rows // min(2, rows),)),
        ],
        compiler_params=params(),
        cost_estimate=cost(2.1, 9),
    )(tokens, w_value)
    one_home = transfer(one_sent)

    three_sent, value, d_mix, tokens_t, turned, direct, skip_term, w_value_t, w_gate_t = pl.pallas_call(
        d_three_kernel,
        grid=(rows // per,),
        in_specs=[row, row, square, square, block, block, line],
        out_specs=[sent, row, row, column, row, square, line, square, square],
        out_shape=[
            shape(sections),
            shape((local_rows, D)),
            shape((local_rows, D)),
            shape((D, local_rows)),
            shape((local_rows, D)),
            shape((D, D), f32),
            shape((1, D), f32),
            shape((D, D)),
            shape((D, D)),
        ],
        compiler_params=params(),
        cost_estimate=cost(8.6, 30),
    )(tokens, cotangent, w_value, w_gate, first_block, fourth_block, skip)
    three_home = transfer(three_sent)

    first_t = first_block.T
    at_home = pl.BlockSpec((N1, GROUP, N2), lambda i: (0, i, 0))
    filters = pl.BlockSpec((GROUP, N1, N2), lambda i: (i, 0, 0))
    three_back, spectrum = pl.pallas_call(
        home_forward_kernel,
        grid=(chans // GROUP,),
        in_specs=[at_home, filters, block, block, block, block],
        out_specs=[at_home, filters],
        out_shape=[shape((N1, chans, N2)), shape((chans, N1, N2), f32)],
        scratch_shapes=[pltpu.VMEM((GROUP, N1, N2), bf16)],
        compiler_params=params(),
        cost_estimate=cost(5.4, 20),
    )(
        one_home.reshape(N1, chans, N2),
        kernel,
        first_t,
        second_block,
        third_block,
        swap,
    )
    three_here = transfer(three_back.reshape(sections))

    one_back, grad_kernel = pl.pallas_call(
        home_backward_kernel,
        grid=(chans // GROUP,),
        in_specs=[at_home, filters, filters, block, block, block],
        out_specs=[at_home, filters],
        out_shape=[shape((N1, chans, N2)), shape((chans, N1, N2))],
        scratch_shapes=[pltpu.VMEM((GROUP, N1, N2), bf16)],
        compiler_params=params(),
        cost_estimate=cost(4.3, 24),
    )(
        three_home.reshape(N1, chans, N2),
        kernel,
        spectrum,
        second_block.T,
        third_block.T,
        swap,
    )
    one_here = transfer(one_back.reshape(sections))

    partial, gate_term = pl.pallas_call(
        gate_kernel,
        grid=(rows // per,),
        in_specs=[sent, column, row, row, row, block, square, square, line, one],
        out_specs=[row, square],
        out_shape=[shape((local_rows, D)), shape((D, D))],
        scratch_shapes=[pltpu.VMEM((D, D), f32), pltpu.VMEM((per * N2, D), bf16)],
        compiler_params=params(),
        cost_estimate=cost(5.4, 25),
    )(
        three_here,
        tokens_t,
        value,
        cotangent,
        d_mix,
        fourth_block,
        w_gate_t,
        w_value_t,
        skip,
        factor,
    )

    skip_lanes = jnp.broadcast_to((skip_term * factor[0, 0]).astype(bf16).T, (D, LANES))
    gate_term = jnp.concatenate([gate_term, skip_lanes], axis=1)
    bits = n.bit_length() - 1
    gate_part = gate_term.reshape((2,) * bits + (D // n, D + LANES))
    for b in range(bits):
        kept, given = halves(gate_part, bits - 1 - b, b)
        gate_part = added(kept, from_partner(given, b, n))

    in_vmem = pl.BlockSpec(memory_space=pltpu.VMEM)
    me = lax.axis_index("seq").reshape(1, 1)
    half = (2, D // 4, D)
    kept, given = pl.pallas_call(
        functools.partial(value_kernel, per),
        in_specs=[unread, unread, unread, one, one, unread],
        out_specs=[in_vmem, in_vmem],
        out_shape=[shape(half), shape(half)],
        scratch_shapes=[
            pltpu.VMEM(sections, bf16),
            pltpu.VMEM((local_rows, D), bf16),
            pltpu.VMEM((D, D), f32),
            pltpu.VMEM((D, D), f32),
            pltpu.SemaphoreType.DMA((rows // per + 1, 2)),
        ],
        compiler_params=params(),
        cost_estimate=cost(2.2, 9.5),
    )(one_here, turned, direct, factor, me & 1, gate_part)

    for b in reversed(range(bits)):
        gate_part = doubled(gate_part, bits - 1 - b, b, n)
    gate_total = gate_part.reshape(D, D + LANES)

    unit = rows // 8
    pieces = [2, 2, 2, 2]

    def piece(i, grad_tokens, after):
        first = sum(pieces[:i])
        lines = pl.BlockSpec((unit * N2, D), lambda g: (g + first, 0))
        held = [] if grad_tokens is None else [grad_tokens]
        return pl.pallas_call(
            tokens_kernel,
            grid=(pieces[i],),
            in_specs=[
                pl.BlockSpec((n, unit, chans, N2), lambda g: (0, g + first, 0, 0)),
                lines,
                block,
                square,
                unread,
            ]
            + [unread] * len(held),
            out_specs=lines,
            out_shape=shape((local_rows, D)),
            input_output_aliases={5: 0} if held else {},
            compiler_params=params(),
            cost_estimate=cost(0.4 * pieces[i], 1.5 * pieces[i]),
        )(one_here, partial, first_t, w_value_t, after, *held)

    grad_tokens = None
    for b in range(bits):
        if b == 1:
            kept, given = halves(value_part, 0, b)
        elif b > 1:
            kept, given = value_part, value_part
        got = from_partner(given, b, n)
        if b < len(pieces):
            grad_tokens = piece(b, grad_tokens, given)
        value_part = added(kept, got)
    for b in (1, 0):
        value_part = doubled(value_part, 1 - b, b, n)
    grad_weights = jnp.stack([value_part.reshape(D, D), gate_total[:, :D]]).astype(f32)
    return grad_tokens, grad_kernel, grad_weights, gate_total[:, D].astype(f32)


def solution(mesh):
    in_specs = (
        P(("parts", "seq"), None),
        P(),
        P(),
        P(),
        P(),
        P(),
        P(),
        P("seq", None, None),
        P(),
        P(("parts", "seq"), None),
    )
    out_specs = (
        P(("parts", "seq"), None),
        P(("parts", "seq"), None, None),
        P("parts", None, None),
        P("parts"),
    )
    return jax.shard_map(
        on_device, mesh=mesh, in_specs=in_specs, out_specs=out_specs, check_vma=False
    )
```

```python
import functools

import functools

import jax
import jax.numpy as jnp
from jax import lax
from jax.experimental import pallas as pl
from jax.experimental.pallas import tpu as pltpu
from jax.sharding import PartitionSpec as P

D = 512
N1 = 256
N2 = 256
GROUP = 16
LANES = 128
VMEM_LIMIT = 56 * 1024 * 1024

f32 = jnp.float32
bf16 = jnp.bfloat16


def dot_nn(a, b):
    return jnp.dot(a, b, preferred_element_type=f32)


def dot_nt(a, b):
    return lax.dot_general(a, b, (((1,), (1,)), ((), ())), preferred_element_type=f32)


def params():
    return pltpu.CompilerParams(vmem_limit_bytes=VMEM_LIMIT)


def whole(shape):
    return pl.BlockSpec(shape, lambda i: (0,) * len(shape))


def rows_of(per):
    return pl.BlockSpec((per * N2, D), lambda i: (i, 0))


def by_device(n, per, chans):
    return pl.BlockSpec((n, per, chans, N2), lambda i: (0, i, 0, 0))


def row_slice(r):
    return slice(r * N2, (r + 1) * N2)


def send_value_kernel(per, tokens, w_value, out, tokens_v, w_v, out_v, arrive, leave):
    rows = out.shape[1]
    n, _, chans, _ = out.shape
    chunks = rows // per
    in_w = pltpu.make_async_copy(w_value, w_v, arrive.at[chunks])
    in_tokens = [
        pltpu.make_async_copy(
            tokens.at[pl.ds(i * per * N2, per * N2)],
            tokens_v.at[pl.ds(i * per * N2, per * N2)],
            arrive.at[i],
        )
        for i in range(chunks)
    ]
    outs = [
        pltpu.make_async_copy(
            out_v.at[:, pl.ds(i * per, per)], out.at[:, pl.ds(i * per, per)], leave.at[i]
        )
        for i in range(chunks)
    ]
    in_w.start()
    for copy in in_tokens:
        copy.start()
    in_w.wait()
    for i in range(chunks):
        in_tokens[i].wait()
        value = dot_nn(tokens_v[i * per * N2 : (i + 1) * per * N2], w_v[...]).astype(bf16)
        for r in range(per):
            out_v[:, i * per + r] = value[row_slice(r)].T.reshape(n, chans, N2)
        outs[i].start()
    for copy in outs:
        copy.wait()


def d_three_kernel(
    tokens,
    cotangent,
    w_value,
    w_gate,
    first,
    fourth,
    skip,
    out,
    value_out,
    d_mix_out,
    tokens_t_out,
    turned_out,
    direct_out,
    skip_out,
    w_value_t,
    w_gate_t,
):
    n, per, chans, _ = out.shape

    @pl.when(pl.program_id(0) == 0)
    def _():
        skip_out[...] = jnp.zeros_like(skip_out)
        direct_out[...] = jnp.zeros_like(direct_out)
        w_value_t[...] = w_value[...].T
        w_gate_t[...] = w_gate[...].T

    for r in range(per):
        here = row_slice(r)
        value = dot_nn(tokens[here], w_value[...]).astype(bf16)
        gate = dot_nn(tokens[here], w_gate[...]).astype(bf16)
        d_mix = (cotangent[here].astype(f32) * gate.astype(f32)).astype(bf16)
        value_out[here] = value
        d_mix_out[here] = d_mix
        tokens_t_out[:, here] = tokens[here].T
        turned_out[here] = dot_nn(first[...], tokens[here]).astype(bf16)
        skip_out[...] += jnp.sum(
            d_mix.astype(f32) * value.astype(f32), axis=0, keepdims=True
        )
        section = dot_nn(d_mix.T, fourth[...]).astype(bf16)
        out[:, r] = section.reshape(n, chans, N2)
    direct_out[...] += dot_nn(tokens_t_out[...], d_mix_out[...])

    @pl.when(pl.program_id(0) == pl.num_programs(0) - 1)
    def _():
        direct_out[...] = direct_out[...] * skip[...]


def turn_in(swap, arrived, by_channel):
    def body(i, _):
        rows = pl.ds(pl.multiple_of(i * GROUP, GROUP), GROUP)
        block = arrived[rows].reshape(GROUP * GROUP, N2)
        turned = dot_nn(swap[...], block).astype(bf16)
        by_channel[:, rows, :] = turned.reshape(GROUP, GROUP, N2)
        return 0

    lax.fori_loop(0, N1 // GROUP, body, 0, unroll=2)


def turn_out(swap, by_channel, out):
    def body(i, _):
        rows = pl.ds(pl.multiple_of(i * GROUP, GROUP), GROUP)
        block = by_channel[:, rows, :].reshape(GROUP * GROUP, N2)
        turned = dot_nn(swap[...], block).astype(bf16)
        out[rows] = turned.reshape(GROUP, GROUP, N2)
        return 0

    lax.fori_loop(0, N1 // GROUP, body, 0, unroll=2)


def home_forward_kernel(
    arrived, kernel, first_t, second, third, swap, out, spectrum_out, by_channel
):
    turn_in(swap, arrived, by_channel)

    def body(c, _):
        section = dot_nn(by_channel[c], first_t[...]).astype(bf16)
        spectrum = dot_nn(second[...], section)
        spectrum_out[c] = spectrum
        filtered = (spectrum * kernel[c].astype(f32)).astype(bf16)
        by_channel[c] = dot_nn(third[...], filtered).astype(bf16)
        return 0

    lax.fori_loop(0, GROUP, body, 0, unroll=2)
    turn_out(swap, by_channel, out)


def home_backward_kernel(
    arrived, kernel, spectrum, second_t, third_t, swap, out, grad_kernel, by_channel
):
    turn_in(swap, arrived, by_channel)

    def body(c, _):
        d_freq = dot_nn(third_t[...], by_channel[c])
        grad_kernel[c] = (d_freq * spectrum[c]).astype(bf16)
        d_spec = (d_freq * kernel[c].astype(f32)).astype(bf16)
        by_channel[c] = dot_nn(second_t[...], d_spec).astype(bf16)
        return 0

    lax.fori_loop(0, GROUP, body, 0, unroll=2)
    turn_out(swap, by_channel, out)


def accumulate(total, term):
    @pl.when(pl.program_id(0) == 0)
    def _():
        total[...] = term

    @pl.when(pl.program_id(0) > 0)
    def _():
        total[...] += term


def finish(total, factor, grad_w):
    @pl.when(pl.program_id(0) == pl.num_programs(0) - 1)
    def _():
        grad_w[...] = (total[...] * factor[0, 0]).astype(bf16)


def gate_kernel(
    arrived,
    tokens_t,
    value,
    cotangent,
    d_mix,
    fourth,
    w_gate_t,
    w_value_t,
    skip,
    factor,
    partial,
    grad_w,
    total,
    d_gate,
):
    for r in range(arrived.shape[1]):
        here = row_slice(r)
        conv = dot_nt(fourth[...], arrived[:, r].reshape(D, N2))
        mixed = conv + skip[...] * value[here].astype(f32)
        d_gate[here] = (cotangent[here].astype(f32) * mixed).astype(bf16)
        direct = (skip[...] * d_mix[here].astype(f32)).astype(bf16)
        partial[here] = (
            dot_nn(d_gate[here], w_gate_t[...]) + dot_nn(direct, w_value_t[...])
        ).astype(bf16)
    accumulate(total, dot_nn(tokens_t[...], d_gate[...]))
    finish(total, factor, grad_w)


def value_kernel(
    per,
    arrived,
    turned,
    direct,
    factor,
    bit,
    _,
    kept,
    given,
    arrived_v,
    turned_v,
    direct_v,
    total,
    arrive,
):
    rows = arrived.shape[1]
    chunks = rows // per
    in_direct = pltpu.make_async_copy(direct, direct_v, arrive.at[chunks, 0])

    def copies(i):
        lines = pl.ds(i * per, per)
        here = pl.ds(i * per * N2, per * N2)
        return [
            pltpu.make_async_copy(
                arrived.at[:, lines], arrived_v.at[:, lines], arrive.at[i, 0]
            ),
            pltpu.make_async_copy(turned.at[here], turned_v.at[here], arrive.at[i, 1]),
        ]

    started = [copies(i) for i in range(chunks)]
    for group in started:
        for copy in group:
            copy.start()
    in_direct.start()
    for i in range(chunks):
        for copy in started[i]:
            copy.wait()
        side = jnp.concatenate(
            [arrived_v[:, r].reshape(D, N2) for r in range(i * per, (i + 1) * per)], axis=1
        )
        term = dot_nn(side, turned_v[i * per * N2 : (i + 1) * per * N2])
        if i == 0:
            total[...] = term
        else:
            total[...] += term
    in_direct.wait()
    size = kept.shape[1]
    total[...] = total[...].T
    for high in range(2):
        for part, low in ((kept, bit[0, 0]), (given, 1 - bit[0, 0])):
            place = pl.ds(pl.multiple_of((2 * high + low) * size, size), size)
            part[high] = ((total[place] + direct_v[place]) * factor[0, 0]).astype(bf16)


def tokens_kernel(arrived, partial, first_t, w_value_t, *rest):
    grad_tokens = rest[-1]
    for r in range(arrived.shape[1]):
        here = row_slice(r)
        d_cube = dot_nt(first_t[...], arrived[:, r].reshape(D, N2)).astype(bf16)
        grad_tokens[here] = (
            partial[here].astype(f32) + dot_nn(d_cube, w_value_t[...])
        ).astype(bf16)


def from_partner(array, b, n):
    return lax.ppermute(array, "seq", [(i, i ^ (1 << b)) for i in range(n)])


def halves(part, axis, b):
    bit = (lax.axis_index("seq") >> b) & 1
    kept = lax.dynamic_index_in_dim(part, bit, axis, keepdims=False)
    sent = lax.dynamic_index_in_dim(part, 1 - bit, axis, keepdims=False)
    return kept, sent


def added(kept, got):
    return (kept.astype(f32) + got.astype(f32)).astype(bf16)


def doubled(part, axis, b, n):
    bit = (lax.axis_index("seq") >> b) & 1
    mine = jnp.expand_dims(part, axis)
    other = jnp.expand_dims(from_partner(part, b, n), axis)
    around = jnp.concatenate([mine, other, mine], axis)
    return lax.dynamic_slice_in_dim(around, bit, 2, axis)


def on_device(
    tokens,
    w_value,
    w_gate,
    first_block,
    second_block,
    third_block,
    fourth_block,
    kernel,
    skip_gain,
    cotangent,
):
    n = lax.axis_size("seq")
    rows = N1 // n
    chans = D // n
    local_rows = tokens.shape[0]
    sections = (n, rows, chans, N2)
    factor = (1.0 / jnp.sqrt(jnp.asarray(N1 * N2, f32))).reshape(1, 1)
    skip = skip_gain.reshape(1, D)
    square = whole((D, D))
    block = whole((N1, N2))
    line = whole((1, D))
    per = min(4, rows)
    row = rows_of(per)
    column = pl.BlockSpec((D, per * N2), lambda i: (0, i))
    sent = by_device(n, per, chans)
    one = pl.BlockSpec(memory_space=pltpu.SMEM)
    place = jnp.arange(GROUP * GROUP)
    swap = (
        place[None, :] == ((place % GROUP) * GROUP + place // GROUP)[:, None]
    ).astype(bf16)

    def cost(gflop, mib):
        scale = rows / 16
        return pl.CostEstimate(
            flops=int(gflop * 1e9 * scale), bytes_accessed=int(mib * 2**20 * scale), transcendentals=0
        )

    def shape(dims, dtype=bf16):
        return jax.ShapeDtypeStruct(dims, dtype)

    def transfer(array):
        return lax.all_to_all(array, "seq", split_axis=0, concat_axis=0, tiled=True)

    unread = pl.BlockSpec(memory_space=pl.ANY)
    one_sent = pl.pallas_call(
        functools.partial(send_value_kernel, per),
        in_specs=[unread] * 2,
        out_specs=unread,
        out_shape=shape(sections),
        scratch_shapes=[
            pltpu.VMEM((local_rows, D), bf16),
            pltpu.VMEM((D, D), bf16),
            pltpu.VMEM(sections, bf16),
            pltpu.SemaphoreType.DMA((rows // per + 1,)),
            pltpu.SemaphoreType.DMA((rows // per,)),
        ],
        compiler_params=params(),
        cost_estimate=cost(2.1, 9),
    )(tokens, w_value)
    one_home = transfer(one_sent)

    three_sent, value, d_mix, tokens_t, turned, direct, skip_term, w_value_t, w_gate_t = pl.pallas_call(
        d_three_kernel,
        grid=(rows // per,),
        in_specs=[row, row, square, square, block, block, line],
        out_specs=[sent, row, row, column, row, square, line, square, square],
        out_shape=[
            shape(sections),
            shape((local_rows, D)),
            shape((local_rows, D)),
            shape((D, local_rows)),
            shape((local_rows, D)),
            shape((D, D), f32),
            shape((1, D), f32),
            shape((D, D)),
            shape((D, D)),
        ],
        compiler_params=params(),
        cost_estimate=cost(8.6, 30),
    )(tokens, cotangent, w_value, w_gate, first_block, fourth_block, skip)
    three_home = transfer(three_sent)

    first_t = first_block.T
    at_home = pl.BlockSpec((N1, GROUP, N2), lambda i: (0, i, 0))
    filters = pl.BlockSpec((GROUP, N1, N2), lambda i: (i, 0, 0))
    three_back, spectrum = pl.pallas_call(
        home_forward_kernel,
        grid=(chans // GROUP,),
        in_specs=[at_home, filters, block, block, block, block],
        out_specs=[at_home, filters],
        out_shape=[shape((N1, chans, N2)), shape((chans, N1, N2), f32)],
        scratch_shapes=[pltpu.VMEM((GROUP, N1, N2), bf16)],
        compiler_params=params(),
        cost_estimate=cost(5.4, 20),
    )(
        one_home.reshape(N1, chans, N2),
        kernel,
        first_t,
        second_block,
        third_block,
        swap,
    )
    three_here = transfer(three_back.reshape(sections))

    one_back, grad_kernel = pl.pallas_call(
        home_backward_kernel,
        grid=(chans // GROUP,),
        in_specs=[at_home, filters, filters, block, block, block],
        out_specs=[at_home, filters],
        out_shape=[shape((N1, chans, N2)), shape((chans, N1, N2))],
        scratch_shapes=[pltpu.VMEM((GROUP, N1, N2), bf16)],
        compiler_params=params(),
        cost_estimate=cost(4.3, 24),
    )(
        three_home.reshape(N1, chans, N2),
        kernel,
        spectrum,
        second_block.T,
        third_block.T,
        swap,
    )
    one_here = transfer(one_back.reshape(sections))

    partial, gate_term = pl.pallas_call(
        gate_kernel,
        grid=(rows // per,),
        in_specs=[sent, column, row, row, row, block, square, square, line, one],
        out_specs=[row, square],
        out_shape=[shape((local_rows, D)), shape((D, D))],
        scratch_shapes=[pltpu.VMEM((D, D), f32), pltpu.VMEM((per * N2, D), bf16)],
        compiler_params=params(),
        cost_estimate=cost(5.4, 25),
    )(
        three_here,
        tokens_t,
        value,
        cotangent,
        d_mix,
        fourth_block,
        w_gate_t,
        w_value_t,
        skip,
        factor,
    )

    skip_lanes = jnp.broadcast_to((skip_term * factor[0, 0]).astype(bf16).T, (D, LANES))
    gate_term = jnp.concatenate([gate_term, skip_lanes], axis=1)
    bits = n.bit_length() - 1
    gate_part = gate_term.reshape((2,) * bits + (D // n, D + LANES))
    for b in range(bits):
        kept, given = halves(gate_part, bits - 1 - b, b)
        gate_part = added(kept, from_partner(given, b, n))

    in_vmem = pl.BlockSpec(memory_space=pltpu.VMEM)
    me = lax.axis_index("seq").reshape(1, 1)
    half = (2, D // 4, D)
    kept, given = pl.pallas_call(
        functools.partial(value_kernel, per),
        in_specs=[unread, unread, unread, one, one, unread],
        out_specs=[in_vmem, in_vmem],
        out_shape=[shape(half), shape(half)],
        scratch_shapes=[
            pltpu.VMEM(sections, bf16),
            pltpu.VMEM((local_rows, D), bf16),
            pltpu.VMEM((D, D), f32),
            pltpu.VMEM((D, D), f32),
            pltpu.SemaphoreType.DMA((rows // per + 1, 2)),
        ],
        compiler_params=params(),
        cost_estimate=cost(2.2, 9.5),
    )(one_here, turned, direct, factor, me & 1, gate_part)

    for b in reversed(range(bits)):
        gate_part = doubled(gate_part, bits - 1 - b, b, n)
    gate_total = gate_part.reshape(D, D + LANES)

    unit = rows // 8
    pieces = [2, 2, 2, 2]

    def piece(i, grad_tokens, after):
        first = sum(pieces[:i])
        lines = pl.BlockSpec((unit * N2, D), lambda g: (g + first, 0))
        held = [] if grad_tokens is None else [grad_tokens]
        return pl.pallas_call(
            tokens_kernel,
            grid=(pieces[i],),
            in_specs=[
                pl.BlockSpec((n, unit, chans, N2), lambda g: (0, g + first, 0, 0)),
                lines,
                block,
                square,
                unread,
            ]
            + [unread] * len(held),
            out_specs=lines,
            out_shape=shape((local_rows, D)),
            input_output_aliases={5: 0} if held else {},
            compiler_params=params(),
            cost_estimate=cost(0.4 * pieces[i], 1.5 * pieces[i]),
        )(one_here, partial, first_t, w_value_t, after, *held)

    grad_tokens = None
    for b in range(bits):
        if b == 1:
            kept, given = halves(value_part, 0, b)
        elif b > 1:
            kept, given = value_part, value_part
        got = from_partner(given, b, n)
        if b < len(pieces):
            grad_tokens = piece(b, grad_tokens, given)
        value_part = added(kept, got)
    for b in (1, 0):
        value_part = doubled(value_part, 1 - b, b, n)
    grad_weights = jnp.stack([value_part.reshape(D, D), gate_total[:, :D]]).astype(f32)
    return grad_tokens, grad_kernel, grad_weights, gate_total[:, D].astype(f32)


def solution(mesh):
    in_specs = (
        P(("parts", "seq"), None),
        P(),
        P(),
        P(),
        P(),
        P(),
        P(),
        P("seq", None, None),
        P(),
        P(("parts", "seq"), None),
    )
    out_specs = (
        P(("parts", "seq"), None),
        P(("parts", "seq"), None, None),
        P("parts", None, None),
        P("parts"),
    )
    return jax.shard_map(
        on_device, mesh=mesh, in_specs=in_specs, out_specs=out_specs, check_vma=False
    )
```
